512 devices in a mesh: harm: 64 (over z, x, core), bus: 8 (over y).
Axes of the slice: x: 4, y: 8, z: 8, core: 2. Of those that a mesh axis runs over, the one named last changes fastest.
Arguments:
- conv_volt: bfloat16 [2, 64, 2048, 128], P(None, None, ('bus', 'harm')), may hold values from -0.75 to 0.75
- conv_power: float32 [2048, 128], P(('bus', 'harm')), may hold values from 0.2 to 2
- conv_type: int32 [2048], P(('bus', 'harm')), may hold values from 0 to 7
- type_steep: float32 [8], replicated, may hold values from 0.5 to 4
- conv_bus: int32 [2048], P(('bus', 'harm')), may hold values from 0 to 8191, as said below
- admittance: float32 [2, 4, 64, 8192], P(None, None, 'harm', 'bus'), may hold values from -0.5 to 1
- link_offset: int32 [3, 8192], P(None, 'bus'), may hold values from -8 to 8, as said below
Outputs:
- bus_volt: bfloat16 [2, 64, 8192, 128], P(None, 'harm', 'bus')
- conv_next: bfloat16 [2, 64, 2048, 128], P(None, None, ('bus', 'harm'))
The draws below stay inside these ranges and needn't reach their ends.
Inputs may be any that keep to these rules, and one draw needn't show every extreme that they name: `conv_bus`: converter c is attached to one of the buses from (c // 4) * 16 to (c // 4 + 1) * 16 - 1; a bus may carry several converters. `link_offset`: the first line of every bus spans exactly 8 buses, up or down; the others span 1 to 8 buses; no offset is zero.
All inputs are finite; a program needn't handle non-finite values.
Results may differ from the reference program's by a relative error of at most 0.0057.
Values may be sent and summed in bfloat16 or wider, within the bound.
No kernel may reach another device: no remote copies, remote signals or barrier semaphores. Data moves between devices by JAX's collectives and lax.ppermute only.
A program may use at most 64 MiB of HBM per device.

```python
import math
import jax
import jax.numpy as jnp
from jax import lax

H = 64
NT = 1024
S = 128
CONV_DEV = 4
BUS_SUB = 16
TYPES = 8
LINKS = 3
REACH = 8
ITERS = 3
CONVS = 2048
BUSES = 8192


def draw_conv_bus(key, part):
    keys = jax.random.split(jax.random.fold_in(key, 11), 3)
    first_pick = jax.random.randint(keys[0], (CONVS,), 0, BUS_SUB)
    second_pick = jax.random.randint(keys[1], (CONVS,), 0, BUS_SUB)
    rotation = jax.random.randint(keys[2], (CONVS // CONV_DEV,), 0, BUS_SUB)
    group_num = jnp.arange(CONVS, dtype=jnp.int32) // CONV_DEV
    local_bus = (jnp.minimum(first_pick, second_pick) + rotation[group_num]) % BUS_SUB
    return (group_num * BUS_SUB + local_bus).astype(jnp.int32)


def draw_link_offset(key, part):
    keys = jax.random.split(jax.random.fold_in(key, 23), 2)
    distance = jax.random.randint(keys[0], (LINKS, BUSES), 1, REACH + 1)
    distance = jnp.where(jnp.arange(LINKS, dtype=jnp.int32)[:, None] == 0, REACH, distance)
    direction = jax.random.randint(keys[1], (LINKS, BUSES), 0, 2) * 2 - 1
    return (distance * direction).astype(jnp.int32)


def draw_admittance(key, part):
    keys = jax.random.split(jax.random.fold_in(key, 37), 3)
    inverse_real = jax.random.uniform(keys[0], (H, BUSES), jnp.float32, 0.4, 1.0)
    inverse_imag = jnp.clip(0.15 * jax.random.normal(keys[1], (H, BUSES), jnp.float32), -0.45, 0.45)
    lines = jnp.clip(0.17 * jax.random.normal(keys[2], (2, LINKS, H, BUSES), jnp.float32), -0.5, 0.5)
    inverse = jnp.stack([inverse_real, inverse_imag])[:, None]
    return jnp.concatenate([inverse, lines], axis=1).astype(jnp.float32)


def place_ends(array, rng, least, largest):
    shape = array.shape
    index_at = [jax.random.randint(jax.random.fold_in(rng, axis), (), 0, shape[axis]) for axis in range(len(shape))]
    array = array.at[tuple(index_at)].set(least)
    longest = shape.index(max(shape))
    index_at[longest] = (index_at[longest] + 1) % shape[longest]
    return array.at[tuple(index_at)].set(largest)


def levels(key, extent, pieces, least, high):
    def one(position, shards_of):
        heights = jax.random.uniform(jax.random.fold_in(jax.random.fold_in(key, 6), position), (shards_of,), jnp.float32, least / len(pieces), high / len(pieces))
        return jnp.repeat(jnp.exp(heights), extent[position] // shards_of).reshape((-1,) + (1,) * (len(extent) - position - 1))

    level = one(*pieces[0])
    for cut in pieces[1:]:
        level = level * one(*cut)
    return level


def centred(key, dims, scale, most, pieces=(), kind=jnp.bfloat16):
    drawn = scale * jax.random.normal(key, dims, jnp.float32)
    if pieces:
        drawn = drawn * levels(key, dims, pieces, -0.22, 0.18)
    return jnp.clip(drawn, -most, most).astype(kind)


def setup_inputs(seed: int = 0) -> dict:
    arg_keys = jax.random.split(jax.random.key(seed), 8)
    conv_volt = centred(arg_keys[0], (2, H, CONVS, S), 0.125, 0.75, ((2, 512),))
    conv_power = jnp.clip(jnp.exp(math.log(2.0) - 2.3025851 * jax.random.uniform(arg_keys[1], (CONVS, S), jnp.float32) ** levels(arg_keys[1], (CONVS, S), ((0, 512),), -0.2, 0.2)), 0.2, 2.0)
    conv_type = place_ends(jax.random.randint(arg_keys[2], (CONVS,), 0, TYPES), jax.random.fold_in(arg_keys[2], 1), 0, TYPES - 1).astype(jnp.int32)
    type_steep = jnp.clip(jax.random.uniform(arg_keys[3], (TYPES,), jnp.float32, 0.5, 4.0), 0.5, 4.0)
    conv_bus = draw_conv_bus(jax.random.fold_in(arg_keys[7], 71), 0)
    admittance = draw_admittance(jax.random.fold_in(arg_keys[7], 71), 0)
    link_offset = draw_link_offset(jax.random.fold_in(arg_keys[7], 71), 0)
    return {"conv_volt": conv_volt, "conv_power": conv_power, "conv_type": conv_type, "type_steep": type_steep, "conv_bus": conv_bus, "admittance": admittance, "link_offset": link_offset}


def make_basis():
    orders = jnp.arange(1, H + 1, dtype=jnp.int32)
    samples = jnp.arange(NT, dtype=jnp.int32)
    phases = ((orders[:, None] * samples[None, :]) % NT).astype(jnp.float32) * (2.0 * math.pi / NT)
    return jnp.concatenate([jnp.cos(phases), -jnp.sin(phases)], axis=0).astype(jnp.bfloat16)


def complex_product(left_real, left_imag, right_real, right_imag):
    return left_real * right_real - left_imag * right_imag, left_real * right_imag + left_imag * right_real


def reference(conv_volt, conv_power, conv_type, type_steep, conv_bus, admittance, link_offset):
    harmonic_basis = make_basis().astype(jnp.float32)
    steepness = type_steep[conv_type]
    volt_rows = conv_volt.reshape(2 * H, CONVS, S)

    def evaluate(group_num):
        first_row = (group_num * CONV_DEV).astype(jnp.int32)
        volt_group = lax.dynamic_slice_in_dim(volt_rows, first_row, CONV_DEV, 1).astype(jnp.float32)
        power_group = lax.dynamic_slice_in_dim(conv_power, first_row, CONV_DEV, 0)
        steep_group = lax.dynamic_slice_in_dim(steepness, first_row, CONV_DEV, 0)
        waveform = jnp.einsum("kcs,kn->csn", volt_group, harmonic_basis)
        current = (power_group[:, :, None] * jnp.tanh(steep_group[:, None, None] * waveform)).astype(jnp.bfloat16)
        spectra = jnp.einsum("csn,kn->kcs", current.astype(jnp.float32), harmonic_basis) * (NT ** -0.5)
        return spectra.astype(jnp.bfloat16)

    groups = lax.map(evaluate, jnp.arange(CONVS // CONV_DEV, dtype=jnp.int32))
    spectra = jnp.transpose(groups, (1, 0, 2, 3)).reshape(2, H, CONVS, S)
    bus_numbers = jnp.arange(BUSES, dtype=jnp.int32)

    def solve(harmonic):
        spectra_here = spectra[:, harmonic].astype(jnp.float32)
        summed = jnp.zeros((2, BUSES, S), jnp.float32).at[:, conv_bus, :].add(spectra_here)
        rounded = lax.optimization_barrier(summed.astype(jnp.bfloat16))
        inject_real = rounded[0].astype(jnp.float32)
        inject_imag = rounded[1].astype(jnp.float32)
        coeffs = admittance[:, :, harmonic]
        diag_real = coeffs[0, 0][:, None]
        diag_imag = coeffs[1, 0][:, None]
        volt_real, volt_imag = complex_product(diag_real, diag_imag, inject_real, inject_imag)
        for sweep_index in range(ITERS - 1):
            total_real, total_imag = inject_real, inject_imag
            for line_num in range(LINKS):
                target = bus_numbers + link_offset[line_num]
                inside = ((target >= 0) & (target < BUSES))[:, None]
                clipped = jnp.clip(target, 0, BUSES - 1)
                near_real = jnp.where(inside, volt_real[clipped], 0.0)
                near_imag = jnp.where(inside, volt_imag[clipped], 0.0)
                term_real, term_imag = complex_product(coeffs[0, 1 + line_num][:, None], coeffs[1, 1 + line_num][:, None], near_real, near_imag)
                total_real = total_real + term_real
                total_imag = total_imag + term_imag
            volt_real, volt_imag = complex_product(diag_real, diag_imag, total_real, total_imag)
        bus_here = jnp.stack([volt_real, volt_imag]).astype(jnp.bfloat16)
        return bus_here, bus_here[:, conv_bus, :]

    bus_all, conv_all = lax.map(solve, jnp.arange(H, dtype=jnp.int32))
    return jnp.transpose(bus_all, (1, 0, 2, 3)), jnp.transpose(conv_all, (1, 0, 2, 3))
```

```python
import math

import jax
import jax.numpy as jnp
import numpy as np
from jax import lax
from jax.experimental import pallas as pl
from jax.experimental.pallas import tpu as pltpu
from jax.sharding import PartitionSpec as P

H = 64
NT = 1024
REACH = 8
LINKS = 3
SUB = 16
CONV = 4
EDGE = 2 * REACH
TILE = 128
WIN = 256
ROWS = 12
F32 = jnp.float32
BF16 = jnp.bfloat16


def make_basis():
    turn = np.arange(1, H + 1)[:, None] * np.arange(NT)[None, :] % NT
    angle = turn * (2.0 * math.pi / NT)
    return np.concatenate([np.cos(angle), -np.sin(angle)], axis=0).astype(BF16)


def iota(shape, dim):
    return lax.broadcasted_iota(jnp.int32, shape, dim)


def sweeps_kernel(adm_ref, off_ref, q_ref):
    inv_r, inv_i = adm_ref[0:1, :], adm_ref[4:5, :]
    steps = []
    for k in range(1, 1 + LINKS):
        line_r, line_i = adm_ref[k : k + 1, :], adm_ref[4 + k : 5 + k, :]
        steps.append((inv_r * line_r - inv_i * line_i, inv_r * line_i + inv_i * line_r))
    rows = iota((WIN, WIN), 0)
    lanes = iota((1, WIN), 1)
    same = iota((TILE, WIN), 0) + EDGE == iota((TILE, WIN), 1)
    for b in range(q_ref.shape[0]):
        win = slice(b * TILE, b * TILE + WIN)
        turned_r = jnp.zeros((WIN, WIN), F32)
        turned_i = jnp.zeros((WIN, WIN), F32)
        for k in range(LINKS):
            here = rows == lanes + off_ref[k : k + 1, win]
            turned_r += jnp.where(here, steps[k][0][:, win], 0.0)
            turned_i += jnp.where(here, steps[k][1][:, win], 0.0)
        step_r, step_i = turned_r.T, turned_i.T
        mid_r, mid_i = step_r[EDGE : EDGE + TILE], step_i[EDGE : EDGE + TILE]
        twice = jnp.dot(
            jnp.concatenate([mid_r, mid_i], axis=0).astype(BF16),
            jnp.concatenate([step_r, step_i], axis=1).astype(BF16),
            preferred_element_type=F32,
        )
        all_r = twice[:TILE, :WIN] - twice[TILE:, WIN:] + mid_r + jnp.where(same, 1.0, 0.0)
        all_i = twice[:TILE, WIN:] + twice[TILE:, :WIN] + mid_i
        dr, di = inv_r[:, win], inv_i[:, win]
        q_ref[b, :TILE, :] = (all_r * dr - all_i * di).astype(BF16)
        q_ref[b, TILE:, :] = (all_r * di + all_i * dr).astype(BF16)


def network_kernel(got_ref, low_ref, high_ref, q_ref, volt_ref, near_ref, rows, inject, out):
    harm_count = got_ref.shape[0] // ROWS
    half = harm_count // 2
    rows[...] = got_ref[...].astype(F32)

    def part(p):
        return jnp.concatenate(
            [
                rows[pl.ds(h * half * ROWS + 2 * c + p, half, stride=ROWS), :]
                for h in range(2)
                for c in range(CONV)
            ],
            axis=0,
        )

    spectra = jnp.concatenate([part(0), part(1)], axis=1).astype(BF16)
    convs = harm_count * CONV
    at = [
        jnp.sum(rows[pl.ds(h * half * ROWS + ROWS - 1, half, stride=ROWS), :], axis=0, keepdims=True)
        for h in range(2)
    ]
    at = jnp.concatenate(at, axis=1).astype(jnp.int32)
    lane = iota((1, convs), 1)
    source = lane // (CONV * half) * half + lane % half
    target = source * SUB + at
    buses = harm_count * SUB
    owner = jnp.where(iota((buses, convs), 0) == target, 1.0, 0.0).astype(BF16)
    inject[EDGE : EDGE + buses, :] = jnp.dot(owner, spectra, preferred_element_type=F32).astype(BF16)
    for ref, lane0, row0 in ((low_ref, half - 1, 0), (high_ref, 0, EDGE + buses)):
        edge = ref[...].astype(F32)
        total_r = jnp.zeros((SUB, 128), F32)
        total_i = jnp.zeros((SUB, 128), F32)
        for c in range(CONV):
            l = c * half + lane0
            bus = jnp.broadcast_to(edge[ROWS - 1 : ROWS, l : l + 1], (SUB, 128)).astype(jnp.int32)
            here = iota((SUB, 128), 0) == bus
            total_r += jnp.where(here, edge[2 * c : 2 * c + 1, :], 0.0)
            total_i += jnp.where(here, edge[2 * c + 1 : 2 * c + 2, :], 0.0)
        inject[row0 : row0 + EDGE, :] = jnp.concatenate([total_r, total_i], axis=1).astype(BF16)
    tail = 2 * EDGE + buses
    inject[tail:, :] = jnp.zeros((inject.shape[0] - tail, 256), BF16)
    volts = []
    for b in range(q_ref.shape[0]):
        acc = jnp.dot(q_ref[b], inject[b * TILE : b * TILE + WIN, :], preferred_element_type=F32)
        volt_r = (acc[:TILE, :128] - acc[TILE:, 128:]).astype(BF16)
        volt_i = (acc[:TILE, 128:] + acc[TILE:, :128]).astype(BF16)
        volt_ref[0, 0, b * TILE : b * TILE + TILE, :] = volt_r
        volt_ref[1, 0, b * TILE : b * TILE + TILE, :] = volt_i
        volts.append(jnp.concatenate([volt_r, volt_i], axis=1))
    picked = lax.dot_general(
        owner,
        jnp.concatenate(volts, axis=0),
        (((0,), (0,)), ((), ())),
        preferred_element_type=F32,
    )
    for h in range(2):
        for c in range(CONV):
            m = (h * CONV + c) * half
            for p in range(2):
                out[pl.ds(h * half * 2 * CONV + 2 * c + p, half, stride=2 * CONV), :] = picked[
                    m : m + half, p * 128 : p * 128 + 128
                ]
    near_ref[...] = out[...].astype(BF16)


def params():
    return pltpu.CompilerParams(vmem_limit_bytes=40 * 2**20)


def local(conv_volt, conv_power, conv_type, type_steep, conv_bus, admittance, link_offset):
    harm_count = lax.axis_size("harm")
    bus_count = lax.axis_size("bus")
    harm = lax.axis_index("harm")
    block = admittance.shape[3]
    snapshots = conv_volt.shape[3]
    up = [(i, i + 1) for i in range(bus_count - 1)]
    down = [(i + 1, i) for i in range(bus_count - 1)]
    half = harm_count // 2

    adm = admittance.reshape(8, block)
    edges = jnp.concatenate([adm, link_offset.astype(F32)], axis=0)
    low = lax.ppermute(edges[:, block - EDGE :], "bus", up)
    high = lax.ppermute(edges[:, :EDGE], "bus", down)
    padding = jnp.zeros((edges.shape[0], 128 - 2 * EDGE), F32)
    extended = jnp.concatenate([low, edges, high, padding], axis=1)
    adm_ext, off_ext = extended[:8], extended[8:].astype(jnp.int32)

    basis = jnp.asarray(make_basis())
    matches = conv_type[:, None] == jnp.arange(type_steep.shape[0], dtype=jnp.int32)[None, :]
    steepness = jnp.sum(jnp.where(matches, type_steep[None, :], 0.0), axis=1)
    volt_rows = conv_volt.reshape(2 * H, CONV, snapshots)
    waveform = jnp.einsum("kcs,kn->csn", volt_rows, basis, preferred_element_type=F32)
    current = (conv_power[:, :, None] * jnp.tanh(steepness[:, None, None] * waveform)).astype(BF16)
    spectra = jnp.einsum("csn,kn->kcs", current, basis, preferred_element_type=F32) * NT ** (-0.5)
    spectra = spectra.astype(BF16).reshape(2, H, CONV, snapshots)
    spectra = jnp.transpose(spectra, (1, 2, 0, 3)).reshape(H, 2 * CONV, snapshots)
    lane = jnp.arange(128, dtype=jnp.int32)
    mine = (lane[None, :] == jnp.arange(CONV)[:, None] * half + harm % half).astype(jnp.int32)
    index = jnp.sum(mine * (conv_bus % SUB)[:, None], axis=0).astype(BF16)
    index = jnp.broadcast_to(index[None, None, :], (H, 1, snapshots))
    blank = jnp.zeros((H, ROWS - 1 - 2 * CONV, snapshots), BF16)
    payload = jnp.concatenate([spectra, blank, index], axis=1).reshape(H, 3, 4, snapshots)
    got = lax.all_to_all(payload, "harm", split_axis=0, concat_axis=0, tiled=True)

    tiles = block // TILE
    q = pl.pallas_call(
        sweeps_kernel,
        out_shape=jax.ShapeDtypeStruct((tiles, 2 * TILE, WIN), BF16),
        compiler_params=params(),
        cost_estimate=pl.CostEstimate(flops=2 * tiles * 256 * 256 * 512, bytes_accessed=2**20, transcendentals=0),
        name="sweeps",
    )(adm_ext, off_ext)

    low_rows = lax.ppermute(got[harm_count - 1].reshape(ROWS, snapshots), "bus", up)
    high_rows = lax.ppermute(got[0].reshape(ROWS, snapshots), "bus", down)
    bus_volt, near = pl.pallas_call(
        network_kernel,
        out_shape=(
            jax.ShapeDtypeStruct((2, 1, block, snapshots), BF16),
            jax.ShapeDtypeStruct((harm_count * 2 * CONV, snapshots), BF16),
        ),
        scratch_shapes=[
            pltpu.VMEM((harm_count * ROWS, 128), F32),
            pltpu.VMEM((block + WIN - TILE, 256), BF16),
            pltpu.VMEM((harm_count * 2 * CONV, 128), F32),
        ],
        compiler_params=params(),
        cost_estimate=pl.CostEstimate(flops=2 * tiles * 256 * 256 * 256, bytes_accessed=2**20, transcendentals=0),
        name="network",
    )(got.reshape(harm_count * ROWS, snapshots), low_rows, high_rows, q)
    near = near.reshape(harm_count, 2 * CONV, snapshots)
    near = lax.all_to_all(near, "harm", split_axis=0, concat_axis=0, tiled=True)
    conv_next = jnp.transpose(near.reshape(H, CONV, 2, snapshots), (2, 0, 1, 3))
    return (bus_volt, conv_next)


def solution(mesh):
    in_specs = (
        P(None, None, ("bus", "harm"), None),
        P(("bus", "harm"), None),
        P(("bus", "harm")),
        P(),
        P(("bus", "harm")),
        P(None, None, "harm", "bus"),
        P(None, "bus"),
    )
    out_specs = (P(None, "harm", "bus", None), P(None, None, ("bus", "harm"), None))
    return jax.shard_map(local, mesh=mesh, in_specs=in_specs, out_specs=out_specs, check_vma=False)
```

```python
import math

import jax
import jax.numpy as jnp
import numpy as np
from jax import lax
from jax.experimental import pallas as pl
from jax.experimental.pallas import tpu as pltpu
from jax.sharding import PartitionSpec as P

H = 64
NT = 1024
REACH = 8
LINKS = 3
SUB = 16
CONV = 4
EDGE = 2 * REACH
TILE = 128
WIN = 256
ROWS = 12
COEF = 8
MARK = 11
HALF = 32
F32 = jnp.float32
BF16 = jnp.bfloat16
I32 = jnp.int32


def make_basis():
    turn = np.arange(1, H + 1)[:, None] * np.arange(NT)[None, :] % NT
    angle = turn * (2.0 * math.pi / NT)
    return np.concatenate([np.cos(angle), -np.sin(angle)], axis=0).astype(BF16)


def iota(shape, dim):
    return lax.broadcasted_iota(I32, shape, dim)


def product(ar, ai, br, bi):
    return ar * br - ai * bi, ar * bi + ai * br


def prepare_kernel(adm_ref, off_ref, coef_ref, first_ref, last_ref):
    inv_r, inv_i = adm_ref[0, 0], adm_ref[1, 0]
    steps = [product(inv_r, inv_i, adm_ref[0, k], adm_ref[1, k]) for k in range(1, 1 + LINKS)]
    blank = jnp.zeros((5, inv_r.shape[1]), F32)
    coefs = jnp.concatenate(
        [inv_r] + [s[0] for s in steps] + [inv_i] + [s[1] for s in steps] + [off_ref[...].astype(F32), blank], axis=0
    )
    coef_ref[...] = coefs
    first_ref[...] = coefs[:, :128]
    last_ref[...] = coefs[:, coefs.shape[1] - 128 :]


def convert_kernel(type_ref, steep_ref, bus_ref, harm_ref, volt_ref, power_ref, turned_ref, basis_ref, out_ref, volts):
    volts[...] = volt_ref[...].astype(F32)
    kinds = 2 * H
    volt = jnp.concatenate(
        [volts[pl.ds(c, kinds, stride=CONV), :] for c in range(CONV)], axis=1
    ).astype(BF16)
    steep = jnp.concatenate([jnp.full((1, 128), steep_ref[type_ref[c]], F32) for c in range(CONV)], axis=1)
    power = jnp.concatenate([power_ref[c : c + 1, :] for c in range(CONV)], axis=1)
    spectra = jnp.zeros((kinds, CONV * 128), F32)
    step = 256
    for n in range(0, NT, step):
        wave = jnp.dot(turned_ref[n : n + step, :], volt, preferred_element_type=F32)
        current = (power * jnp.tanh(steep * wave)).astype(BF16)
        spectra += jnp.dot(basis_ref[:, n : n + step], current, preferred_element_type=F32)
    spectra = spectra * NT ** (-0.5)
    for c in range(CONV):
        for p in range(2):
            out_ref[pl.ds(2 * c + p, H, stride=ROWS), :] = spectra[p * H : p * H + H, c * 128 : c * 128 + 128]
    lane = iota((H, 128), 1)
    column = lax.rem(harm_ref[0], HALF)
    mark = jnp.zeros((H, 128), F32)
    for c in range(CONV):
        mark += jnp.where(lane == c * HALF + column, lax.rem(bus_ref[c], SUB).astype(F32), 0.0)
    out_ref[pl.ds(MARK, H, stride=ROWS), :] = mark


def pack_kernel(rows_ref, coef_ref, low_ref, high_ref, out_ref, ext_ref, rows, groups):
    rows[...] = rows_ref[...]
    whole = jnp.concatenate([low_ref[...], coef_ref[...], high_ref[...]], axis=1)
    width = whole.shape[1]
    ext = pltpu.roll(whole, width - (128 - EDGE), 1)[:, : width - 128]
    ext_ref[...] = ext
    k, j = iota((8, 128), 0), iota((8, 128), 1) // SUB
    for v in range(ext.shape[1] // 128):
        x = ext[:8, v * 128 : v * 128 + 128]
        for s in (1, 2, 4):
            later = pltpu.roll(pltpu.roll(x, s, 0), 128 - SUB * s, 1)
            sooner = pltpu.roll(pltpu.roll(x, 8 - s, 0), SUB * s, 1)
            bk, bj = (k // s) % 2, (j // s) % 2
            x = jnp.where(bk == bj, x, jnp.where(bk == 1, later, sooner))
        groups[v * 8 : v * 8 + 8, :] = x
    for q in range(3):
        rows[pl.ds(COEF + q, H, stride=ROWS), :] = groups[q : q + H, :]
    out_ref[...] = rows[...].astype(BF16)


def sweeps_kernel(ext_ref, q_ref):
    rows = iota((WIN, WIN), 0)
    lanes = iota((1, WIN), 1)
    same = iota((TILE, WIN), 0) + EDGE == iota((TILE, WIN), 1)
    for b in range(q_ref.shape[0]):
        win = slice(b * TILE, b * TILE + WIN)
        turned_r = jnp.zeros((WIN, WIN), F32)
        turned_i = jnp.zeros((WIN, WIN), F32)
        for k in range(LINKS):
            here = rows == lanes + ext_ref[8 + k : 9 + k, win].astype(I32)
            turned_r += jnp.where(here, ext_ref[1 + k : 2 + k, win], 0.0)
            turned_i += jnp.where(here, ext_ref[5 + k : 6 + k, win], 0.0)
        step_r, step_i = turned_r.T, turned_i.T
        mid_r, mid_i = step_r[EDGE : EDGE + TILE], step_i[EDGE : EDGE + TILE]
        twice = jnp.dot(
            jnp.concatenate([mid_r, mid_i], axis=0).astype(BF16),
            jnp.concatenate([step_r, step_i], axis=1).astype(BF16),
            preferred_element_type=F32,
        )
        all_r = twice[:TILE, :WIN] - twice[TILE:, WIN:] + mid_r + jnp.where(same, 1.0, 0.0)
        all_i = twice[:TILE, WIN:] + twice[TILE:, :WIN] + mid_i
        q_r, q_i = product(all_r, all_i, ext_ref[0:1, win], ext_ref[4:5, win])
        q_ref[b, :TILE, :] = q_r.astype(BF16)
        q_ref[b, TILE:, :] = q_i.astype(BF16)


def network_kernel(got_ref, low_ref, high_ref, q_ref, volt_ref, rows, inject):
    rows[...] = got_ref[...].astype(F32)

    def part(p):
        return jnp.concatenate(
            [
                rows[pl.ds(h * HALF * ROWS + 2 * c + p, HALF, stride=ROWS), :]
                for h in range(2)
                for c in range(CONV)
            ],
            axis=0,
        )

    spectra = jnp.concatenate([part(0), part(1)], axis=1).astype(BF16)
    convs = H * CONV
    at = [
        jnp.sum(rows[pl.ds(h * HALF * ROWS + MARK, HALF, stride=ROWS), :], axis=0, keepdims=True)
        for h in range(2)
    ]
    at = jnp.concatenate(at, axis=1).astype(I32)
    lane = iota((1, convs), 1)
    source = lane // (CONV * HALF) * HALF + lane % HALF
    target = source * SUB + at
    buses = H * SUB
    owner = jnp.where(iota((buses, convs), 0) == target, 1.0, 0.0).astype(BF16)
    inject[EDGE : EDGE + buses, :] = jnp.dot(owner, spectra, preferred_element_type=F32).astype(BF16)
    for ref, lane0, row0 in ((low_ref, HALF - 1, 0), (high_ref, 0, EDGE + buses)):
        edge = ref[...].astype(F32)
        total_r = jnp.zeros((SUB, 128), F32)
        total_i = jnp.zeros((SUB, 128), F32)
        for c in range(CONV):
            at = c * HALF + lane0
            bus = jnp.broadcast_to(edge[MARK : MARK + 1, at : at + 1], (SUB, 128)).astype(I32)
            here = iota((SUB, 128), 0) == bus
            total_r += jnp.where(here, edge[2 * c : 2 * c + 1, :], 0.0)
            total_i += jnp.where(here, edge[2 * c + 1 : 2 * c + 2, :], 0.0)
        inject[row0 : row0 + EDGE, :] = jnp.concatenate([total_r, total_i], axis=1).astype(BF16)
    tail = 2 * EDGE + buses
    inject[tail:, :] = jnp.zeros((inject.shape[0] - tail, 256), BF16)
    for b in range(q_ref.shape[0]):
        acc = jnp.dot(q_ref[b], inject[b * TILE : b * TILE + WIN, :], preferred_element_type=F32)
        volt_ref[0, 0, b * TILE : b * TILE + TILE, :] = (acc[:TILE, :128] - acc[TILE:, 128:]).astype(BF16)
        volt_ref[1, 0, b * TILE : b * TILE + TILE, :] = (acc[:TILE, 128:] + acc[TILE:, :128]).astype(BF16)


def swapped(x):
    return pltpu.roll(x, 64, 1)


def packed_product(a, b, real):
    turned = swapped(b)
    return a * jnp.where(real, b, turned) + swapped(a) * jnp.where(real, -turned, b)


def near_kernel(bus_ref, harm_ref, got_ref, mine_ref, prev_ref, next_ref, ext_ref, out_ref, coefs, rows, out):
    harm = harm_ref[0]
    coefs[...] = got_ref[...].astype(F32)
    size = mine_ref.shape[0]
    for q, ref in enumerate((prev_ref, mine_ref, next_ref)):
        rows[q * size : q * size + size, :] = ref[...].astype(F32)

    shape = (8, 128)
    lane = iota(shape, 1)
    real = lane < 64
    spot = lane % 64
    conv, path = spot // 16, spot % 16
    base = pl.multiple_of(harm * SUB // 128 * 128, 128)
    offs = ext_ref[8:16, pl.ds(base, 256)]
    offs = pltpu.roll(offs, 256 - lax.rem(harm * SUB, 128), 1)[:, :128].astype(I32)
    offs = [jnp.broadcast_to(offs[k : k + 1, :], shape) for k in range(LINKS)]

    def hop(bus, line):
        total = bus
        for k in range(LINKS):
            total += jnp.where(line == k + 1, jnp.take_along_axis(offs[k], bus, axis=1), 0)
        return total

    def place(bus, line, used):
        at = bus // SUB * 128 + line * SUB + bus % SUB + jnp.where(real, 0, 64)
        return jnp.where(used, at, -1)[:1]

    bus0 = jnp.full(shape, SUB, I32)
    for c in range(CONV):
        bus0 += jnp.where(conv == c, lax.rem(bus_ref[c], SUB), 0)
    two = path >= 1 + LINKS
    line1 = jnp.where(two, 1 + (path - 1 - LINKS) // LINKS, path)
    line2 = jnp.where(two, 1 + (path - 1 - LINKS) % LINKS, 0)
    valid = path < 1 + LINKS + LINKS * LINKS
    line1 = jnp.where(valid, line1, 0)
    line2 = jnp.where(valid, line2, 0)
    bus1 = hop(bus0, line1)
    bus2 = hop(bus1, line2)
    places = jnp.concatenate(
        [place(bus0, line1, valid & (path >= 1)), place(bus1, line2, valid & two), place(bus2, 0, valid)], axis=1
    )
    pick = jnp.where(iota((3 * 128, 3 * 128), 0) == places, 1.0, 0.0).astype(BF16)
    window = jnp.concatenate(
        [coefs[pl.ds(COEF + q, H, stride=ROWS), :] for q in range(3)], axis=1
    ).astype(BF16)
    found = jnp.dot(window, pick, preferred_element_type=F32)
    real, path = real[:1], path[:1]
    first = found[:, :128] + jnp.where(real & (path == 0), 1.0, 0.0)
    second = found[:, 128:256] + jnp.where(real & (path <= LINKS), 1.0, 0.0)
    weight = packed_product(packed_product(first, second, real), found[:, 256:], real)

    many = (128, 128)
    row = iota(many, 0)
    other = row % 64 % (3 * CONV)
    bus_of = jnp.zeros(many, I32)
    for q in range(3):
        marks = rows[q * size + MARK : q * size + MARK + 1, :]
        column = lax.rem(harm + q - 1 + HALF, HALF)
        for c in range(CONV):
            bus = jnp.sum(jnp.where(iota((1, 128), 1) == c * HALF + column, marks, 0.0), axis=1, keepdims=True)
            bus = jnp.broadcast_to(bus.astype(I32), many) + q * SUB
            bus_of = jnp.where(other == q * CONV + c, bus, bus_of)
    wide = iota(many, 1)
    match = (row // 64 == wide // 64) & (row % 64 // (3 * CONV) == wide % 64 // 16) & (bus_of == bus2[:1])
    match = jnp.where(match, 1.0, 0.0).astype(BF16)
    high = weight.astype(BF16)
    rest = (weight - high.astype(F32)).astype(BF16)
    dims = (((1,), (1,)), ((), ()))
    table = lax.dot_general(high, match, dims, preferred_element_type=F32)
    table += lax.dot_general(rest, match, dims, preferred_element_type=F32)

    total = [[jnp.zeros((H, 128), F32) for _ in range(2)] for _ in range(CONV)]
    for q in range(3):
        for o in range(CONV):
            spec_r = rows[pl.ds(q * size + 2 * o, H, stride=ROWS), :]
            spec_i = rows[pl.ds(q * size + 2 * o + 1, H, stride=ROWS), :]
            for c in range(CONV):
                at = c * 3 * CONV + q * CONV + o
                add_r, add_i = product(table[:, at : at + 1], table[:, 64 + at : 65 + at], spec_r, spec_i)
                total[c][0] += add_r
                total[c][1] += add_i
    for c in range(CONV):
        for p in range(2):
            out[pl.ds(p * H * CONV + c, H, stride=CONV), :] = total[c][p]
    out_ref[...] = out[...].astype(BF16)


SMEM = pl.BlockSpec(memory_space=pltpu.SMEM)
VMEM = pl.BlockSpec(memory_space=pltpu.VMEM)


def call(kernel, name, out_shape, in_specs, scratch=(), cost=(0, 0, 0)):
    flops, moved, hard = cost
    return pl.pallas_call(
        kernel,
        out_shape=out_shape,
        in_specs=in_specs,
        out_specs=jax.tree.map(lambda _: VMEM, out_shape),
        scratch_shapes=list(scratch),
        compiler_params=pltpu.CompilerParams(vmem_limit_bytes=40 * 2**20),
        cost_estimate=pl.CostEstimate(flops=flops, bytes_accessed=moved, transcendentals=hard),
        name=name,
    )


def local(conv_volt, conv_power, conv_type, type_steep, conv_bus, admittance, link_offset):
    harm_count = lax.axis_size("harm")
    bus_count = lax.axis_size("bus")
    block = admittance.shape[3]
    snapshots = conv_volt.shape[3]
    tiles = block // TILE
    size = harm_count * ROWS
    up = [(i, i + 1) for i in range(bus_count - 1)]
    down = [(i + 1, i) for i in range(bus_count - 1)]
    along = harm_count * bus_count
    harm = lax.axis_index("harm").astype(I32).reshape(1)
    S = jax.ShapeDtypeStruct

    coef, first, last = call(
        prepare_kernel,
        "prepare",
        (S((16, block), F32), S((16, 128), F32), S((16, 128), F32)),
        [VMEM] * 2,
    )(admittance.reshape(2, 4, 1, block), link_offset)
    low = lax.ppermute(last, "bus", up)
    high = lax.ppermute(first, "bus", down)

    basis = make_basis()
    rows = call(
        convert_kernel,
        "convert",
        S((size, 128), F32),
        [SMEM] * 4 + [VMEM] * 4,
        [pltpu.VMEM((2 * H * CONV, 128), F32)],
        (2 * 2 * 128 * 1024 * 512, 2**20, 2**19),
    )(
        conv_type,
        type_steep,
        conv_bus,
        harm,
        conv_volt.reshape(2 * H * CONV, snapshots),
        conv_power,
        jnp.asarray(np.ascontiguousarray(basis.T)),
        jnp.asarray(basis),
    )
    payload, ext = call(
        pack_kernel,
        "pack",
        (S((size, 128), BF16), S((16, block + 128), F32)),
        [VMEM] * 4,
        [pltpu.VMEM((size, 128), F32), pltpu.VMEM((block // SUB + 8, 128), F32)],
    )(rows, coef, low, high)

    four = (harm_count, ROWS // 4, 4, snapshots)
    got = lax.all_to_all(payload.reshape(four), "harm", split_axis=0, concat_axis=0, tiled=True)

    q = call(
        sweeps_kernel,
        "sweeps",
        S((tiles, 2 * TILE, WIN), BF16),
        [VMEM],
        cost=(2 * tiles * 256 * 256 * 512, 2**20, 0),
    )(ext)
    sideways = [[(i, i + 1) for i in range(along - 1)], [(i + 1, i) for i in range(along - 1)]]
    prev = turn(payload, sideways[0], harm_count)
    following = turn(payload, sideways[1], harm_count)

    low_rows = lax.ppermute(got[harm_count - 1].reshape(ROWS, snapshots), "bus", up)
    high_rows = lax.ppermute(got[0].reshape(ROWS, snapshots), "bus", down)
    got = got.reshape(size, snapshots)
    near = call(
        near_kernel,
        "near",
        S((2 * H * CONV, snapshots), BF16),
        [SMEM] * 2 + [VMEM] * 5,
        [
            pltpu.VMEM((size, 128), F32),
            pltpu.VMEM((3 * size, 128), F32),
            pltpu.VMEM((2 * H * CONV, 128), F32),
        ],
        (2 * 10**7, 2**20, 0),
    )(conv_bus, harm, got, payload, prev, following, ext)
    bus_volt = call(
        network_kernel,
        "network",
        S((2, 1, block, snapshots), BF16),
        [VMEM] * 4,
        [pltpu.VMEM((size, 128), F32), pltpu.VMEM((block + WIN - TILE, 256), BF16)],
        (2 * tiles * 256 * 256 * 256, 2**20, 0),
    )(got, low_rows, high_rows, q)
    return (bus_volt, near.reshape(2, H, CONV, snapshots))


def turn(array, pairs, harm_count):
    bus_count = lax.axis_size("bus")
    number = lambda r: r % harm_count * bus_count + r // harm_count
    return lax.ppermute(array, ("harm", "bus"), [(number(s), number(d)) for s, d in pairs])


def solution(mesh):
    in_specs = (
        P(None, None, ("bus", "harm"), None),
        P(("bus", "harm"), None),
        P(("bus", "harm")),
        P(),
        P(("bus", "harm")),
        P(None, None, "harm", "bus"),
        P(None, "bus"),
    )
    out_specs = (P(None, "harm", "bus", None), P(None, None, ("bus", "harm"), None))
    return jax.shard_map(local, mesh=mesh, in_specs=in_specs, out_specs=out_specs, check_vma=False)
```

```python
import math

import jax
import jax.numpy as jnp
import numpy as np
from jax import lax
from jax.experimental import pallas as pl
from jax.experimental.pallas import tpu as pltpu
from jax.sharding import PartitionSpec as P

H = 64
NT = 1024
REACH = 8
LINKS = 3
SUB = 16
CONV = 4
EDGE = 2 * REACH
TILE = 128
WIN = 256
ROWS = 12
COEF = 8
MARK = 11
EXTRA = 11
HALF = 32
F32 = jnp.float32
BF16 = jnp.bfloat16
I32 = jnp.int32


def make_basis():
    turn = np.arange(1, H + 1)[:, None] * np.arange(NT)[None, :] % NT
    angle = turn * (2.0 * math.pi / NT)
    return np.concatenate([np.cos(angle), -np.sin(angle)], axis=0).astype(BF16)


def iota(shape, dim):
    return lax.broadcasted_iota(I32, shape, dim)


def product(ar, ai, br, bi):
    return ar * br - ai * bi, ar * bi + ai * br


def grouped(x):
    k, j = iota((8, 128), 0), iota((8, 128), 1) // SUB
    for s in (1, 2, 4):
        later = pltpu.roll(pltpu.roll(x, s, 0), 128 - SUB * s, 1)
        sooner = pltpu.roll(pltpu.roll(x, 8 - s, 0), SUB * s, 1)
        bk, bj = (k // s) % 2, (j // s) % 2
        x = jnp.where(bk == bj, x, jnp.where(bk == 1, later, sooner))
    return x


def even(axis):
    return lax.rem(lax.axis_index(axis), 2) == 0


def prepare_kernel(
    adm_hbm, off_hbm, type_hbm, steep_hbm, bus_hbm, power_hbm, volt_hbm, turned_hbm, basis_hbm,
    coef_ref, a_ref, b_ref, aux_ref, group_ref, volt_ref, turned_ref, basis_ref,
    adm, off, kind, steep, bus, power, sems,
):
    pairs = [
        (adm_hbm, adm), (off_hbm, off), (type_hbm, kind), (steep_hbm, steep), (bus_hbm, bus), (power_hbm, power),
        (volt_hbm, volt_ref), (turned_hbm, turned_ref), (basis_hbm, basis_ref),
    ]
    copies = [pltpu.make_async_copy(src, dst, sems.at[i]) for i, (src, dst) in enumerate(pairs)]
    for copy in copies:
        copy.start()
    for copy in copies[:2]:
        copy.wait()
    inv_r, inv_i = adm[0, 0], adm[1, 0]
    steps = [product(inv_r, inv_i, adm[0, k], adm[1, k]) for k in range(1, 1 + LINKS)]
    blank = jnp.zeros((5, inv_r.shape[1]), F32)
    coefs = jnp.concatenate(
        [inv_r] + [s[0] for s in steps] + [inv_i] + [s[1] for s in steps] + [off[...].astype(F32), blank], axis=0
    )
    coef_ref[...] = coefs
    tiles = coefs.shape[1] // 128
    for v in range(tiles):
        group_ref[v * 8 : v * 8 + 8, :] = grouped(coefs[:8, v * 128 : v * 128 + 128])
    row = iota((16, 128), 0)

    def edge(v, at):
        group = jnp.broadcast_to(group_ref[at : at + 1, :], (16, 128))
        return jnp.where(row == EXTRA, group, coefs[:, v * 128 : v * 128 + 128])

    first, last = edge(0, 0), edge(tiles - 1, tiles * 8 - 1)
    is_even = even("bus")
    a_ref[...] = jnp.where(is_even, last, first)
    b_ref[...] = jnp.where(is_even, first, last)

    for copy in copies[2:6]:
        copy.wait()
    for c in range(CONV):
        lanes = slice(c * 128, c * 128 + 128)
        aux_ref[0:1, lanes] = jnp.full((1, 128), steep[kind[c]], F32)
        aux_ref[1:2, lanes] = power[c : c + 1, :]
    lane = iota((1, 128), 1)
    column = lax.rem(lax.axis_index("harm"), HALF)
    mark = jnp.zeros((1, 128), F32)
    start = jnp.full((1, 128), SUB, F32)
    for c in range(CONV):
        number = lax.rem(bus[c], SUB).astype(F32)
        mark += jnp.where(lane == c * HALF + column, number, 0.0)
        start += jnp.where(lane % 64 // 16 == c, number, 0.0)
    aux_ref[2:3, :128] = mark
    aux_ref[3:4, :128] = start
    for copy in copies[6:]:
        copy.wait()


def convert_kernel(volt_ref, turned_ref, basis_ref, aux_ref, group_ref, out_ref, volts, rows):
    volts[...] = volt_ref[...].astype(F32)
    kinds = 2 * H
    volt = jnp.concatenate(
        [volts[pl.ds(c, kinds, stride=CONV), :] for c in range(CONV)], axis=1
    ).astype(BF16)
    steep, power = aux_ref[0:1, :], aux_ref[1:2, :]
    spectra = jnp.zeros((kinds, CONV * 128), F32)
    step = 256
    for n in range(0, NT, step):
        wave = jnp.dot(turned_ref[n : n + step, :], volt, preferred_element_type=F32)
        current = (power * jnp.tanh(steep * wave)).astype(BF16)
        spectra += jnp.dot(basis_ref[:, n : n + step], current, preferred_element_type=F32)
    spectra = spectra * NT ** (-0.5)
    for c in range(CONV):
        for p in range(2):
            rows[pl.ds(2 * c + p, H, stride=ROWS), :] = spectra[p * H : p * H + H, c * 128 : c * 128 + 128]
    rows[pl.ds(COEF, H, stride=ROWS), :] = pltpu.roll(group_ref[...], 1, 0)
    rows[pl.ds(COEF + 1, H, stride=ROWS), :] = group_ref[...]
    rows[pl.ds(COEF + 2, H, stride=ROWS), :] = pltpu.roll(group_ref[...], H - 1, 0)
    rows[pl.ds(MARK, H, stride=ROWS), :] = jnp.broadcast_to(aux_ref[2:3, :128], (H, 128))
    out_ref[...] = rows[...].astype(BF16)


def low_high(a, b):
    is_even = even("bus")
    return jnp.where(is_even, b, a), jnp.where(is_even, a, b)


def patch_kernel(rows_ref, a_ref, b_ref, out_ref):
    low, high = low_high(a_ref[EXTRA : EXTRA + 1, :], b_ref[EXTRA : EXTRA + 1, :])
    size = rows_ref.shape[0]
    out_ref[16 : size - 16, :] = rows_ref[16 : size - 16, :]
    row = iota((16, 128), 0)
    out_ref[:16, :] = jnp.where(row == COEF, low, rows_ref[:16, :].astype(F32)).astype(BF16)
    at = 16 - ROWS + COEF + 2
    out_ref[size - 16 :, :] = jnp.where(row == at, high, rows_ref[size - 16 :, :].astype(F32)).astype(BF16)


def sweeps_kernel(coef_ref, a_ref, b_ref, q_ref, ext_ref):
    low, high = low_high(a_ref[...], b_ref[...])
    whole = jnp.concatenate([low, coef_ref[...], high], axis=1)
    width = whole.shape[1]
    ext_ref[...] = pltpu.roll(whole, width - (128 - EDGE), 1)[:, : width - 128]
    rows = iota((WIN, WIN), 0)
    lanes = iota((1, WIN), 1)
    same = iota((TILE, WIN), 0) + EDGE == iota((TILE, WIN), 1)
    for b in range(q_ref.shape[0]):
        win = slice(b * TILE, b * TILE + WIN)
        turned_r = jnp.zeros((WIN, WIN), F32)
        turned_i = jnp.zeros((WIN, WIN), F32)
        for k in range(LINKS):
            here = rows == lanes + ext_ref[8 + k : 9 + k, win].astype(I32)
            turned_r += jnp.where(here, ext_ref[1 + k : 2 + k, win], 0.0)
            turned_i += jnp.where(here, ext_ref[5 + k : 6 + k, win], 0.0)
        step_r, step_i = turned_r.T, turned_i.T
        mid_r, mid_i = step_r[EDGE : EDGE + TILE], step_i[EDGE : EDGE + TILE]
        twice = jnp.dot(
            jnp.concatenate([mid_r, mid_i], axis=0).astype(BF16),
            jnp.concatenate([step_r, step_i], axis=1).astype(BF16),
            preferred_element_type=F32,
        )
        all_r = twice[:TILE, :WIN] - twice[TILE:, WIN:] + mid_r + jnp.where(same, 1.0, 0.0)
        all_i = twice[:TILE, WIN:] + twice[TILE:, :WIN] + mid_i
        q_r, q_i = product(all_r, all_i, ext_ref[0:1, win], ext_ref[4:5, win])
        q_ref[b, :TILE, :] = q_r.astype(BF16)
        q_ref[b, TILE:, :] = q_i.astype(BF16)


def network_kernel(got_ref, a_ref, b_ref, q_ref, volt_ref, rows, inject):
    rows[...] = got_ref[...].astype(F32)
    low, high = low_high(a_ref[...].astype(F32), b_ref[...].astype(F32))

    def part(p):
        return jnp.concatenate(
            [
                rows[pl.ds(h * HALF * ROWS + 2 * c + p, HALF, stride=ROWS), :]
                for h in range(2)
                for c in range(CONV)
            ],
            axis=0,
        )

    spectra = jnp.concatenate([part(0), part(1)], axis=1).astype(BF16)
    convs = H * CONV
    at = [
        jnp.sum(rows[pl.ds(h * HALF * ROWS + MARK, HALF, stride=ROWS), :], axis=0, keepdims=True)
        for h in range(2)
    ]
    at = jnp.concatenate(at, axis=1).astype(I32)
    lane = iota((1, convs), 1)
    source = lane // (CONV * HALF) * HALF + lane % HALF
    target = source * SUB + at
    buses = H * SUB
    owner = jnp.where(iota((buses, convs), 0) == target, 1.0, 0.0).astype(BF16)
    inject[EDGE : EDGE + buses, :] = jnp.dot(owner, spectra, preferred_element_type=F32).astype(BF16)
    for edge, lane0, row0 in ((low, HALF - 1, 0), (high, 0, EDGE + buses)):
        total_r = jnp.zeros((SUB, 128), F32)
        total_i = jnp.zeros((SUB, 128), F32)
        for c in range(CONV):
            at = c * HALF + lane0
            bus = jnp.broadcast_to(edge[MARK : MARK + 1, at : at + 1], (SUB, 128)).astype(I32)
            here = iota((SUB, 128), 0) == bus
            total_r += jnp.where(here, edge[2 * c : 2 * c + 1, :], 0.0)
            total_i += jnp.where(here, edge[2 * c + 1 : 2 * c + 2, :], 0.0)
        inject[row0 : row0 + EDGE, :] = jnp.concatenate([total_r, total_i], axis=1).astype(BF16)
    tail = 2 * EDGE + buses
    inject[tail:, :] = jnp.zeros((inject.shape[0] - tail, 256), BF16)
    for b in range(q_ref.shape[0]):
        acc = jnp.dot(q_ref[b], inject[b * TILE : b * TILE + WIN, :], preferred_element_type=F32)
        volt_ref[0, 0, b * TILE : b * TILE + TILE, :] = (acc[:TILE, :128] - acc[TILE:, 128:]).astype(BF16)
        volt_ref[1, 0, b * TILE : b * TILE + TILE, :] = (acc[:TILE, 128:] + acc[TILE:, :128]).astype(BF16)


def swapped(x):
    return pltpu.roll(x, 64, 1)


def packed_product(a, b, real):
    turned = swapped(b)
    return a * jnp.where(real, b, turned) + swapped(a) * jnp.where(real, -turned, b)


def aim_kernel(aux_ref, mine_ref, a_ref, b_ref, ext_ref, pick_ref, match_ref, spec_ref, rows):
    harm = lax.axis_index("harm")
    is_even = even("harm")
    size = mine_ref.shape[0]
    got_a, got_b = a_ref[...].astype(F32), b_ref[...].astype(F32)
    rows[:size, :] = jnp.where(is_even, got_b, got_a)
    rows[size : 2 * size, :] = mine_ref[...].astype(F32)
    rows[2 * size :, :] = jnp.where(is_even, got_a, got_b)

    shape = (8, 128)
    lane = iota(shape, 1)
    real = lane < 64
    spot = lane % 64
    path = spot % 16
    base = pl.multiple_of(harm * SUB // 128 * 128, 128)
    offs = ext_ref[8:16, pl.ds(base, 256)]
    offs = pltpu.roll(offs, 256 - lax.rem(harm * SUB, 128), 1)[:, :128].astype(I32)
    offs = [jnp.broadcast_to(offs[k : k + 1, :], shape) for k in range(LINKS)]

    def hop(bus, line):
        total = bus
        for k in range(LINKS):
            total += jnp.where(line == k + 1, jnp.take_along_axis(offs[k], bus, axis=1), 0)
        return total

    def place(bus, line, used):
        at = bus // SUB * 128 + line * SUB + bus % SUB + jnp.where(real, 0, 64)
        return jnp.where(used, at, -1)[:1]

    bus0 = jnp.broadcast_to(aux_ref[3:4, :128], shape).astype(I32)
    two = path >= 1 + LINKS
    line1 = jnp.where(two, 1 + (path - 1 - LINKS) // LINKS, path)
    line2 = jnp.where(two, 1 + (path - 1 - LINKS) % LINKS, 0)
    valid = path < 1 + LINKS + LINKS * LINKS
    line1 = jnp.where(valid, line1, 0)
    line2 = jnp.where(valid, line2, 0)
    bus1 = hop(bus0, line1)
    bus2 = hop(bus1, line2)
    places = jnp.concatenate(
        [place(bus0, line1, valid & (path >= 1)), place(bus1, line2, valid & two), place(bus2, 0, valid)], axis=1
    )
    pick_ref[...] = jnp.where(iota((3 * 128, 3 * 128), 0) == places, 1.0, 0.0).astype(BF16)
    many = (128, 128)
    row = iota(many, 0)
    other = row % 64 % (3 * CONV)
    bus_of = jnp.zeros(many, I32)
    for q in range(3):
        marks = rows[q * size + MARK : q * size + MARK + 1, :]
        column = lax.rem(harm + q - 1 + HALF, HALF)
        for c in range(CONV):
            bus = jnp.sum(jnp.where(iota((1, 128), 1) == c * HALF + column, marks, 0.0), axis=1, keepdims=True)
            bus = jnp.broadcast_to(bus.astype(I32), many) + q * SUB
            bus_of = jnp.where(other == q * CONV + c, bus, bus_of)
    wide = iota(many, 1)
    match = (row // 64 == wide // 64) & (row % 64 // (3 * CONV) == wide % 64 // 16) & (bus_of == bus2[:1])
    match_ref[...] = jnp.where(match, 1.0, 0.0).astype(BF16)
    for q in range(3):
        for o in range(2 * CONV):
            at = (q * 2 * CONV + o) * H
            spec_ref[at : at + H, :] = rows[pl.ds(q * size + o, H, stride=ROWS), :]


def near_kernel(got_ref, pick_ref, match_ref, spec_ref, out_ref, coefs, out):
    coefs[...] = got_ref[...].astype(F32)
    window = jnp.concatenate(
        [coefs[pl.ds(COEF + q, H, stride=ROWS), :] for q in range(3)], axis=1
    ).astype(BF16)
    found = jnp.dot(window, pick_ref[...], preferred_element_type=F32)
    lane = iota((1, 128), 1)
    real, path = lane < 64, lane % 16
    first = found[:, :128] + jnp.where(real & (path == 0), 1.0, 0.0)
    second = found[:, 128:256] + jnp.where(real & (path <= LINKS), 1.0, 0.0)
    weight = packed_product(packed_product(first, second, real), found[:, 256:], real)
    high = weight.astype(BF16)
    rest = (weight - high.astype(F32)).astype(BF16)
    dims = (((1,), (1,)), ((), ()))
    table = lax.dot_general(high, match_ref[...], dims, preferred_element_type=F32)
    table += lax.dot_general(rest, match_ref[...], dims, preferred_element_type=F32)

    total = [[jnp.zeros((H, 128), F32) for _ in range(2)] for _ in range(CONV)]
    for q in range(3):
        for o in range(CONV):
            at = (q * CONV + o) * 2 * H
            spec_r, spec_i = spec_ref[at : at + H, :], spec_ref[at + H : at + 2 * H, :]
            for c in range(CONV):
                at = c * 3 * CONV + q * CONV + o
                add_r, add_i = product(table[:, at : at + 1], table[:, 64 + at : 65 + at], spec_r, spec_i)
                total[c][0] += add_r
                total[c][1] += add_i
    for c in range(CONV):
        for p in range(2):
            out[pl.ds(p * H * CONV + c, H, stride=CONV), :] = total[c][p]
    out_ref[...] = out[...].astype(BF16)


VMEM = pl.BlockSpec(memory_space=pltpu.VMEM)
HBM = pl.BlockSpec(memory_space=pltpu.HBM)


def call(kernel, name, out_shape, in_specs, scratch=(), cost=(0, 0, 0)):
    flops, moved, hard = cost
    return pl.pallas_call(
        kernel,
        out_shape=out_shape,
        in_specs=in_specs,
        out_specs=jax.tree.map(lambda _: VMEM, out_shape),
        scratch_shapes=list(scratch),
        compiler_params=pltpu.CompilerParams(vmem_limit_bytes=40 * 2**20),
        cost_estimate=pl.CostEstimate(flops=flops, bytes_accessed=moved, transcendentals=hard),
        name=name,
    )


def swaps(count):
    rounds = []
    for start in (0, 1):
        firsts = range(start, count - 1, 2)
        rounds.append([(i, i + 1) for i in firsts] + [(i + 1, i) for i in firsts])
    return rounds


def local(conv_volt, conv_power, conv_type, type_steep, conv_bus, admittance, link_offset):
    harm_count = lax.axis_size("harm")
    bus_count = lax.axis_size("bus")
    block = admittance.shape[3]
    snapshots = conv_volt.shape[3]
    tiles = block // TILE
    size = harm_count * ROWS
    kinds = 2 * H
    S = jax.ShapeDtypeStruct
    over_bus = swaps(bus_count)
    number = lambda r: r % harm_count * bus_count + r // harm_count
    over_ranges = [[(number(s), number(d)) for s, d in pairs] for pairs in swaps(harm_count * bus_count)]

    basis = make_basis()
    coef, edge_a, edge_b, aux, group, volt, turned, basis = call(
        prepare_kernel,
        "prepare",
        (
            S((16, block), F32),
            S((16, 128), F32),
            S((16, 128), F32),
            S((8, CONV * 128), F32),
            S((harm_count, 128), F32),
            S((kinds * CONV, snapshots), BF16),
            S((NT, kinds), BF16),
            S((kinds, NT), BF16),
        ),
        [HBM] * 9,
        [
            pltpu.VMEM((2, 4, 1, block), F32),
            pltpu.VMEM((LINKS, block), I32),
            pltpu.SMEM((CONV,), I32),
            pltpu.SMEM(type_steep.shape, F32),
            pltpu.SMEM((CONV,), I32),
            pltpu.VMEM((CONV, snapshots), F32),
            pltpu.SemaphoreType.DMA((9,)),
        ],
    )(
        *(
            pltpu.with_memory_space_constraint(array, pltpu.HBM)
            for array in (
                admittance,
                link_offset,
                conv_type,
                type_steep,
                conv_bus,
                conv_power,
                conv_volt.reshape(kinds * CONV, snapshots),
                jnp.asarray(np.ascontiguousarray(basis.T)),
                jnp.asarray(basis),
            )
        )
    )
    edge_a = lax.ppermute(edge_a, "bus", over_bus[0])
    edge_b = lax.ppermute(edge_b, "bus", over_bus[1])

    payload = call(
        convert_kernel,
        "convert",
        S((size, 128), BF16),
        [VMEM] * 5,
        [pltpu.VMEM((kinds * CONV, 128), F32), pltpu.VMEM((size, 128), F32)],
        (2 * 2 * 128 * 1024 * 512, 2**20, 2**19),
    )(volt, turned, basis, aux, group)
    payload = call(patch_kernel, "patch", S((size, 128), BF16), [VMEM] * 3)(payload, edge_a, edge_b)

    four = (harm_count, ROWS // 4, 4, snapshots)
    got = lax.all_to_all(payload.reshape(four), "harm", split_axis=0, concat_axis=0, tiled=True)

    q, ext = call(
        sweeps_kernel,
        "sweeps",
        (S((tiles, 2 * TILE, WIN), BF16), S((16, block + 128), F32)),
        [VMEM] * 3,
        cost=(2 * tiles * 256 * 256 * 512, 2**20, 0),
    )(coef, edge_a, edge_b)
    beside_a = lax.ppermute(payload, ("harm", "bus"), over_ranges[0])
    beside_b = lax.ppermute(payload, ("harm", "bus"), over_ranges[1])
    pick, match, spec = call(
        aim_kernel,
        "aim",
        (S((3 * 128, 3 * 128), BF16), S((128, 128), BF16), S((3 * 2 * CONV * H, 128), F32)),
        [VMEM] * 5,
        [pltpu.VMEM((3 * size, 128), F32)],
        (10**6, 2**20, 0),
    )(aux, payload, beside_a, beside_b, ext)
    got, q, pick, match, spec = lax.optimization_barrier((got, q, pick, match, spec))

    is_even = even("bus")
    outer = harm_count - 1
    rows_a = lax.dynamic_index_in_dim(got, jnp.where(is_even, outer, 0), 0, keepdims=False)
    rows_b = lax.dynamic_index_in_dim(got, jnp.where(is_even, 0, outer), 0, keepdims=False)
    rows_a = lax.ppermute(rows_a.reshape(ROWS, snapshots), "bus", over_bus[0])
    rows_b = lax.ppermute(rows_b.reshape(ROWS, snapshots), "bus", over_bus[1])
    got = got.reshape(size, snapshots)
    near = call(
        near_kernel,
        "near",
        S((kinds * CONV, snapshots), BF16),
        [VMEM] * 4,
        [pltpu.VMEM((size, 128), F32), pltpu.VMEM((kinds * CONV, 128), F32)],
        (2 * 10**7, 2**20, 0),
    )(got, pick, match, spec)
    bus_volt = call(
        network_kernel,
        "network",
        S((2, 1, block, snapshots), BF16),
        [VMEM] * 4,
        [pltpu.VMEM((size, 128), F32), pltpu.VMEM((block + WIN - TILE, 256), BF16)],
        (2 * tiles * 256 * 256 * 256, 2**20, 0),
    )(got, rows_a, rows_b, q)
    return (bus_volt, near.reshape(2, H, CONV, snapshots))


def solution(mesh):
    in_specs = (
        P(None, None, ("bus", "harm"), None),
        P(("bus", "harm"), None),
        P(("bus", "harm")),
        P(),
        P(("bus", "harm")),
        P(None, None, "harm", "bus"),
        P(None, "bus"),
    )
    out_specs = (P(None, "harm", "bus", None), P(None, None, ("bus", "harm"), None))
    return jax.shard_map(local, mesh=mesh, in_specs=in_specs, out_specs=out_specs, check_vma=False)
```

```python
import math

import jax
import jax.numpy as jnp
import numpy as np
from jax import lax
from jax.experimental import pallas as pl
from jax.experimental.pallas import tpu as pltpu
from jax.sharding import PartitionSpec as P

H = 64
NT = 1024
REACH = 8
LINKS = 3
SUB = 16
CONV = 4
EDGE = 2 * REACH
TILE = 128
WIN = 256
ROWS = 12
COEF = 8
PAIR = 9
SPAN = 10
MARK = 11
HALF = 32
F32 = jnp.float32
BF16 = jnp.bfloat16
I32 = jnp.int32


def make_basis():
    turn = np.arange(1, H + 1)[:, None] * np.arange(NT)[None, :] % NT
    angle = turn * (2.0 * math.pi / NT)
    return np.concatenate([np.cos(angle), -np.sin(angle)], axis=0).astype(BF16)


def iota(shape, dim):
    return lax.broadcasted_iota(I32, shape, dim)


def product(ar, ai, br, bi):
    return ar * br - ai * bi, ar * bi + ai * br


def grouped(x):
    k, j = iota((8, 128), 0), iota((8, 128), 1) // SUB
    for s in (1, 2, 4):
        later = pltpu.roll(pltpu.roll(x, s, 0), 128 - SUB * s, 1)
        sooner = pltpu.roll(pltpu.roll(x, 8 - s, 0), SUB * s, 1)
        bk, bj = (k // s) % 2, (j // s) % 2
        x = jnp.where(bk == bj, x, jnp.where(bk == 1, later, sooner))
    return x


def even(axis):
    return lax.rem(lax.axis_index(axis), 2) == 0


def prepare_kernel(
    adm_hbm, off_hbm, type_hbm, steep_hbm, bus_hbm, power_hbm, volt_hbm, turned_hbm, basis_hbm,
    coef_ref, a_ref, b_ref, aux_ref, group_ref, volt_ref, turned_ref, basis_ref,
    adm, off, kind, steep, bus, power, spans, sems,
):
    pairs = [
        (adm_hbm, adm), (off_hbm, off), (type_hbm, kind), (steep_hbm, steep), (bus_hbm, bus), (power_hbm, power),
        (volt_hbm, volt_ref), (turned_hbm, turned_ref), (basis_hbm, basis_ref),
    ]
    copies = [pltpu.make_async_copy(src, dst, sems.at[i]) for i, (src, dst) in enumerate(pairs)]
    for copy in copies:
        copy.start()
    for copy in copies[:2]:
        copy.wait()
    inv_r, inv_i = adm[0, 0], adm[1, 0]
    steps = [product(inv_r, inv_i, adm[0, k], adm[1, k]) for k in range(1, 1 + LINKS)]
    blank = jnp.zeros((5, inv_r.shape[1]), F32)
    coefs = jnp.concatenate(
        [inv_r] + [s[0] for s in steps] + [inv_i] + [s[1] for s in steps] + [off[...].astype(F32), blank], axis=0
    )
    coef_ref[...] = coefs
    tiles = coefs.shape[1] // 128
    for v in range(tiles):
        group_ref[v * 8 : v * 8 + 8, :] = grouped(coefs[:8, v * 128 : v * 128 + 128])
        spans[v * 8 : v * 8 + 8, :] = grouped(coefs[8:, v * 128 : v * 128 + 128])
    first, last = coefs[:, :128], coefs[:, tiles * 128 - 128 :]
    is_even = even("bus")
    a_ref[...] = jnp.where(is_even, last, first)
    b_ref[...] = jnp.where(is_even, first, last)

    for copy in copies[2:6]:
        copy.wait()
    for c in range(CONV):
        lanes = slice(c * 128, c * 128 + 128)
        aux_ref[0:1, lanes] = jnp.full((1, 128), steep[kind[c]], F32)
        aux_ref[1:2, lanes] = power[c : c + 1, :]
    lane = iota((1, 128), 1)
    harm = lax.axis_index("harm")
    column = lax.rem(harm, HALF)
    mark = jnp.zeros((1, 128), F32)
    start = jnp.full((1, 128), SUB, F32)
    for c in range(CONV):
        number = lax.rem(bus[c], SUB).astype(F32)
        mark += jnp.where(lane == c * HALF + column, number, 0.0)
        start += jnp.where(lane % 64 // 16 == c, number, 0.0)
    aux_ref[2:3, :128] = mark
    aux_ref[3:4, :128] = start
    aux_ref[4:5, :128] = spans[pl.ds(harm, 1), :]
    aux_ref[5:6, :128] = spans[pl.ds(harm + jnp.where(even("harm"), 1, -1), 1), :]
    for copy in copies[6:]:
        copy.wait()


def convert_kernel(volt_ref, turned_ref, basis_ref, aux_ref, group_ref, out_ref, volts, rows):
    volts[...] = volt_ref[...].astype(F32)
    kinds = 2 * H
    volt = jnp.concatenate(
        [volts[pl.ds(c, kinds, stride=CONV), :] for c in range(CONV)], axis=1
    ).astype(BF16)
    steep, power = aux_ref[0:1, :], aux_ref[1:2, :]
    spectra = jnp.zeros((kinds, CONV * 128), F32)
    step = 256
    for n in range(0, NT, step):
        wave = jnp.dot(turned_ref[n : n + step, :], volt, preferred_element_type=F32)
        current = (power * jnp.tanh(steep * wave)).astype(BF16)
        spectra += jnp.dot(basis_ref[:, n : n + step], current, preferred_element_type=F32)
    spectra = spectra * NT ** (-0.5)
    for c in range(CONV):
        for p in range(2):
            rows[pl.ds(2 * c + p, H, stride=ROWS), :] = spectra[p * H : p * H + H, c * 128 : c * 128 + 128]
    group = group_ref[...]
    pair = jnp.where(iota((H, 128), 0) % 2 == 0, pltpu.roll(group, H - 1, 0), pltpu.roll(group, 1, 0))
    rows[pl.ds(COEF, H, stride=ROWS), :] = group
    rows[pl.ds(PAIR, H, stride=ROWS), :] = pair
    rows[pl.ds(SPAN, H, stride=ROWS), :] = jnp.broadcast_to(aux_ref[4:5, :128], (H, 128))
    rows[pl.ds(MARK, H, stride=ROWS), :] = jnp.broadcast_to(aux_ref[2:3, :128], (H, 128))
    out_ref[...] = rows[...].astype(BF16)


def low_high(a, b):
    is_even = even("bus")
    return jnp.where(is_even, b, a), jnp.where(is_even, a, b)


def sweeps_matrix(coefs):
    coefs = pltpu.roll(coefs, 3 * TILE - (TILE - EDGE), 1)[:, :WIN]
    rows = iota((WIN, WIN), 0)
    lanes = iota((1, WIN), 1)
    turned_r = jnp.zeros((WIN, WIN), F32)
    turned_i = jnp.zeros((WIN, WIN), F32)
    for k in range(LINKS):
        here = rows == lanes + coefs[8 + k : 9 + k].astype(I32)
        turned_r += jnp.where(here, coefs[1 + k : 2 + k], 0.0)
        turned_i += jnp.where(here, coefs[5 + k : 6 + k], 0.0)
    step_r, step_i = turned_r.T, turned_i.T
    mid_r, mid_i = step_r[EDGE : EDGE + TILE], step_i[EDGE : EDGE + TILE]
    twice = jnp.dot(
        jnp.concatenate([mid_r, mid_i], axis=0).astype(BF16),
        jnp.concatenate([step_r, step_i], axis=1).astype(BF16),
        preferred_element_type=F32,
    )
    same = iota((TILE, WIN), 0) + EDGE == iota((TILE, WIN), 1)
    all_r = twice[:TILE, :WIN] - twice[TILE:, WIN:] + mid_r + jnp.where(same, 1.0, 0.0)
    all_i = twice[:TILE, WIN:] + twice[TILE:, :WIN] + mid_i
    q_r, q_i = product(all_r, all_i, coefs[0:1], coefs[4:5])
    return jnp.concatenate([q_r, q_i], axis=0).astype(BF16)


def sweeps_kernel(coef_ref, q_ref):
    for b in range(q_ref.shape[0]):
        q_ref[b] = sweeps_matrix(coef_ref[:, b * TILE : (b + 3) * TILE])


def mix_kernel(got_ref, mine_ref, a_ref, b_ref, range_ref, out_a_ref, out_b_ref):
    shape = got_ref.shape
    got = got_ref[...].astype(F32)
    here = iota(shape, 0) % ROWS == COEF
    range_ref[...] = jnp.where(here, got, mine_ref[...].astype(F32)).astype(BF16)
    first, last = got[:16], got[shape[0] - 16 :]
    last = pltpu.roll(last, ROWS, 0)
    is_even = even("bus")
    out_a_ref[:16, :] = jnp.where(is_even, last, first)
    out_b_ref[:16, :] = jnp.where(is_even, first, last)
    out_a_ref[16:, :] = a_ref[...]
    out_b_ref[16:, :] = b_ref[...]


def network_kernel(got_ref, a_ref, b_ref, q_ref, coef_ref, volt_ref, rows, inject):
    rows[...] = got_ref[...].astype(F32)
    is_even = even("bus")
    low = jnp.where(is_even, b_ref[...], a_ref[...])
    high = jnp.where(is_even, a_ref[...], b_ref[...])

    def part(p):
        return jnp.concatenate(
            [
                rows[pl.ds(h * HALF * ROWS + 2 * c + p, HALF, stride=ROWS), :]
                for h in range(2)
                for c in range(CONV)
            ],
            axis=0,
        )

    spectra = jnp.concatenate([part(0), part(1)], axis=1).astype(BF16)
    convs = H * CONV
    at = [
        jnp.sum(rows[pl.ds(h * HALF * ROWS + MARK, HALF, stride=ROWS), :], axis=0, keepdims=True)
        for h in range(2)
    ]
    at = jnp.concatenate(at, axis=1).astype(I32)
    lane = iota((1, convs), 1)
    source = lane // (CONV * HALF) * HALF + lane % HALF
    target = source * SUB + at
    buses = H * SUB
    owner = jnp.where(iota((buses, convs), 0) == target, 1.0, 0.0).astype(BF16)
    inject[EDGE : EDGE + buses, :] = jnp.dot(owner, spectra, preferred_element_type=F32).astype(BF16)
    for edge, lane0, row0 in ((low, HALF - 1, 0), (high, 0, EDGE + buses)):
        total_r = jnp.zeros((SUB, 128), F32)
        total_i = jnp.zeros((SUB, 128), F32)
        for c in range(CONV):
            at = c * HALF + lane0
            bus = jnp.broadcast_to(edge[MARK : MARK + 1, at : at + 1], (SUB, 128)).astype(I32)
            here = iota((SUB, 128), 0) == bus
            total_r += jnp.where(here, edge[2 * c : 2 * c + 1, :], 0.0)
            total_i += jnp.where(here, edge[2 * c + 1 : 2 * c + 2, :], 0.0)
        inject[row0 : row0 + EDGE, :] = jnp.concatenate([total_r, total_i], axis=1).astype(BF16)
    tail = 2 * EDGE + buses
    inject[tail:, :] = jnp.zeros((inject.shape[0] - tail, 256), BF16)
    tiles = buses // TILE
    for b in range(tiles):
        if b == 0:
            matrix = sweeps_matrix(jnp.concatenate([low[16:], coef_ref[:, : 2 * TILE]], axis=1))
        elif b == tiles - 1:
            matrix = sweeps_matrix(jnp.concatenate([coef_ref[:, buses - 2 * TILE :], high[16:]], axis=1))
        else:
            matrix = q_ref[b - 1]
        acc = jnp.dot(matrix, inject[b * TILE : b * TILE + WIN, :], preferred_element_type=F32)
        volt_ref[0, 0, b * TILE : b * TILE + TILE, :] = (acc[:TILE, :128] - acc[TILE:, 128:]).astype(BF16)
        volt_ref[1, 0, b * TILE : b * TILE + TILE, :] = (acc[:TILE, 128:] + acc[TILE:, :128]).astype(BF16)


def swapped(x):
    return pltpu.roll(x, 64, 1)


def packed_product(a, b, real):
    turned = swapped(b)
    return a * jnp.where(real, b, turned) + swapped(a) * jnp.where(real, -turned, b)


def lift_kernel(mine_ref, a_ref, spec_ref, mark_ref, rows):
    size = mine_ref.shape[0]
    rows[:size, :] = mine_ref[...].astype(F32)
    rows[size:, :] = a_ref[...].astype(F32)
    for q in range(2):
        for o in range(2 * CONV):
            at = (q * 2 * CONV + o) * H
            spec_ref[at : at + H, :] = rows[pl.ds(q * size + o, H, stride=ROWS), :]
        mark_ref[q : q + 1, :] = rows[q * size + MARK : q * size + MARK + 1, :]


def near_kernel(aux_ref, got_ref, spec_ref, mark_ref, b_ref, out_ref, coefs, rows, out):
    coefs[...] = got_ref[...].astype(F32)
    rows[...] = b_ref[...].astype(F32)
    harm = lax.axis_index("harm")
    is_even = even("harm")
    a_at = jnp.where(is_even, 2, 0)
    b_at = 2 - a_at

    shape = (8, 128)
    lane = iota(shape, 1)
    real = lane < 64
    path = lane % 16
    spans = [aux_ref[4:5, :128], aux_ref[5:6, :128], rows[SPAN : SPAN + 1, :]]
    spans = [jnp.broadcast_to(x, shape).astype(I32) for x in spans]

    def place(bus, line):
        at = bus // SUB
        slot = jnp.where(at == 1, 0, jnp.where(at == a_at, 1, 2))
        return slot, line * SUB + bus % SUB

    def hop(bus, line):
        slot, at = place(bus, jnp.maximum(line - 1, 0))
        found = [jnp.take_along_axis(x, at, axis=1) for x in spans]
        far = jnp.where(slot == 0, found[0], jnp.where(slot == 1, found[1], found[2]))
        return bus + jnp.where(line == 0, 0, far)

    def coef_at(bus, line, used):
        slot, at = place(bus, line)
        return jnp.where(used, slot * 128 + at + jnp.where(real, 0, 64), -1)[:1]

    bus0 = jnp.broadcast_to(aux_ref[3:4, :128], shape).astype(I32)
    valid = path < 1 + LINKS + LINKS * LINKS
    two = (path >= 1 + LINKS) & valid
    line1 = jnp.where(two, 1 + (path - 1 - LINKS) // LINKS, jnp.where(valid, path, 0))
    line2 = jnp.where(two, 1 + (path - 1 - LINKS) % LINKS, 0)
    bus1 = hop(bus0, line1)
    bus2 = hop(bus1, line2)
    places = [coef_at(bus0, line1, valid & (path >= 1)), coef_at(bus1, line2, two), coef_at(bus2, 0, valid)]
    pick = jnp.where(iota((3 * 128, 3 * 128), 0) == jnp.concatenate(places, axis=1), 1.0, 0.0).astype(BF16)
    window = jnp.concatenate(
        [
            coefs[pl.ds(COEF, H, stride=ROWS), :],
            coefs[pl.ds(PAIR, H, stride=ROWS), :],
            rows[pl.ds(COEF, H, stride=ROWS), :],
        ],
        axis=1,
    ).astype(BF16)
    found = jnp.dot(window, pick, preferred_element_type=F32)
    real, path = real[:1], path[:1]
    first = found[:, :128] + jnp.where(real & (path == 0), 1.0, 0.0)
    second = found[:, 128:256] + jnp.where(real & (path <= LINKS), 1.0, 0.0)
    weight = packed_product(packed_product(first, second, real), found[:, 256:], real)

    many = (128, 128)
    row = iota(many, 0)
    other = row % 64 % (3 * CONV)
    bus_of = jnp.zeros(many, I32)
    marks = [mark_ref[0:1, :], mark_ref[1:2, :], rows[MARK : MARK + 1, :]]
    beside = jnp.where(is_even, 1, -1)
    for q, (at, column) in enumerate(((1, harm), (a_at, harm + beside), (b_at, harm - beside))):
        column = lax.rem(column + HALF, HALF)
        for c in range(CONV):
            bus = jnp.sum(jnp.where(iota((1, 128), 1) == c * HALF + column, marks[q], 0.0), axis=1, keepdims=True)
            bus = jnp.broadcast_to(bus.astype(I32), many) + at * SUB
            bus_of = jnp.where(other == q * CONV + c, bus, bus_of)
    wide = iota(many, 1)
    match = (row // 64 == wide // 64) & (row % 64 // (3 * CONV) == wide % 64 // 16) & (bus_of == bus2[:1])
    match = jnp.where(match, 1.0, 0.0).astype(BF16)
    high = weight.astype(BF16)
    rest = (weight - high.astype(F32)).astype(BF16)
    dims = (((1,), (1,)), ((), ()))
    table = lax.dot_general(high, match, dims, preferred_element_type=F32)
    table += lax.dot_general(rest, match, dims, preferred_element_type=F32)

    total = [[jnp.zeros((H, 128), F32) for _ in range(2)] for _ in range(CONV)]
    for q in range(3):
        for o in range(CONV):
            if q < 2:
                at = (q * CONV + o) * 2 * H
                spec_r, spec_i = spec_ref[at : at + H, :], spec_ref[at + H : at + 2 * H, :]
            else:
                spec_r, spec_i = (rows[pl.ds(2 * o + p, H, stride=ROWS), :] for p in range(2))
            for c in range(CONV):
                at = c * 3 * CONV + q * CONV + o
                add_r, add_i = product(table[:, at : at + 1], table[:, 64 + at : 65 + at], spec_r, spec_i)
                total[c][0] += add_r
                total[c][1] += add_i
    for c in range(CONV):
        for p in range(2):
            out[pl.ds(p * H * CONV + c, H, stride=CONV), :] = total[c][p]
    out_ref[...] = out[...].astype(BF16)


VMEM = pl.BlockSpec(memory_space=pltpu.VMEM)
HBM = pl.BlockSpec(memory_space=pltpu.HBM)


def call(kernel, name, out_shape, in_specs, scratch=(), cost=(0, 0, 0)):
    flops, moved, hard = cost
    return pl.pallas_call(
        kernel,
        out_shape=out_shape,
        in_specs=in_specs,
        out_specs=jax.tree.map(lambda _: VMEM, out_shape),
        scratch_shapes=list(scratch),
        compiler_params=pltpu.CompilerParams(vmem_limit_bytes=40 * 2**20),
        cost_estimate=pl.CostEstimate(flops=flops, bytes_accessed=moved, transcendentals=hard),
        name=name,
    )


def swaps(count):
    rounds = []
    for start in (0, 1):
        firsts = range(start, count - 1, 2)
        rounds.append([(i, i + 1) for i in firsts] + [(i + 1, i) for i in firsts])
    return rounds


def local(conv_volt, conv_power, conv_type, type_steep, conv_bus, admittance, link_offset):
    harm_count = lax.axis_size("harm")
    bus_count = lax.axis_size("bus")
    block = admittance.shape[3]
    snapshots = conv_volt.shape[3]
    tiles = block // TILE
    size = harm_count * ROWS
    kinds = 2 * H
    S = jax.ShapeDtypeStruct
    over_bus = swaps(bus_count)
    number = lambda r: r % harm_count * bus_count + r // harm_count
    over_ranges = [[(number(s), number(d)) for s, d in pairs] for pairs in swaps(harm_count * bus_count)]

    basis = make_basis()
    coef, edge_a, edge_b, aux, group, volt, turned, basis = call(
        prepare_kernel,
        "prepare",
        (
            S((16, block), F32),
            S((16, 128), F32),
            S((16, 128), F32),
            S((8, CONV * 128), F32),
            S((harm_count, 128), F32),
            S((kinds * CONV, snapshots), BF16),
            S((NT, kinds), BF16),
            S((kinds, NT), BF16),
        ),
        [HBM] * 9,
        [
            pltpu.VMEM((2, 4, 1, block), F32),
            pltpu.VMEM((LINKS, block), I32),
            pltpu.SMEM((CONV,), I32),
            pltpu.SMEM(type_steep.shape, F32),
            pltpu.SMEM((CONV,), I32),
            pltpu.VMEM((CONV, snapshots), F32),
            pltpu.VMEM((harm_count, 128), F32),
            pltpu.SemaphoreType.DMA((9,)),
        ],
    )(
        *(
            pltpu.with_memory_space_constraint(array, pltpu.HBM)
            for array in (
                admittance,
                link_offset,
                conv_type,
                type_steep,
                conv_bus,
                conv_power,
                conv_volt.reshape(kinds * CONV, snapshots),
                jnp.asarray(np.ascontiguousarray(basis.T)),
                jnp.asarray(basis),
            )
        )
    )
    payload = call(
        convert_kernel,
        "convert",
        S((size, 128), BF16),
        [VMEM] * 5,
        [pltpu.VMEM((kinds * CONV, 128), F32), pltpu.VMEM((size, 128), F32)],
        (2 * 2 * 128 * 1024 * 512, 2**20, 2**19),
    )(volt, turned, basis, aux, group)

    four = (harm_count, ROWS // 4, 4, snapshots)
    got = lax.all_to_all(payload.reshape(four), "harm", split_axis=0, concat_axis=0, tiled=True)

    beside_a = lax.ppermute(payload, ("harm", "bus"), over_ranges[0])
    q = call(
        sweeps_kernel,
        "sweeps",
        S((tiles - 2, 2 * TILE, WIN), BF16),
        [VMEM],
        cost=(2 * tiles * 256 * 256 * 512, 2**20, 0),
    )(coef)
    spec, mark = call(
        lift_kernel,
        "lift",
        (S((2 * 2 * CONV * H, 128), F32), S((8, 128), F32)),
        [VMEM] * 2,
        [pltpu.VMEM((2 * size, 128), F32)],
        (10**6, 2**20, 0),
    )(payload, beside_a)
    got, q, spec, mark = lax.optimization_barrier((got, q, spec, mark))

    got = got.reshape(size, snapshots)
    beside_b, halo_a, halo_b = call(
        mix_kernel, "mix", (S((size, 128), BF16), S((32, 128), F32), S((32, 128), F32)), [VMEM] * 4
    )(got, payload, edge_a, edge_b)
    beside_b = lax.ppermute(beside_b, ("harm", "bus"), over_ranges[1])
    halo_a = lax.ppermute(halo_a, "bus", over_bus[0])
    halo_b = lax.ppermute(halo_b, "bus", over_bus[1])
    near = call(
        near_kernel,
        "near",
        S((kinds * CONV, snapshots), BF16),
        [VMEM] * 5,
        [pltpu.VMEM((size, 128), F32), pltpu.VMEM((size, 128), F32), pltpu.VMEM((kinds * CONV, 128), F32)],
        (2 * 10**7, 2**20, 0),
    )(aux, got, spec, mark, beside_b)
    bus_volt = call(
        network_kernel,
        "network",
        S((2, 1, block, snapshots), BF16),
        [VMEM] * 5,
        [pltpu.VMEM((size, 128), F32), pltpu.VMEM((block + WIN - TILE, 256), BF16)],
        (2 * tiles * 256 * 256 * 256, 2**20, 0),
    )(got, halo_a, halo_b, q, coef)
    return (bus_volt, near.reshape(2, H, CONV, snapshots))


def solution(mesh):
    in_specs = (
        P(None, None, ("bus", "harm"), None),
        P(("bus", "harm"), None),
        P(("bus", "harm")),
        P(),
        P(("bus", "harm")),
        P(None, None, "harm", "bus"),
        P(None, "bus"),
    )
    out_specs = (P(None, "harm", "bus", None), P(None, None, ("bus", "harm"), None))
    return jax.shard_map(local, mesh=mesh, in_specs=in_specs, out_specs=out_specs, check_vma=False)
```

```python
import math

import jax
import jax.numpy as jnp
import numpy as np
from jax import lax
from jax.experimental import pallas as pl
from jax.experimental.pallas import tpu as pltpu
from jax.sharding import PartitionSpec as P

H = 64
NT = 1024
REACH = 8
LINKS = 3
SUB = 16
CONV = 4
EDGE = 2 * REACH
TILE = 128
WIN = 256
ROWS = 12
COEF = 8
PAIR = 9
SPAN = 10
MARK = 11
LIFT = 8 * H
HALF = 32
F32 = jnp.float32
BF16 = jnp.bfloat16
I32 = jnp.int32


def make_basis():
    turn = np.arange(1, H + 1)[:, None] * np.arange(NT)[None, :] % NT
    angle = turn * (2.0 * math.pi / NT)
    return np.concatenate([np.cos(angle), -np.sin(angle)], axis=0).astype(BF16)


def iota(shape, dim):
    return lax.broadcasted_iota(I32, shape, dim)


def product(ar, ai, br, bi):
    return ar * br - ai * bi, ar * bi + ai * br


def grouped(x):
    k, j = iota((8, 128), 0), iota((8, 128), 1) // SUB
    for s in (1, 2, 4):
        later = pltpu.roll(pltpu.roll(x, s, 0), 128 - SUB * s, 1)
        sooner = pltpu.roll(pltpu.roll(x, 8 - s, 0), SUB * s, 1)
        bk, bj = (k // s) % 2, (j // s) % 2
        x = jnp.where(bk == bj, x, jnp.where(bk == 1, later, sooner))
    return x


def even(axis):
    return lax.rem(lax.axis_index(axis), 2) == 0


def begin_kernel(
    adm_hbm, off_hbm, type_hbm, steep_hbm, bus_hbm, power_hbm, volt_hbm, turned_hbm, basis_hbm,
    coef_ref, a_ref, b_ref, aux_ref, out_ref, lift_ref,
    adm, off, kind, steep, bus, power, volt_in, turned, basis, volts, groups, spans, rows, sems,
):
    pairs = [
        (adm_hbm, adm), (off_hbm, off), (type_hbm, kind), (steep_hbm, steep), (bus_hbm, bus), (power_hbm, power),
        (volt_hbm, volt_in), (turned_hbm, turned), (basis_hbm, basis),
    ]
    copies = [pltpu.make_async_copy(src, dst, sems.at[i]) for i, (src, dst) in enumerate(pairs)]
    for copy in copies:
        copy.start()
    for copy in copies[:2]:
        copy.wait()
    inv_r, inv_i = adm[0, 0], adm[1, 0]
    steps = [product(inv_r, inv_i, adm[0, k], adm[1, k]) for k in range(1, 1 + LINKS)]
    blank = jnp.zeros((5, inv_r.shape[1]), F32)
    coefs = jnp.concatenate(
        [inv_r] + [s[0] for s in steps] + [inv_i] + [s[1] for s in steps] + [off[...].astype(F32), blank], axis=0
    )
    coef_ref[...] = coefs
    tiles = coefs.shape[1] // 128
    for v in range(tiles):
        groups[v * 8 : v * 8 + 8, :] = grouped(coefs[:8, v * 128 : v * 128 + 128])
        spans[v * 8 : v * 8 + 8, :] = grouped(coefs[8:, v * 128 : v * 128 + 128])
    first, last = coefs[:, :128], coefs[:, tiles * 128 - 128 :]
    is_even = even("bus")
    a_ref[...] = jnp.where(is_even, last, first)
    b_ref[...] = jnp.where(is_even, first, last)
    harm = lax.axis_index("harm")
    span = spans[pl.ds(harm, 1), :]
    aux_ref[1:2, :] = span
    aux_ref[2:3, :] = spans[pl.ds(harm + jnp.where(even("harm"), 1, -1), 1), :]
    group = groups[...]
    pair = jnp.where(iota((H, 128), 0) % 2 == 0, pltpu.roll(group, H - 1, 0), pltpu.roll(group, 1, 0))
    rows[pl.ds(COEF, H, stride=ROWS), :] = group
    rows[pl.ds(PAIR, H, stride=ROWS), :] = pair
    rows[pl.ds(SPAN, H, stride=ROWS), :] = jnp.broadcast_to(span, (H, 128))

    for copy in copies[2:]:
        copy.wait()
    lane = iota((1, 128), 1)
    column = lax.rem(harm, HALF)
    mark = jnp.zeros((1, 128), F32)
    start = jnp.full((1, 128), SUB, F32)
    for c in range(CONV):
        number = lax.rem(bus[c], SUB).astype(F32)
        mark += jnp.where(lane == c * HALF + column, number, 0.0)
        start += jnp.where(lane % 64 // 16 == c, number, 0.0)
    aux_ref[0:1, :] = start
    rows[pl.ds(MARK, H, stride=ROWS), :] = jnp.broadcast_to(mark, (H, 128))

    volts[...] = volt_in[...].astype(F32)
    kinds = 2 * H
    volt = jnp.concatenate(
        [volts[pl.ds(c, kinds, stride=CONV), :] for c in range(CONV)], axis=1
    ).astype(BF16)
    sharp = jnp.concatenate([jnp.full((1, 128), steep[kind[c]], F32) for c in range(CONV)], axis=1)
    strong = jnp.concatenate([power[c : c + 1, :] for c in range(CONV)], axis=1)
    spectra = jnp.zeros((kinds, CONV * 128), F32)
    step = 256
    for n in range(0, NT, step):
        wave = jnp.dot(turned[n : n + step, :], volt, preferred_element_type=F32)
        current = (strong * jnp.tanh(sharp * wave)).astype(BF16)
        spectra += jnp.dot(basis[:, n : n + step], current, preferred_element_type=F32)
    spectra = spectra * NT ** (-0.5)
    for c in range(CONV):
        for p in range(2):
            piece = spectra[p * H : p * H + H, c * 128 : c * 128 + 128]
            at = (2 * c + p) * H
            rows[pl.ds(2 * c + p, H, stride=ROWS), :] = piece
            lift_ref[at : at + H, :] = piece.astype(BF16)
    row = iota((16, 128), 0)
    notes = jnp.where(row == 0, span, jnp.where(row == 1, mark, 0.0))
    lift_ref[LIFT:, :] = notes.astype(BF16)
    out_ref[...] = rows[...].astype(BF16)


def sweeps_matrix(coefs):
    coefs = pltpu.roll(coefs, 3 * TILE - (TILE - EDGE), 1)[:, :WIN]
    rows = iota((WIN, WIN), 0)
    lanes = iota((1, WIN), 1)
    turned_r = jnp.zeros((WIN, WIN), F32)
    turned_i = jnp.zeros((WIN, WIN), F32)
    for k in range(LINKS):
        here = rows == lanes + coefs[8 + k : 9 + k].astype(I32)
        turned_r += jnp.where(here, coefs[1 + k : 2 + k], 0.0)
        turned_i += jnp.where(here, coefs[5 + k : 6 + k], 0.0)
    step_r, step_i = turned_r.T, turned_i.T
    mid_r, mid_i = step_r[EDGE : EDGE + TILE], step_i[EDGE : EDGE + TILE]
    twice = jnp.dot(
        jnp.concatenate([mid_r, mid_i], axis=0).astype(BF16),
        jnp.concatenate([step_r, step_i], axis=1).astype(BF16),
        preferred_element_type=F32,
    )
    same = iota((TILE, WIN), 0) + EDGE == iota((TILE, WIN), 1)
    all_r = twice[:TILE, :WIN] - twice[TILE:, WIN:] + mid_r + jnp.where(same, 1.0, 0.0)
    all_i = twice[:TILE, WIN:] + twice[TILE:, :WIN] + mid_i
    q_r, q_i = product(all_r, all_i, coefs[0:1], coefs[4:5])
    return jnp.concatenate([q_r, q_i], axis=0).astype(BF16)


def sweeps_kernel(coef_ref, q_ref):
    for b in range(q_ref.shape[0]):
        q_ref[b] = sweeps_matrix(coef_ref[:, b * TILE : (b + 3) * TILE])


def mix_kernel(got_ref, lift_ref, a_ref, b_ref, rows_ref, range_ref, out_a_ref, out_b_ref):
    size = got_ref.shape[0]
    rows_ref[...] = got_ref[...].astype(F32)
    range_ref[: LIFT + 16, :] = lift_ref[...]
    range_ref[LIFT + 16 :, :] = rows_ref[pl.ds(COEF, H, stride=ROWS), :].astype(BF16)
    first, last = rows_ref[:16, :], pltpu.roll(rows_ref[size - 16 :, :], ROWS, 0)
    is_even = even("bus")
    out_a_ref[:16, :] = jnp.where(is_even, last, first)
    out_b_ref[:16, :] = jnp.where(is_even, first, last)
    out_a_ref[16:, :] = a_ref[...]
    out_b_ref[16:, :] = b_ref[...]


def volt_of(matrix, inject):
    acc = jnp.dot(matrix, inject, preferred_element_type=F32)
    return (acc[:TILE, :128] - acc[TILE:, 128:]).astype(BF16), (acc[:TILE, 128:] + acc[TILE:, :128]).astype(BF16)


def inner_network(rows, q_ref, inject, volt, volt_hbm, sems):
    def part(p):
        return jnp.concatenate(
            [
                rows[pl.ds(h * HALF * ROWS + 2 * c + p, HALF, stride=ROWS), :]
                for h in range(2)
                for c in range(CONV)
            ],
            axis=0,
        )

    spectra = jnp.concatenate([part(0), part(1)], axis=1).astype(BF16)
    convs = H * CONV
    at = [
        jnp.sum(rows[pl.ds(h * HALF * ROWS + MARK, HALF, stride=ROWS), :], axis=0, keepdims=True)
        for h in range(2)
    ]
    at = jnp.concatenate(at, axis=1).astype(I32)
    lane = iota((1, convs), 1)
    source = lane // (CONV * HALF) * HALF + lane % HALF
    target = source * SUB + at
    buses = H * SUB
    owner = jnp.where(iota((buses, convs), 0) == target, 1.0, 0.0).astype(BF16)
    inject[...] = jnp.dot(owner, spectra, preferred_element_type=F32).astype(BF16)
    for b in range(1, buses // TILE - 1):
        window = inject[b * TILE - EDGE : b * TILE - EDGE + WIN, :]
        volt[0, 0, b * TILE : b * TILE + TILE, :], volt[1, 0, b * TILE : b * TILE + TILE, :] = volt_of(
            q_ref[b - 1], window
        )
    inner = pl.ds(TILE, buses - 2 * TILE)
    copies = [pltpu.make_async_copy(volt.at[p, 0, inner], volt_hbm.at[p, 0, inner], sems.at[p]) for p in range(2)]
    for copy in copies:
        copy.start()
    return copies


def edge_kernel(a_ref, b_ref, inject_ref, coef_ref, done_hbm, volt_hbm, volt, sems):
    del done_hbm
    is_even = even("bus")
    low = jnp.where(is_even, b_ref[...], a_ref[...])
    high = jnp.where(is_even, a_ref[...], b_ref[...])
    buses = inject_ref.shape[0]

    def injected(edge, lane0):
        total_r = jnp.zeros((SUB, 128), F32)
        total_i = jnp.zeros((SUB, 128), F32)
        for c in range(CONV):
            at = c * HALF + lane0
            bus = jnp.broadcast_to(edge[MARK : MARK + 1, at : at + 1], (SUB, 128)).astype(I32)
            here = iota((SUB, 128), 0) == bus
            total_r += jnp.where(here, edge[2 * c : 2 * c + 1, :], 0.0)
            total_i += jnp.where(here, edge[2 * c + 1 : 2 * c + 2, :], 0.0)
        return jnp.concatenate([total_r, total_i], axis=1).astype(BF16)

    rest = WIN - TILE - 2 * EDGE
    windows = [
        jnp.concatenate([injected(low, HALF - 1), inject_ref[: WIN - EDGE, :]], axis=0),
        jnp.concatenate(
            [inject_ref[buses - TILE - EDGE :, :], injected(high, 0), jnp.zeros((rest, 256), BF16)], axis=0
        ),
    ]
    coefs = [
        jnp.concatenate([low[16:], coef_ref[:, : 2 * TILE]], axis=1),
        jnp.concatenate([coef_ref[:, buses - 2 * TILE :], high[16:]], axis=1),
    ]
    copies = []
    for e in range(2):
        volt[e, 0], volt[e, 1] = volt_of(sweeps_matrix(coefs[e]), windows[e])
        for p in range(2):
            place = volt_hbm.at[p, 0, pl.ds(e * (buses - TILE), TILE)]
            copies.append(pltpu.make_async_copy(volt.at[e, p], place, sems.at[2 * e + p]))
            copies[-1].start()
    for copy in copies:
        copy.wait()


def swapped(x):
    return pltpu.roll(x, 64, 1)


def packed_product(a, b, real):
    turned = swapped(b)
    return a * jnp.where(real, b, turned) + swapped(a) * jnp.where(real, -turned, b)


def solve_kernel(
    aux_ref, rows, mine_ref, a_ref, b_ref, q_ref, inject_ref, near_hbm, volt_hbm, near, volt, out, sems
):
    copies = inner_network(rows, q_ref, inject_ref, volt, volt_hbm, sems)
    near_converters(aux_ref, rows, (mine_ref, a_ref, b_ref), out)
    near[...] = out[...].astype(BF16)
    copies.append(pltpu.make_async_copy(near, near_hbm, sems.at[2]))
    copies[-1].start()
    for copy in copies:
        copy.wait()


def near_converters(aux_ref, rows, lifts, out):
    harm = lax.axis_index("harm")
    is_even = even("harm")
    a_at = jnp.where(is_even, 2, 0)
    b_at = 2 - a_at

    shape = (8, 128)
    lane = iota(shape, 1)
    real = lane < 64
    path = lane % 16
    notes = [ref[LIFT : LIFT + 16, :].astype(F32) for ref in lifts]
    spans = [aux_ref[1:2, :], aux_ref[2:3, :], notes[2][:1]]
    spans = [jnp.broadcast_to(x, shape).astype(I32) for x in spans]

    def place(bus, line):
        at = bus // SUB
        slot = jnp.where(at == 1, 0, jnp.where(at == a_at, 1, 2))
        return slot, line * SUB + bus % SUB

    def hop(bus, line):
        slot, at = place(bus, jnp.maximum(line - 1, 0))
        found = [jnp.take_along_axis(x, at, axis=1) for x in spans]
        far = jnp.where(slot == 0, found[0], jnp.where(slot == 1, found[1], found[2]))
        return bus + jnp.where(line == 0, 0, far)

    def coef_at(bus, line, used):
        slot, at = place(bus, line)
        return jnp.where(used, slot * 128 + at + jnp.where(real, 0, 64), -1)[:1]

    bus0 = jnp.broadcast_to(aux_ref[0:1, :], shape).astype(I32)
    valid = path < 1 + LINKS + LINKS * LINKS
    two = (path >= 1 + LINKS) & valid
    line1 = jnp.where(two, 1 + (path - 1 - LINKS) // LINKS, jnp.where(valid, path, 0))
    line2 = jnp.where(two, 1 + (path - 1 - LINKS) % LINKS, 0)
    bus1 = hop(bus0, line1)
    bus2 = hop(bus1, line2)
    places = [coef_at(bus0, line1, valid & (path >= 1)), coef_at(bus1, line2, two), coef_at(bus2, 0, valid)]
    pick = jnp.where(iota((3 * 128, 3 * 128), 0) == jnp.concatenate(places, axis=1), 1.0, 0.0).astype(BF16)
    window = jnp.concatenate(
        [
            rows[pl.ds(COEF, H, stride=ROWS), :].astype(BF16),
            rows[pl.ds(PAIR, H, stride=ROWS), :].astype(BF16),
            lifts[2][LIFT + 16 :, :],
        ],
        axis=1,
    )
    found = jnp.dot(window, pick, preferred_element_type=F32)
    real, path = real[:1], path[:1]
    first = found[:, :128] + jnp.where(real & (path == 0), 1.0, 0.0)
    second = found[:, 128:256] + jnp.where(real & (path <= LINKS), 1.0, 0.0)
    weight = packed_product(packed_product(first, second, real), found[:, 256:], real)

    many = (128, 128)
    row = iota(many, 0)
    other = row % 64 % (3 * CONV)
    bus_of = jnp.zeros(many, I32)
    marks = [x[1:2] for x in notes]
    beside = jnp.where(is_even, 1, -1)
    for q, (at, column) in enumerate(((1, harm), (a_at, harm + beside), (b_at, harm - beside))):
        column = lax.rem(column + HALF, HALF)
        for c in range(CONV):
            bus = jnp.sum(jnp.where(iota((1, 128), 1) == c * HALF + column, marks[q], 0.0), axis=1, keepdims=True)
            bus = jnp.broadcast_to(bus.astype(I32), many) + at * SUB
            bus_of = jnp.where(other == q * CONV + c, bus, bus_of)
    wide = iota(many, 1)
    match = (row // 64 == wide // 64) & (row % 64 // (3 * CONV) == wide % 64 // 16) & (bus_of == bus2[:1])
    match = jnp.where(match, 1.0, 0.0).astype(BF16)
    high = weight.astype(BF16)
    rest = (weight - high.astype(F32)).astype(BF16)
    dims = (((1,), (1,)), ((), ()))
    table = lax.dot_general(high, match, dims, preferred_element_type=F32)
    table += lax.dot_general(rest, match, dims, preferred_element_type=F32)

    total = [[jnp.zeros((H, 128), F32) for _ in range(2)] for _ in range(CONV)]
    for q in range(3):
        for o in range(CONV):
            spec_r, spec_i = (lifts[q][(2 * o + p) * H : (2 * o + p + 1) * H, :].astype(F32) for p in range(2))
            for c in range(CONV):
                at = c * 3 * CONV + q * CONV + o
                add_r, add_i = product(table[:, at : at + 1], table[:, 64 + at : 65 + at], spec_r, spec_i)
                total[c][0] += add_r
                total[c][1] += add_i
    for c in range(CONV):
        for p in range(2):
            out[pl.ds(p * H * CONV + c, H, stride=CONV), :] = total[c][p]


VMEM = pl.BlockSpec(memory_space=pltpu.VMEM)
HBM = pl.BlockSpec(memory_space=pltpu.HBM)


def call(kernel, name, out_shape, in_specs, scratch=(), cost=(0, 0, 0), out_specs=None, aliases=None):
    flops, moved, hard = cost
    return pl.pallas_call(
        kernel,
        out_shape=out_shape,
        in_specs=in_specs,
        out_specs=out_specs or jax.tree.map(lambda _: VMEM, out_shape),
        input_output_aliases=aliases or {},
        scratch_shapes=list(scratch),
        compiler_params=pltpu.CompilerParams(vmem_limit_bytes=40 * 2**20),
        cost_estimate=pl.CostEstimate(flops=flops, bytes_accessed=moved, transcendentals=hard),
        name=name,
    )


def swaps(count):
    rounds = []
    for start in (0, 1):
        firsts = range(start, count - 1, 2)
        rounds.append([(i, i + 1) for i in firsts] + [(i + 1, i) for i in firsts])
    return rounds


def local(conv_volt, conv_power, conv_type, type_steep, conv_bus, admittance, link_offset):
    harm_count = lax.axis_size("harm")
    bus_count = lax.axis_size("bus")
    block = admittance.shape[3]
    snapshots = conv_volt.shape[3]
    tiles = block // TILE
    size = harm_count * ROWS
    kinds = 2 * H
    S = jax.ShapeDtypeStruct
    over_bus = swaps(bus_count)
    number = lambda r: r % harm_count * bus_count + r // harm_count
    over_ranges = [[(number(s), number(d)) for s, d in pairs] for pairs in swaps(harm_count * bus_count)]

    basis = make_basis()
    coef, edge_a, edge_b, aux, payload, lift = call(
        begin_kernel,
        "begin",
        (
            S((16, block), F32),
            S((16, 128), F32),
            S((16, 128), F32),
            S((8, 128), F32),
            S((size, 128), BF16),
            S((LIFT + 16, 128), BF16),
        ),
        [HBM] * 9,
        [
            pltpu.VMEM((2, 4, 1, block), F32),
            pltpu.VMEM((LINKS, block), I32),
            pltpu.SMEM((CONV,), I32),
            pltpu.SMEM(type_steep.shape, F32),
            pltpu.SMEM((CONV,), I32),
            pltpu.VMEM((CONV, snapshots), F32),
            pltpu.VMEM((kinds * CONV, snapshots), BF16),
            pltpu.VMEM((NT, kinds), BF16),
            pltpu.VMEM((kinds, NT), BF16),
            pltpu.VMEM((kinds * CONV, snapshots), F32),
            pltpu.VMEM((harm_count, 128), F32),
            pltpu.VMEM((harm_count, 128), F32),
            pltpu.VMEM((size, 128), F32),
            pltpu.SemaphoreType.DMA((9,)),
        ],
        (2 * 2 * 128 * 1024 * 512, 2**20, 2**19),
    )(
        *(
            pltpu.with_memory_space_constraint(array, pltpu.HBM)
            for array in (
                admittance,
                link_offset,
                conv_type,
                type_steep,
                conv_bus,
                conv_power,
                conv_volt.reshape(kinds * CONV, snapshots),
                jnp.asarray(np.ascontiguousarray(basis.T)),
                jnp.asarray(basis),
            )
        )
    )

    four = (harm_count, ROWS // 4, 4, snapshots)
    got = lax.all_to_all(payload.reshape(four), "harm", split_axis=0, concat_axis=0, tiled=True)

    beside_a = lax.ppermute(lift, ("harm", "bus"), over_ranges[0])
    q = call(
        sweeps_kernel,
        "sweeps",
        S((tiles - 2, 2 * TILE, WIN), BF16),
        [VMEM],
        cost=(2 * tiles * 256 * 256 * 512, 2**20, 0),
    )(coef)
    got, q, beside_a = lax.optimization_barrier((got, q, beside_a))

    rows, beside_b, halo_a, halo_b = call(
        mix_kernel,
        "mix",
        (S((size, 128), F32), S((LIFT + 16 + H, 128), BF16), S((32, 128), F32), S((32, 128), F32)),
        [VMEM] * 4,
    )(got.reshape(size, snapshots), lift, edge_a, edge_b)
    beside_b = lax.ppermute(beside_b, ("harm", "bus"), over_ranges[1])
    halo_a = lax.ppermute(halo_a, "bus", over_bus[0])
    halo_b = lax.ppermute(halo_b, "bus", over_bus[1])
    out_volt = S((2, 1, block, snapshots), BF16)
    inject, near, bus_volt = call(
        solve_kernel,
        "solve",
        (S((block, 256), BF16), S((kinds * CONV, snapshots), BF16), out_volt),
        [VMEM] * 6,
        [
            pltpu.VMEM((kinds * CONV, snapshots), BF16),
            pltpu.VMEM((2, 1, block, snapshots), BF16),
            pltpu.VMEM((kinds * CONV, 128), F32),
            pltpu.SemaphoreType.DMA((3,)),
        ],
        (2 * tiles * 256 * 256 * 256, 2**20, 0),
        (VMEM, HBM, HBM),
    )(aux, rows, lift, beside_a, beside_b, q)
    halo_a, halo_b, near = lax.optimization_barrier((halo_a, halo_b, near))
    bus_volt = call(
        edge_kernel,
        "edge",
        out_volt,
        [VMEM] * 4 + [HBM],
        [pltpu.VMEM((2, 2, TILE, snapshots), BF16), pltpu.SemaphoreType.DMA((4,))],
        (4 * 256 * 256 * 512, 2**20, 0),
        HBM,
        {4: 0},
    )(halo_a, halo_b, inject, coef, bus_volt)
    return (bus_volt, near.reshape(2, H, CONV, snapshots))


def solution(mesh):
    in_specs = (
        P(None, None, ("bus", "harm"), None),
        P(("bus", "harm"), None),
        P(("bus", "harm")),
        P(),
        P(("bus", "harm")),
        P(None, None, "harm", "bus"),
        P(None, "bus"),
    )
    out_specs = (P(None, "harm", "bus", None), P(None, None, ("bus", "harm"), None))
    return jax.shard_map(local, mesh=mesh, in_specs=in_specs, out_specs=out_specs, check_vma=False)
```

```python
import math

import jax
import jax.numpy as jnp
import numpy as np
from jax import lax
from jax.experimental import pallas as pl
from jax.experimental.pallas import tpu as pltpu
from jax.sharding import PartitionSpec as P

H = 64
NT = 1024
REACH = 8
LINKS = 3
SUB = 16
CONV = 4
EDGE = 2 * REACH
TILE = 128
WIN = 256
ROWS = 12
COEF = 8
PAIR = 9
SPAN = 10
MARK = 11
LIFT = 8 * H
HALF = 32
F32 = jnp.float32
BF16 = jnp.bfloat16
I32 = jnp.int32


def make_basis():
    turn = np.arange(1, H + 1)[:, None] * np.arange(NT)[None, :] % NT
    angle = turn * (2.0 * math.pi / NT)
    return np.concatenate([np.cos(angle), -np.sin(angle)], axis=0).astype(BF16)


def iota(shape, dim):
    return lax.broadcasted_iota(I32, shape, dim)


def product(ar, ai, br, bi):
    return ar * br - ai * bi, ar * bi + ai * br


def grouped(x):
    k, j = iota((8, 128), 0), iota((8, 128), 1) // SUB
    for s in (1, 2, 4):
        later = pltpu.roll(pltpu.roll(x, s, 0), 128 - SUB * s, 1)
        sooner = pltpu.roll(pltpu.roll(x, 8 - s, 0), SUB * s, 1)
        bk, bj = (k // s) % 2, (j // s) % 2
        x = jnp.where(bk == bj, x, jnp.where(bk == 1, later, sooner))
    return x


def even(axis):
    return lax.rem(lax.axis_index(axis), 2) == 0


def begin_kernel(
    adm_hbm, off_hbm, type_hbm, steep_hbm, bus_hbm, power_hbm, volt_hbm, turned_hbm, basis_hbm,
    coef_ref, a_ref, b_ref, aux_ref, out_ref, lift_ref,
    adm, off, kind, steep, bus, power, volt_in, turned, basis, volts, groups, spans, rows, sems,
):
    pairs = [
        (adm_hbm, adm), (off_hbm, off), (type_hbm, kind), (steep_hbm, steep), (bus_hbm, bus), (power_hbm, power),
        (volt_hbm, volt_in), (turned_hbm, turned), (basis_hbm, basis),
    ]
    copies = [pltpu.make_async_copy(src, dst, sems.at[i]) for i, (src, dst) in enumerate(pairs)]
    for copy in copies:
        copy.start()
    for copy in copies:
        copy.wait()
    inv_r, inv_i = adm[0, 0], adm[1, 0]
    steps = [product(inv_r, inv_i, adm[0, k], adm[1, k]) for k in range(1, 1 + LINKS)]
    blank = jnp.zeros((5, inv_r.shape[1]), F32)
    coefs = jnp.concatenate(
        [inv_r] + [s[0] for s in steps] + [inv_i] + [s[1] for s in steps] + [off[...].astype(F32), blank], axis=0
    )
    coef_ref[...] = coefs
    tiles = coefs.shape[1] // 128
    for v in range(tiles):
        groups[v * 8 : v * 8 + 8, :] = grouped(coefs[:8, v * 128 : v * 128 + 128])
        spans[v * 8 : v * 8 + 8, :] = grouped(coefs[8:, v * 128 : v * 128 + 128])
    first, last = coefs[:, :128], coefs[:, tiles * 128 - 128 :]
    is_even = even("bus")
    a_ref[...] = jnp.where(is_even, last, first)
    b_ref[...] = jnp.where(is_even, first, last)
    harm = lax.axis_index("harm")
    span = spans[pl.ds(harm, 1), :]
    aux_ref[1:2, :] = span
    aux_ref[2:3, :] = spans[pl.ds(harm + jnp.where(even("harm"), 1, -1), 1), :]
    group = groups[...]
    pair = jnp.where(iota((H, 128), 0) % 2 == 0, pltpu.roll(group, H - 1, 0), pltpu.roll(group, 1, 0))
    rows[pl.ds(COEF, H, stride=ROWS), :] = group
    rows[pl.ds(PAIR, H, stride=ROWS), :] = pair
    rows[pl.ds(SPAN, H, stride=ROWS), :] = jnp.broadcast_to(span, (H, 128))

    lane = iota((1, 128), 1)
    column = lax.rem(harm, HALF)
    mark = jnp.zeros((1, 128), F32)
    start = jnp.full((1, 128), SUB, F32)
    for c in range(CONV):
        number = lax.rem(bus[c], SUB).astype(F32)
        mark += jnp.where(lane == c * HALF + column, number, 0.0)
        start += jnp.where(lane % 64 // 16 == c, number, 0.0)
    aux_ref[0:1, :] = start
    rows[pl.ds(MARK, H, stride=ROWS), :] = jnp.broadcast_to(mark, (H, 128))

    volts[...] = volt_in[...].astype(F32)
    kinds = 2 * H
    volt = jnp.concatenate(
        [volts[pl.ds(c, kinds, stride=CONV), :] for c in range(CONV)], axis=1
    ).astype(BF16)
    sharp = jnp.concatenate([jnp.full((1, 128), steep[kind[c]], F32) for c in range(CONV)], axis=1)
    strong = jnp.concatenate([power[c : c + 1, :] for c in range(CONV)], axis=1)
    spectra = jnp.zeros((kinds, CONV * 128), F32)
    step = 256
    for n in range(0, NT, step):
        wave = jnp.dot(turned[n : n + step, :], volt, preferred_element_type=F32)
        current = (strong * jnp.tanh(sharp * wave)).astype(BF16)
        spectra += jnp.dot(basis[:, n : n + step], current, preferred_element_type=F32)
    spectra = spectra * NT ** (-0.5)
    for c in range(CONV):
        for p in range(2):
            piece = spectra[p * H : p * H + H, c * 128 : c * 128 + 128]
            at = (2 * c + p) * H
            rows[pl.ds(2 * c + p, H, stride=ROWS), :] = piece
            lift_ref[at : at + H, :] = piece.astype(BF16)
    row = iota((16, 128), 0)
    notes = jnp.where(row == 0, span, jnp.where(row == 1, mark, 0.0))
    lift_ref[LIFT:, :] = notes.astype(BF16)
    out_ref[...] = rows[...].astype(BF16)


def sweeps_matrix(coefs, first, count):
    width = coefs.shape[1]
    rows = iota((width, width), 0)
    lanes = iota((1, width), 1)
    turned_r = jnp.zeros((width, width), F32)
    turned_i = jnp.zeros((width, width), F32)
    for k in range(LINKS):
        here = rows == lanes + coefs[8 + k : 9 + k].astype(I32)
        turned_r += jnp.where(here, coefs[1 + k : 2 + k], 0.0)
        turned_i += jnp.where(here, coefs[5 + k : 6 + k], 0.0)
    step_r, step_i = turned_r.T, turned_i.T
    mid_r, mid_i = step_r[first : first + count], step_i[first : first + count]
    twice = jnp.dot(
        jnp.concatenate([mid_r, mid_i], axis=0).astype(BF16),
        jnp.concatenate([step_r, step_i], axis=1).astype(BF16),
        preferred_element_type=F32,
    )
    same = iota((count, width), 0) + first == iota((count, width), 1)
    all_r = twice[:count, :width] - twice[count:, width:] + mid_r + jnp.where(same, 1.0, 0.0)
    all_i = twice[:count, width:] + twice[count:, :width] + mid_i
    q_r, q_i = product(all_r, all_i, coefs[0:1], coefs[4:5])
    return jnp.concatenate([q_r, q_i], axis=0).astype(BF16)


def volt_of(matrix, inject):
    count = matrix.shape[0] // 2
    acc = jnp.dot(matrix, inject, preferred_element_type=F32)
    return (acc[:count, :128] - acc[count:, 128:]).astype(BF16), (acc[:count, 128:] + acc[count:, :128]).astype(BF16)


def sweeps_kernel(coef_ref, q_ref):
    blank = jnp.zeros((coef_ref.shape[0], TILE), F32)
    tiles = q_ref.shape[0]
    for b in range(tiles):
        around = [coef_ref[:, t * TILE : t * TILE + TILE] if 0 <= t < tiles else blank for t in (b - 1, b, b + 1)]
        coefs = pltpu.roll(jnp.concatenate(around, axis=1), 2 * TILE + EDGE, 1)[:, :WIN]
        q_ref[b] = sweeps_matrix(coefs, EDGE, TILE)


def mix_kernel(got_ref, lift_ref, a_ref, b_ref, rows_ref, range_ref, out_a_ref, out_b_ref):
    size = got_ref.shape[0]
    rows_ref[...] = got_ref[...].astype(F32)
    range_ref[: LIFT + 16, :] = lift_ref[...]
    range_ref[LIFT + 16 :, :] = rows_ref[pl.ds(COEF, H, stride=ROWS), :].astype(BF16)
    first, last = rows_ref[:16, :], pltpu.roll(rows_ref[size - 16 :, :], ROWS, 0)
    is_even = even("bus")
    out_a_ref[:16, :] = jnp.where(is_even, last, first)
    out_b_ref[:16, :] = jnp.where(is_even, first, last)
    out_a_ref[16:, :] = a_ref[...]
    out_b_ref[16:, :] = b_ref[...]


def inner_kernel(rows, q_ref, inject, volt_hbm, volt, sems):
    def part(p):
        return jnp.concatenate(
            [
                rows[pl.ds(h * HALF * ROWS + 2 * c + p, HALF, stride=ROWS), :]
                for h in range(2)
                for c in range(CONV)
            ],
            axis=0,
        )

    spectra = jnp.concatenate([part(0), part(1)], axis=1).astype(BF16)
    convs = H * CONV
    at = [
        jnp.sum(rows[pl.ds(h * HALF * ROWS + MARK, HALF, stride=ROWS), :], axis=0, keepdims=True)
        for h in range(2)
    ]
    at = jnp.concatenate(at, axis=1).astype(I32)
    lane = iota((1, convs), 1)
    source = lane // (CONV * HALF) * HALF + lane % HALF
    target = source * SUB + at
    buses = H * SUB
    owner = jnp.where(iota((buses, convs), 0) == target, 1.0, 0.0).astype(BF16)
    inject[...] = jnp.dot(owner, spectra, preferred_element_type=F32).astype(BF16)
    tiles = q_ref.shape[0]
    copies = []
    for b in range(tiles):
        first = max(b * TILE - EDGE, 0)
        last = min(b * TILE - EDGE + WIN, buses)
        pieces = [jnp.zeros((n, 256), BF16) for n in (first - b * TILE + EDGE, b * TILE - EDGE + WIN - last)]
        pieces.insert(1, inject[first:last, :])
        window = jnp.concatenate([x for x in pieces if x.shape[0]], axis=0)
        volt[0, 0, b * TILE : b * TILE + TILE, :], volt[1, 0, b * TILE : b * TILE + TILE, :] = volt_of(
            q_ref[b], window
        )
        if b % 2:
            place = pl.ds(b * TILE - TILE, 2 * TILE)
            for p in range(2):
                copies.append(
                    pltpu.make_async_copy(volt.at[p, 0, place], volt_hbm.at[p, 0, place], sems.at[b - 1 + p])
                )
                copies[-1].start()
    for copy in copies:
        copy.wait()


def edges(low, high, inject_ref, coef_ref, volt):
    buses = inject_ref.shape[0]

    def injected(edge, lane0):
        total_r = jnp.zeros((SUB, 128), F32)
        total_i = jnp.zeros((SUB, 128), F32)
        for c in range(CONV):
            at = c * HALF + lane0
            bus = jnp.broadcast_to(edge[MARK : MARK + 1, at : at + 1], (SUB, 128)).astype(I32)
            here = iota((SUB, 128), 0) == bus
            total_r += jnp.where(here, edge[2 * c : 2 * c + 1, :], 0.0)
            total_i += jnp.where(here, edge[2 * c + 1 : 2 * c + 2, :], 0.0)
        return jnp.concatenate([total_r, total_i], axis=1).astype(BF16)

    coefs = jnp.concatenate([low[16:], coef_ref[:, :128]], axis=1)
    coefs = pltpu.roll(coefs, 128 + EDGE, 1)[:, :128]
    window = jnp.concatenate([injected(low, HALF - 1), inject_ref[: 128 - EDGE, :]], axis=0)
    volt[0, 0], volt[0, 1] = volt_of(sweeps_matrix(coefs, EDGE, EDGE), window)
    coefs = jnp.concatenate([coef_ref[:, buses - 128 :], high[16:]], axis=1)
    coefs = pltpu.roll(coefs, 256 - EDGE, 1)[:, :128]
    window = jnp.concatenate([inject_ref[buses - 128 + EDGE :, :], injected(high, 0)], axis=0)
    volt[1, 0], volt[1, 1] = volt_of(sweeps_matrix(coefs, 128 - 2 * EDGE, EDGE), window)


def swapped(x):
    return pltpu.roll(x, 64, 1)


def packed_product(a, b, real):
    turned = swapped(b)
    return a * jnp.where(real, b, turned) + swapped(a) * jnp.where(real, -turned, b)


def finish_kernel(
    aux_ref, rows, mine_ref, beside_a_ref, beside_b_ref, halo_a_ref, halo_b_ref, inject_ref, coef_ref, done_hbm,
    near_hbm, volt_hbm, near, volt, out, sems,
):
    del done_hbm
    is_even = even("bus")
    low = jnp.where(is_even, halo_b_ref[...], halo_a_ref[...])
    high = jnp.where(is_even, halo_a_ref[...], halo_b_ref[...])
    edges(low, high, inject_ref, coef_ref, volt)
    near_converters(aux_ref, rows, (mine_ref, beside_a_ref, beside_b_ref), out)
    near[...] = out[...].astype(BF16)
    copies = [pltpu.make_async_copy(near, near_hbm, sems.at[4])]
    for e in range(2):
        for p in range(2):
            place = volt_hbm.at[p, 0, pl.ds(e * (inject_ref.shape[0] - EDGE), EDGE)]
            copies.append(pltpu.make_async_copy(volt.at[e, p], place, sems.at[2 * e + p]))
    for copy in copies:
        copy.start()
    for copy in copies:
        copy.wait()


def near_converters(aux_ref, rows, lifts, out):
    harm = lax.axis_index("harm")
    is_even = even("harm")
    a_at = jnp.where(is_even, 2, 0)
    b_at = 2 - a_at

    shape = (8, 128)
    lane = iota(shape, 1)
    real = lane < 64
    path = lane % 16
    notes = [ref[LIFT : LIFT + 16, :].astype(F32) for ref in lifts]
    spans = [aux_ref[1:2, :], aux_ref[2:3, :], notes[2][:1]]
    spans = [jnp.broadcast_to(x, shape).astype(I32) for x in spans]

    def place(bus, line):
        at = bus // SUB
        slot = jnp.where(at == 1, 0, jnp.where(at == a_at, 1, 2))
        return slot, line * SUB + bus % SUB

    def hop(bus, line):
        slot, at = place(bus, jnp.maximum(line - 1, 0))
        found = [jnp.take_along_axis(x, at, axis=1) for x in spans]
        far = jnp.where(slot == 0, found[0], jnp.where(slot == 1, found[1], found[2]))
        return bus + jnp.where(line == 0, 0, far)

    def coef_at(bus, line, used):
        slot, at = place(bus, line)
        return jnp.where(used, slot * 128 + at + jnp.where(real, 0, 64), -1)[:1]

    bus0 = jnp.broadcast_to(aux_ref[0:1, :], shape).astype(I32)
    valid = path < 1 + LINKS + LINKS * LINKS
    two = (path >= 1 + LINKS) & valid
    line1 = jnp.where(two, 1 + (path - 1 - LINKS) // LINKS, jnp.where(valid, path, 0))
    line2 = jnp.where(two, 1 + (path - 1 - LINKS) % LINKS, 0)
    bus1 = hop(bus0, line1)
    bus2 = hop(bus1, line2)
    places = [coef_at(bus0, line1, valid & (path >= 1)), coef_at(bus1, line2, two), coef_at(bus2, 0, valid)]
    pick = jnp.where(iota((3 * 128, 3 * 128), 0) == jnp.concatenate(places, axis=1), 1.0, 0.0).astype(BF16)
    window = jnp.concatenate(
        [
            rows[pl.ds(COEF, H, stride=ROWS), :].astype(BF16),
            rows[pl.ds(PAIR, H, stride=ROWS), :].astype(BF16),
            lifts[2][LIFT + 16 :, :],
        ],
        axis=1,
    )
    found = jnp.dot(window, pick, preferred_element_type=F32)
    real, path = real[:1], path[:1]
    first = found[:, :128] + jnp.where(real & (path == 0), 1.0, 0.0)
    second = found[:, 128:256] + jnp.where(real & (path <= LINKS), 1.0, 0.0)
    weight = packed_product(packed_product(first, second, real), found[:, 256:], real)

    many = (128, 128)
    row = iota(many, 0)
    other = row % 64 % (3 * CONV)
    bus_of = jnp.zeros(many, I32)
    marks = [x[1:2] for x in notes]
    beside = jnp.where(is_even, 1, -1)
    for q, (at, column) in enumerate(((1, harm), (a_at, harm + beside), (b_at, harm - beside))):
        column = lax.rem(column + HALF, HALF)
        for c in range(CONV):
            bus = jnp.sum(jnp.where(iota((1, 128), 1) == c * HALF + column, marks[q], 0.0), axis=1, keepdims=True)
            bus = jnp.broadcast_to(bus.astype(I32), many) + at * SUB
            bus_of = jnp.where(other == q * CONV + c, bus, bus_of)
    wide = iota(many, 1)
    match = (row // 64 == wide // 64) & (row % 64 // (3 * CONV) == wide % 64 // 16) & (bus_of == bus2[:1])
    match = jnp.where(match, 1.0, 0.0).astype(BF16)
    high = weight.astype(BF16)
    rest = (weight - high.astype(F32)).astype(BF16)
    dims = (((1,), (1,)), ((), ()))
    table = lax.dot_general(high, match, dims, preferred_element_type=F32)
    table += lax.dot_general(rest, match, dims, preferred_element_type=F32)

    total = [[jnp.zeros((H, 128), F32) for _ in range(2)] for _ in range(CONV)]
    for q in range(3):
        for o in range(CONV):
            spec_r, spec_i = (lifts[q][(2 * o + p) * H : (2 * o + p + 1) * H, :].astype(F32) for p in range(2))
            for c in range(CONV):
                at = c * 3 * CONV + q * CONV + o
                add_r, add_i = product(table[:, at : at + 1], table[:, 64 + at : 65 + at], spec_r, spec_i)
                total[c][0] += add_r
                total[c][1] += add_i
    for c in range(CONV):
        for p in range(2):
            out[pl.ds(p * H * CONV + c, H, stride=CONV), :] = total[c][p]


VMEM = pl.BlockSpec(memory_space=pltpu.VMEM)
HBM = pl.BlockSpec(memory_space=pltpu.HBM)


def call(kernel, name, out_shape, in_specs, scratch=(), cost=(0, 0, 0), out_specs=None, aliases=None):
    flops, moved, hard = cost
    return pl.pallas_call(
        kernel,
        out_shape=out_shape,
        in_specs=in_specs,
        out_specs=out_specs or jax.tree.map(lambda _: VMEM, out_shape),
        input_output_aliases=aliases or {},
        scratch_shapes=list(scratch),
        compiler_params=pltpu.CompilerParams(vmem_limit_bytes=40 * 2**20),
        cost_estimate=pl.CostEstimate(flops=flops, bytes_accessed=moved, transcendentals=hard),
        name=name,
    )


def swaps(count):
    rounds = []
    for start in (0, 1):
        firsts = range(start, count - 1, 2)
        rounds.append([(i, i + 1) for i in firsts] + [(i + 1, i) for i in firsts])
    return rounds


def local(conv_volt, conv_power, conv_type, type_steep, conv_bus, admittance, link_offset):
    harm_count = lax.axis_size("harm")
    bus_count = lax.axis_size("bus")
    block = admittance.shape[3]
    snapshots = conv_volt.shape[3]
    tiles = block // TILE
    size = harm_count * ROWS
    kinds = 2 * H
    S = jax.ShapeDtypeStruct
    over_bus = swaps(bus_count)
    number = lambda r: r % harm_count * bus_count + r // harm_count
    over_ranges = [[(number(s), number(d)) for s, d in pairs] for pairs in swaps(harm_count * bus_count)]

    basis = make_basis()
    coef, edge_a, edge_b, aux, payload, lift = call(
        begin_kernel,
        "begin",
        (
            S((16, block), F32),
            S((16, 128), F32),
            S((16, 128), F32),
            S((8, 128), F32),
            S((size, 128), BF16),
            S((LIFT + 16, 128), BF16),
        ),
        [HBM] * 9,
        [
            pltpu.VMEM((2, 4, 1, block), F32),
            pltpu.VMEM((LINKS, block), I32),
            pltpu.SMEM((CONV,), I32),
            pltpu.SMEM(type_steep.shape, F32),
            pltpu.SMEM((CONV,), I32),
            pltpu.VMEM((CONV, snapshots), F32),
            pltpu.VMEM((kinds * CONV, snapshots), BF16),
            pltpu.VMEM((NT, kinds), BF16),
            pltpu.VMEM((kinds, NT), BF16),
            pltpu.VMEM((kinds * CONV, snapshots), F32),
            pltpu.VMEM((harm_count, 128), F32),
            pltpu.VMEM((harm_count, 128), F32),
            pltpu.VMEM((size, 128), F32),
            pltpu.SemaphoreType.DMA((9,)),
        ],
        (2 * 2 * 128 * 1024 * 512, 2**20, 2**19),
    )(
        *(
            pltpu.with_memory_space_constraint(array, pltpu.HBM)
            for array in (
                admittance,
                link_offset,
                conv_type,
                type_steep,
                conv_bus,
                conv_power,
                conv_volt.reshape(kinds * CONV, snapshots),
                jnp.asarray(np.ascontiguousarray(basis.T)),
                jnp.asarray(basis),
            )
        )
    )

    four = (harm_count, ROWS // 4, 4, snapshots)
    got = lax.all_to_all(payload.reshape(four), "harm", split_axis=0, concat_axis=0, tiled=True)

    beside_a = lax.ppermute(lift, ("harm", "bus"), over_ranges[0])
    q = call(
        sweeps_kernel,
        "sweeps",
        S((tiles, 2 * TILE, WIN), BF16),
        [VMEM],
        cost=(2 * tiles * 256 * 256 * 512, 2**20, 0),
    )(coef)
    got, q, beside_a = lax.optimization_barrier((got, q, beside_a))

    rows, beside_b, halo_a, halo_b = call(
        mix_kernel,
        "mix",
        (S((size, 128), F32), S((LIFT + 16 + H, 128), BF16), S((32, 128), F32), S((32, 128), F32)),
        [VMEM] * 4,
    )(got.reshape(size, snapshots), lift, edge_a, edge_b)
    beside_b = lax.ppermute(beside_b, ("harm", "bus"), over_ranges[1])
    halo_a = lax.ppermute(halo_a, "bus", over_bus[0])
    halo_b = lax.ppermute(halo_b, "bus", over_bus[1])
    out_volt = S((2, 1, block, snapshots), BF16)
    inject, bus_volt = call(
        inner_kernel,
        "inner",
        (S((block, 256), BF16), out_volt),
        [VMEM] * 2,
        [pltpu.VMEM((2, 1, block, snapshots), BF16), pltpu.SemaphoreType.DMA((tiles,))],
        (2 * tiles * 256 * 256 * 256, 2**20, 0),
        (VMEM, HBM),
    )(rows, q)
    beside_b, halo_a, halo_b, inject, bus_volt = lax.optimization_barrier((beside_b, halo_a, halo_b, inject, bus_volt))
    near, bus_volt = call(
        finish_kernel,
        "finish",
        (S((kinds * CONV, snapshots), BF16), out_volt),
        [VMEM] * 9 + [HBM],
        [
            pltpu.VMEM((kinds * CONV, snapshots), BF16),
            pltpu.VMEM((2, 2, EDGE, snapshots), BF16),
            pltpu.VMEM((kinds * CONV, 128), F32),
            pltpu.SemaphoreType.DMA((5,)),
        ],
        (2 * 10**7, 2**20, 0),
        (HBM, HBM),
        {9: 1},
    )(aux, rows, lift, beside_a, beside_b, halo_a, halo_b, inject, coef, bus_volt)
    return (bus_volt, near.reshape(2, H, CONV, snapshots))


def solution(mesh):
    in_specs = (
        P(None, None, ("bus", "harm"), None),
        P(("bus", "harm"), None),
        P(("bus", "harm")),
        P(),
        P(("bus", "harm")),
        P(None, None, "harm", "bus"),
        P(None, "bus"),
    )
    out_specs = (P(None, "harm", "bus", None), P(None, None, ("bus", "harm"), None))
    return jax.shard_map(local, mesh=mesh, in_specs=in_specs, out_specs=out_specs, check_vma=False)
```

```python
import math

import jax
import jax.numpy as jnp
import numpy as np
from jax import lax
from jax.experimental import pallas as pl
from jax.experimental.pallas import tpu as pltpu
from jax.sharding import PartitionSpec as P

H = 64
NT = 1024
REACH = 8
LINKS = 3
SUB = 16
CONV = 4
EDGE = 2 * REACH
TILE = 128
WIN = 256
ROWS = 12
COEF = 8
PAIR = 9
FAR = 10
MARK = 11
LIFT = 8 * H
HALF = 32
F32 = jnp.float32
BF16 = jnp.bfloat16
I32 = jnp.int32


def make_basis():
    turn = np.arange(1, H + 1)[:, None] * np.arange(NT)[None, :] % NT
    angle = turn * (2.0 * math.pi / NT)
    return np.concatenate([np.cos(angle), -np.sin(angle)], axis=0).astype(BF16)


def iota(shape, dim):
    return lax.broadcasted_iota(I32, shape, dim)


def product(ar, ai, br, bi):
    return ar * br - ai * bi, ar * bi + ai * br


def grouped(x):
    k, j = iota((8, 128), 0), iota((8, 128), 1) // SUB
    for s in (1, 2, 4):
        later = pltpu.roll(pltpu.roll(x, s, 0), 128 - SUB * s, 1)
        sooner = pltpu.roll(pltpu.roll(x, 8 - s, 0), SUB * s, 1)
        bk, bj = (k // s) % 2, (j // s) % 2
        x = jnp.where(bk == bj, x, jnp.where(bk == 1, later, sooner))
    return x


def even(axis):
    return lax.rem(lax.axis_index(axis), 2) == 0


def begin_kernel(
    adm_hbm, off_hbm, type_hbm, steep_hbm, bus_hbm, power_hbm, volt_hbm, turned_hbm, basis_hbm,
    coef_ref, a_ref, b_ref, aux_ref, out_ref, lift_ref,
    adm, off, kind, steep, bus, power, volt_in, turned, basis, volts, groups, spans, rows, sems,
):
    pairs = [
        (adm_hbm, adm), (off_hbm, off), (type_hbm, kind), (steep_hbm, steep), (bus_hbm, bus), (power_hbm, power),
        (volt_hbm, volt_in), (turned_hbm, turned), (basis_hbm, basis),
    ]
    copies = [pltpu.make_async_copy(src, dst, sems.at[i]) for i, (src, dst) in enumerate(pairs)]
    for copy in copies:
        copy.start()
    for copy in copies:
        copy.wait()
    inv_r, inv_i = adm[0, 0], adm[1, 0]
    steps = [product(inv_r, inv_i, adm[0, k], adm[1, k]) for k in range(1, 1 + LINKS)]
    blank = jnp.zeros((5, inv_r.shape[1]), F32)
    coefs = jnp.concatenate(
        [inv_r] + [s[0] for s in steps] + [inv_i] + [s[1] for s in steps] + [off[...].astype(F32), blank], axis=0
    )
    coef_ref[...] = coefs
    tiles = coefs.shape[1] // 128
    for v in range(tiles):
        groups[v * 8 : v * 8 + 8, :] = grouped(coefs[:8, v * 128 : v * 128 + 128])
        spans[v * 8 : v * 8 + 8, :] = grouped(coefs[8:, v * 128 : v * 128 + 128])
    first, last = coefs[:, :128], coefs[:, tiles * 128 - 128 :]
    is_even = even("bus")
    a_ref[...] = jnp.where(is_even, last, first)
    b_ref[...] = jnp.where(is_even, first, last)
    harm = lax.axis_index("harm")
    span = spans[pl.ds(harm, 1), :]
    aux_ref[1:2, :] = span
    aux_ref[2:3, :] = spans[pl.ds(harm + jnp.where(even("harm"), 1, -1), 1), :]
    group = groups[...]
    after, before = pltpu.roll(group, H - 1, 0), pltpu.roll(group, 1, 0)
    first_core = iota((H, 128), 0) % 2 == 0
    pair, far = jnp.where(first_core, after, before), jnp.where(first_core, before, after)
    rows[pl.ds(COEF, H, stride=ROWS), :] = group
    rows[pl.ds(PAIR, H, stride=ROWS), :] = pair
    rows[pl.ds(FAR, H, stride=ROWS), :] = far

    lane = iota((1, 128), 1)
    column = lax.rem(harm, HALF)
    mark = jnp.zeros((1, 128), F32)
    start = jnp.full((1, 128), SUB, F32)
    for c in range(CONV):
        number = lax.rem(bus[c], SUB).astype(F32)
        mark += jnp.where(lane == c * HALF + column, number, 0.0)
        start += jnp.where(lane % 64 // 16 == c, number, 0.0)
    aux_ref[0:1, :] = start
    rows[pl.ds(MARK, H, stride=ROWS), :] = jnp.broadcast_to(mark, (H, 128))

    volts[...] = volt_in[...].astype(F32)
    kinds = 2 * H
    volt = jnp.concatenate(
        [volts[pl.ds(c, kinds, stride=CONV), :] for c in range(CONV)], axis=1
    ).astype(BF16)
    sharp = jnp.concatenate([jnp.full((1, 128), steep[kind[c]], F32) for c in range(CONV)], axis=1)
    strong = jnp.concatenate([power[c : c + 1, :] for c in range(CONV)], axis=1)
    spectra = jnp.zeros((kinds, CONV * 128), F32)
    step = 256
    for n in range(0, NT, step):
        wave = jnp.dot(turned[n : n + step, :], volt, preferred_element_type=F32)
        current = (strong * jnp.tanh(sharp * wave)).astype(BF16)
        spectra += jnp.dot(basis[:, n : n + step], current, preferred_element_type=F32)
    spectra = spectra * NT ** (-0.5)
    for c in range(CONV):
        for p in range(2):
            piece = spectra[p * H : p * H + H, c * 128 : c * 128 + 128]
            at = (2 * c + p) * H
            rows[pl.ds(2 * c + p, H, stride=ROWS), :] = piece
            lift_ref[at : at + H, :] = piece.astype(BF16)
    row = iota((16, 128), 0)
    notes = jnp.where(row == 0, span, jnp.where(row == 1, mark, 0.0))
    lift_ref[LIFT:, :] = notes.astype(BF16)
    out_ref[...] = rows[...].astype(BF16)


def sweeps_matrix(coefs, first, count):
    width = coefs.shape[1]
    rows = iota((width, width), 0)
    lanes = iota((1, width), 1)
    turned_r = jnp.zeros((width, width), F32)
    turned_i = jnp.zeros((width, width), F32)
    for k in range(LINKS):
        here = rows == lanes + coefs[8 + k : 9 + k].astype(I32)
        turned_r += jnp.where(here, coefs[1 + k : 2 + k], 0.0)
        turned_i += jnp.where(here, coefs[5 + k : 6 + k], 0.0)
    step_r, step_i = turned_r.T, turned_i.T
    mid_r, mid_i = step_r[first : first + count], step_i[first : first + count]
    twice = jnp.dot(
        jnp.concatenate([mid_r, mid_i], axis=0).astype(BF16),
        jnp.concatenate([step_r, step_i], axis=1).astype(BF16),
        preferred_element_type=F32,
    )
    same = iota((count, width), 0) + first == iota((count, width), 1)
    all_r = twice[:count, :width] - twice[count:, width:] + mid_r + jnp.where(same, 1.0, 0.0)
    all_i = twice[:count, width:] + twice[count:, :width] + mid_i
    q_r, q_i = product(all_r, all_i, coefs[0:1], coefs[4:5])
    return jnp.concatenate([q_r, q_i], axis=0).astype(BF16)


def volt_of(matrix, inject):
    count = matrix.shape[0] // 2
    acc = jnp.dot(matrix, inject, preferred_element_type=F32)
    return (acc[:count, :128] - acc[count:, 128:]).astype(BF16), (acc[:count, 128:] + acc[count:, :128]).astype(BF16)


def sweeps_kernel(coef_ref, q_ref):
    blank = jnp.zeros((coef_ref.shape[0], TILE), F32)
    tiles = q_ref.shape[0]
    for b in range(tiles):
        around = [coef_ref[:, t * TILE : t * TILE + TILE] if 0 <= t < tiles else blank for t in (b - 1, b, b + 1)]
        coefs = pltpu.roll(jnp.concatenate(around, axis=1), 2 * TILE + EDGE, 1)[:, :WIN]
        q_ref[b] = sweeps_matrix(coefs, EDGE, TILE)


def mix_kernel(got_ref, a_ref, b_ref, rows_ref, out_a_ref, out_b_ref):
    size = got_ref.shape[0]
    rows_ref[...] = got_ref[...].astype(F32)
    first, last = rows_ref[:16, :], pltpu.roll(rows_ref[size - 16 :, :], ROWS, 0)
    far = rows_ref[pl.ds(FAR, H, stride=ROWS), :]
    is_even = even("bus")
    for ref, edge, range_rows in (
        (out_a_ref, a_ref, jnp.where(is_even, last, first)),
        (out_b_ref, b_ref, jnp.where(is_even, first, last)),
    ):
        ref[:16, :] = range_rows
        ref[16:32, :] = edge[...]
        ref[32:, :] = far


def inner_kernel(rows, q_ref, inject, volt_hbm, volt, sems):
    def part(p):
        return jnp.concatenate(
            [
                rows[pl.ds(h * HALF * ROWS + 2 * c + p, HALF, stride=ROWS), :]
                for h in range(2)
                for c in range(CONV)
            ],
            axis=0,
        )

    spectra = jnp.concatenate([part(0), part(1)], axis=1).astype(BF16)
    convs = H * CONV
    at = [
        jnp.sum(rows[pl.ds(h * HALF * ROWS + MARK, HALF, stride=ROWS), :], axis=0, keepdims=True)
        for h in range(2)
    ]
    at = jnp.concatenate(at, axis=1).astype(I32)
    lane = iota((1, convs), 1)
    source = lane // (CONV * HALF) * HALF + lane % HALF
    target = source * SUB + at
    buses = H * SUB
    owner = jnp.where(iota((buses, convs), 0) == target, 1.0, 0.0).astype(BF16)
    inject[...] = jnp.dot(owner, spectra, preferred_element_type=F32).astype(BF16)
    tiles = q_ref.shape[0]
    copies = []
    for b in range(tiles):
        first = max(b * TILE - EDGE, 0)
        last = min(b * TILE - EDGE + WIN, buses)
        pieces = [jnp.zeros((n, 256), BF16) for n in (first - b * TILE + EDGE, b * TILE - EDGE + WIN - last)]
        pieces.insert(1, inject[first:last, :])
        window = jnp.concatenate([x for x in pieces if x.shape[0]], axis=0)
        volt[0, 0, b * TILE : b * TILE + TILE, :], volt[1, 0, b * TILE : b * TILE + TILE, :] = volt_of(
            q_ref[b], window
        )
        if b % 2:
            place = pl.ds(b * TILE - TILE, 2 * TILE)
            for p in range(2):
                copies.append(
                    pltpu.make_async_copy(volt.at[p, 0, place], volt_hbm.at[p, 0, place], sems.at[b - 1 + p])
                )
                copies[-1].start()
    for copy in copies:
        copy.wait()


def edges(low, high, inject_ref, coef_ref, volt):
    buses = inject_ref.shape[0]

    def injected(edge, lane0):
        total_r = jnp.zeros((SUB, 128), F32)
        total_i = jnp.zeros((SUB, 128), F32)
        for c in range(CONV):
            at = c * HALF + lane0
            bus = jnp.broadcast_to(edge[MARK : MARK + 1, at : at + 1], (SUB, 128)).astype(I32)
            here = iota((SUB, 128), 0) == bus
            total_r += jnp.where(here, edge[2 * c : 2 * c + 1, :], 0.0)
            total_i += jnp.where(here, edge[2 * c + 1 : 2 * c + 2, :], 0.0)
        return jnp.concatenate([total_r, total_i], axis=1).astype(BF16)

    coefs = jnp.concatenate([low[16:32], coef_ref[:, :128]], axis=1)
    coefs = pltpu.roll(coefs, 128 + EDGE, 1)[:, :128]
    window = jnp.concatenate([injected(low, HALF - 1), inject_ref[: 128 - EDGE, :]], axis=0)
    volt[0, 0], volt[0, 1] = volt_of(sweeps_matrix(coefs, EDGE, EDGE), window)
    coefs = jnp.concatenate([coef_ref[:, buses - 128 :], high[16:32]], axis=1)
    coefs = pltpu.roll(coefs, 256 - EDGE, 1)[:, :128]
    window = jnp.concatenate([inject_ref[buses - 128 + EDGE :, :], injected(high, 0)], axis=0)
    volt[1, 0], volt[1, 1] = volt_of(sweeps_matrix(coefs, 128 - 2 * EDGE, EDGE), window)


def swapped(x):
    return pltpu.roll(x, 64, 1)


def packed_product(a, b, real):
    turned = swapped(b)
    return a * jnp.where(real, b, turned) + swapped(a) * jnp.where(real, -turned, b)


def finish_kernel(
    aux_ref, rows, mine_ref, beside_a_ref, beside_b_ref, halo_a_ref, halo_b_ref, inject_ref, coef_ref, done_hbm,
    near_hbm, volt_hbm, near, volt, out, sems,
):
    del done_hbm
    is_even = even("bus")
    low = jnp.where(is_even, halo_b_ref[...], halo_a_ref[...])
    high = jnp.where(is_even, halo_a_ref[...], halo_b_ref[...])
    edges(low, high, inject_ref, coef_ref, volt)
    harm = lax.axis_index("harm")
    far = rows[pl.ds(FAR, H, stride=ROWS), :]
    far = jnp.where(harm == 0, low[32:], jnp.where(harm == H - 1, high[32:], far))
    near_converters(aux_ref, rows, far, (mine_ref, beside_a_ref, beside_b_ref), out)
    near[...] = out[...].astype(BF16)
    copies = [pltpu.make_async_copy(near, near_hbm, sems.at[4])]
    for e in range(2):
        for p in range(2):
            place = volt_hbm.at[p, 0, pl.ds(e * (inject_ref.shape[0] - EDGE), EDGE)]
            copies.append(pltpu.make_async_copy(volt.at[e, p], place, sems.at[2 * e + p]))
    for copy in copies:
        copy.start()
    for copy in copies:
        copy.wait()


def near_converters(aux_ref, rows, far, lifts, out):
    harm = lax.axis_index("harm")
    is_even = even("harm")
    a_at = jnp.where(is_even, 2, 0)
    b_at = 2 - a_at

    shape = (8, 128)
    lane = iota(shape, 1)
    real = lane < 64
    path = lane % 16
    notes = [ref[LIFT : LIFT + 16, :].astype(F32) for ref in lifts]
    spans = [aux_ref[1:2, :], aux_ref[2:3, :], notes[2][:1]]
    spans = [jnp.broadcast_to(x, shape).astype(I32) for x in spans]

    def place(bus, line):
        at = bus // SUB
        slot = jnp.where(at == 1, 0, jnp.where(at == a_at, 1, 2))
        return slot, line * SUB + bus % SUB

    def hop(bus, line):
        slot, at = place(bus, jnp.maximum(line - 1, 0))
        found = [jnp.take_along_axis(x, at, axis=1) for x in spans]
        far = jnp.where(slot == 0, found[0], jnp.where(slot == 1, found[1], found[2]))
        return bus + jnp.where(line == 0, 0, far)

    def coef_at(bus, line, used):
        slot, at = place(bus, line)
        return jnp.where(used, slot * 128 + at + jnp.where(real, 0, 64), -1)[:1]

    bus0 = jnp.broadcast_to(aux_ref[0:1, :], shape).astype(I32)
    valid = path < 1 + LINKS + LINKS * LINKS
    two = (path >= 1 + LINKS) & valid
    line1 = jnp.where(two, 1 + (path - 1 - LINKS) // LINKS, jnp.where(valid, path, 0))
    line2 = jnp.where(two, 1 + (path - 1 - LINKS) % LINKS, 0)
    bus1 = hop(bus0, line1)
    bus2 = hop(bus1, line2)
    places = [coef_at(bus0, line1, valid & (path >= 1)), coef_at(bus1, line2, two), coef_at(bus2, 0, valid)]
    pick = jnp.where(iota((3 * 128, 3 * 128), 0) == jnp.concatenate(places, axis=1), 1.0, 0.0).astype(BF16)
    window = jnp.concatenate(
        [
            rows[pl.ds(COEF, H, stride=ROWS), :].astype(BF16),
            rows[pl.ds(PAIR, H, stride=ROWS), :].astype(BF16),
            far.astype(BF16),
        ],
        axis=1,
    )
    found = jnp.dot(window, pick, preferred_element_type=F32)
    real, path = real[:1], path[:1]
    first = found[:, :128] + jnp.where(real & (path == 0), 1.0, 0.0)
    second = found[:, 128:256] + jnp.where(real & (path <= LINKS), 1.0, 0.0)
    weight = packed_product(packed_product(first, second, real), found[:, 256:], real)

    many = (128, 128)
    row = iota(many, 0)
    other = row % 64 % (3 * CONV)
    bus_of = jnp.zeros(many, I32)
    marks = [x[1:2] for x in notes]
    beside = jnp.where(is_even, 1, -1)
    for q, (at, column) in enumerate(((1, harm), (a_at, harm + beside), (b_at, harm - beside))):
        column = lax.rem(column + HALF, HALF)
        for c in range(CONV):
            bus = jnp.sum(jnp.where(iota((1, 128), 1) == c * HALF + column, marks[q], 0.0), axis=1, keepdims=True)
            bus = jnp.broadcast_to(bus.astype(I32), many) + at * SUB
            bus_of = jnp.where(other == q * CONV + c, bus, bus_of)
    wide = iota(many, 1)
    match = (row // 64 == wide // 64) & (row % 64 // (3 * CONV) == wide % 64 // 16) & (bus_of == bus2[:1])
    match = jnp.where(match, 1.0, 0.0).astype(BF16)
    high = weight.astype(BF16)
    rest = (weight - high.astype(F32)).astype(BF16)
    dims = (((1,), (1,)), ((), ()))
    table = lax.dot_general(high, match, dims, preferred_element_type=F32)
    table += lax.dot_general(rest, match, dims, preferred_element_type=F32)

    step = 16
    for h in range(0, H, step):
        total = [[jnp.zeros((step, 128), F32) for _ in range(2)] for _ in range(CONV)]
        for q in range(3):
            for o in range(CONV):
                at = 2 * o * H + h
                spec_r, spec_i = (lifts[q][at + p * H : at + p * H + step, :].astype(F32) for p in range(2))
                for c in range(CONV):
                    at = c * 3 * CONV + q * CONV + o
                    weights = (table[h : h + step, n : n + 1] for n in (at, 64 + at))
                    add_r, add_i = product(*weights, spec_r, spec_i)
                    total[c][0] += add_r
                    total[c][1] += add_i
        for c in range(CONV):
            for p in range(2):
                out[pl.ds((p * H + h) * CONV + c, step, stride=CONV), :] = total[c][p]


VMEM = pl.BlockSpec(memory_space=pltpu.VMEM)
HBM = pl.BlockSpec(memory_space=pltpu.HBM)


def call(kernel, name, out_shape, in_specs, scratch=(), cost=(0, 0, 0), out_specs=None, aliases=None):
    flops, moved, hard = cost
    return pl.pallas_call(
        kernel,
        out_shape=out_shape,
        in_specs=in_specs,
        out_specs=out_specs or jax.tree.map(lambda _: VMEM, out_shape),
        input_output_aliases=aliases or {},
        scratch_shapes=list(scratch),
        compiler_params=pltpu.CompilerParams(vmem_limit_bytes=40 * 2**20),
        cost_estimate=pl.CostEstimate(flops=flops, bytes_accessed=moved, transcendentals=hard),
        name=name,
    )


def swaps(count):
    rounds = []
    for start in (0, 1):
        firsts = range(start, count - 1, 2)
        rounds.append([(i, i + 1) for i in firsts] + [(i + 1, i) for i in firsts])
    return rounds


def local(conv_volt, conv_power, conv_type, type_steep, conv_bus, admittance, link_offset):
    harm_count = lax.axis_size("harm")
    bus_count = lax.axis_size("bus")
    block = admittance.shape[3]
    snapshots = conv_volt.shape[3]
    tiles = block // TILE
    size = harm_count * ROWS
    kinds = 2 * H
    S = jax.ShapeDtypeStruct
    over_bus = swaps(bus_count)
    number = lambda r: r % harm_count * bus_count + r // harm_count
    over_ranges = [[(number(s), number(d)) for s, d in pairs] for pairs in swaps(harm_count * bus_count)]

    basis = make_basis()
    coef, edge_a, edge_b, aux, payload, lift = call(
        begin_kernel,
        "begin",
        (
            S((16, block), F32),
            S((16, 128), F32),
            S((16, 128), F32),
            S((8, 128), F32),
            S((size, 128), BF16),
            S((LIFT + 16, 128), BF16),
        ),
        [HBM] * 9,
        [
            pltpu.VMEM((2, 4, 1, block), F32),
            pltpu.VMEM((LINKS, block), I32),
            pltpu.SMEM((CONV,), I32),
            pltpu.SMEM(type_steep.shape, F32),
            pltpu.SMEM((CONV,), I32),
            pltpu.VMEM((CONV, snapshots), F32),
            pltpu.VMEM((kinds * CONV, snapshots), BF16),
            pltpu.VMEM((NT, kinds), BF16),
            pltpu.VMEM((kinds, NT), BF16),
            pltpu.VMEM((kinds * CONV, snapshots), F32),
            pltpu.VMEM((harm_count, 128), F32),
            pltpu.VMEM((harm_count, 128), F32),
            pltpu.VMEM((size, 128), F32),
            pltpu.SemaphoreType.DMA((9,)),
        ],
        (2 * 2 * 128 * 1024 * 512, 2**20, 2**19),
    )(
        *(
            pltpu.with_memory_space_constraint(array, pltpu.HBM)
            for array in (
                admittance,
                link_offset,
                conv_type,
                type_steep,
                conv_bus,
                conv_power,
                conv_volt.reshape(kinds * CONV, snapshots),
                jnp.asarray(np.ascontiguousarray(basis.T)),
                jnp.asarray(basis),
            )
        )
    )

    four = (harm_count, ROWS // 4, 4, snapshots)
    got = lax.all_to_all(payload.reshape(four), "harm", split_axis=0, concat_axis=0, tiled=True)

    beside_a = lax.ppermute(lift, ("harm", "bus"), over_ranges[0])
    q = call(
        sweeps_kernel,
        "sweeps",
        S((tiles, 2 * TILE, WIN), BF16),
        [VMEM],
        cost=(2 * tiles * 256 * 256 * 512, 2**20, 0),
    )(coef)
    lift_b, q = lax.optimization_barrier((lift, q))
    beside_b = lax.ppermute(lift_b, ("harm", "bus"), over_ranges[1])
    got, q, beside_a = lax.optimization_barrier((got, q, beside_a))

    halo = S((32 + harm_count, 128), F32)
    rows, halo_a, halo_b = call(
        mix_kernel,
        "mix",
        (S((size, 128), F32), halo, halo),
        [VMEM] * 3,
    )(got.reshape(size, snapshots), edge_a, edge_b)
    halo_a = lax.ppermute(halo_a, "bus", over_bus[0])
    halo_b = lax.ppermute(halo_b, "bus", over_bus[1])
    out_volt = S((2, 1, block, snapshots), BF16)
    inject, bus_volt = call(
        inner_kernel,
        "inner",
        (S((block, 256), BF16), out_volt),
        [VMEM] * 2,
        [pltpu.VMEM((2, 1, block, snapshots), BF16), pltpu.SemaphoreType.DMA((tiles,))],
        (2 * tiles * 256 * 256 * 256, 2**20, 0),
        (VMEM, HBM),
    )(rows, q)
    beside_b, halo_a, halo_b, inject, bus_volt = lax.optimization_barrier((beside_b, halo_a, halo_b, inject, bus_volt))
    near, bus_volt = call(
        finish_kernel,
        "finish",
        (S((kinds * CONV, snapshots), BF16), out_volt),
        [VMEM] * 9 + [HBM],
        [
            pltpu.VMEM((kinds * CONV, snapshots), BF16),
            pltpu.VMEM((2, 2, EDGE, snapshots), BF16),
            pltpu.VMEM((kinds * CONV, 128), F32),
            pltpu.SemaphoreType.DMA((5,)),
        ],
        (2 * 10**7, 2**20, 0),
        (HBM, HBM),
        {9: 1},
    )(aux, rows, lift, beside_a, beside_b, halo_a, halo_b, inject, coef, bus_volt)
    return (bus_volt, near.reshape(2, H, CONV, snapshots))


def solution(mesh):
    in_specs = (
        P(None, None, ("bus", "harm"), None),
        P(("bus", "harm"), None),
        P(("bus", "harm")),
        P(),
        P(("bus", "harm")),
        P(None, None, "harm", "bus"),
        P(None, "bus"),
    )
    out_specs = (P(None, "harm", "bus", None), P(None, None, ("bus", "harm"), None))
    return jax.shard_map(local, mesh=mesh, in_specs=in_specs, out_specs=out_specs, check_vma=False)
```

```python
import math

import jax
import jax.numpy as jnp
import numpy as np
from jax import lax
from jax.experimental import pallas as pl
from jax.experimental.pallas import tpu as pltpu
from jax.sharding import PartitionSpec as P

H = 64
NT = 1024
REACH = 8
LINKS = 3
SUB = 16
CONV = 4
EDGE = 2 * REACH
TILE = 128
WIN = 256
ROWS = 12
COEF = 8
PAIR = 9
FAR = 10
MARK = 11
LIFT = 8 * H
HALF = 32
F32 = jnp.float32
BF16 = jnp.bfloat16
I32 = jnp.int32


def make_basis():
    turn = np.arange(1, H + 1)[:, None] * np.arange(NT)[None, :] % NT
    angle = turn * (2.0 * math.pi / NT)
    return np.concatenate([np.cos(angle), -np.sin(angle)], axis=0).astype(BF16)


def iota(shape, dim):
    return lax.broadcasted_iota(I32, shape, dim)


def product(ar, ai, br, bi):
    return ar * br - ai * bi, ar * bi + ai * br


def grouped(x):
    k, j = iota((8, 128), 0), iota((8, 128), 1) // SUB
    for s in (1, 2, 4):
        later = pltpu.roll(pltpu.roll(x, s, 0), 128 - SUB * s, 1)
        sooner = pltpu.roll(pltpu.roll(x, 8 - s, 0), SUB * s, 1)
        bk, bj = (k // s) % 2, (j // s) % 2
        x = jnp.where(bk == bj, x, jnp.where(bk == 1, later, sooner))
    return x


def even(axis):
    return lax.rem(lax.axis_index(axis), 2) == 0


def begin_kernel(
    adm_hbm, off_hbm, type_hbm, steep_hbm, bus_hbm, power_hbm, volt_hbm, turned_hbm, basis_hbm,
    coef_ref, a_ref, b_ref, aux_ref, out_ref, lift_ref,
    adm, off, kind, steep, bus, power, volt_in, turned, basis, volts, groups, spans, rows, sems,
):
    pairs = [
        (adm_hbm, adm), (off_hbm, off), (type_hbm, kind), (steep_hbm, steep), (bus_hbm, bus), (power_hbm, power),
        (volt_hbm, volt_in), (turned_hbm, turned), (basis_hbm, basis),
    ]
    copies = [pltpu.make_async_copy(src, dst, sems.at[i]) for i, (src, dst) in enumerate(pairs)]
    for copy in copies:
        copy.start()
    for copy in copies:
        copy.wait()
    inv_r, inv_i = adm[0, 0], adm[1, 0]
    steps = [product(inv_r, inv_i, adm[0, k], adm[1, k]) for k in range(1, 1 + LINKS)]
    blank = jnp.zeros((5, inv_r.shape[1]), F32)
    coefs = jnp.concatenate(
        [inv_r] + [s[0] for s in steps] + [inv_i] + [s[1] for s in steps] + [off[...].astype(F32), blank], axis=0
    )
    coef_ref[...] = coefs
    tiles = coefs.shape[1] // 128
    for v in range(tiles):
        groups[v * 8 : v * 8 + 8, :] = grouped(coefs[:8, v * 128 : v * 128 + 128])
        spans[v * 8 : v * 8 + 8, :] = grouped(coefs[8:, v * 128 : v * 128 + 128])
    first, last = coefs[:, :128], coefs[:, tiles * 128 - 128 :]
    is_odd = ~even("bus")
    a_ref[...] = jnp.where(is_odd, last, first)
    b_ref[...] = jnp.where(is_odd, first, last)
    harm = lax.axis_index("harm")
    span = spans[pl.ds(harm, 1), :]
    aux_ref[1:2, :] = span
    aux_ref[2:3, :] = spans[pl.ds(harm + jnp.where(even("harm"), 1, -1), 1), :]
    group = groups[...]
    after, before = pltpu.roll(group, H - 1, 0), pltpu.roll(group, 1, 0)
    first_core = iota((H, 128), 0) % 2 == 0
    pair, far = jnp.where(first_core, after, before), jnp.where(first_core, before, after)
    rows[pl.ds(COEF, H, stride=ROWS), :] = group
    rows[pl.ds(PAIR, H, stride=ROWS), :] = pair
    rows[pl.ds(FAR, H, stride=ROWS), :] = far

    lane = iota((1, 128), 1)
    column = lax.rem(harm, HALF)
    mark = jnp.zeros((1, 128), F32)
    start = jnp.full((1, 128), SUB, F32)
    for c in range(CONV):
        number = lax.rem(bus[c], SUB).astype(F32)
        mark += jnp.where(lane == c * HALF + column, number, 0.0)
        start += jnp.where(lane % 64 // 16 == c, number, 0.0)
    aux_ref[0:1, :] = start
    rows[pl.ds(MARK, H, stride=ROWS), :] = jnp.broadcast_to(mark, (H, 128))

    volts[...] = volt_in[...].astype(F32)
    kinds = 2 * H
    volt = jnp.concatenate(
        [volts[pl.ds(c, kinds, stride=CONV), :] for c in range(CONV)], axis=1
    ).astype(BF16)
    sharp = jnp.concatenate([jnp.full((1, 128), steep[kind[c]], F32) for c in range(CONV)], axis=1)
    strong = jnp.concatenate([power[c : c + 1, :] for c in range(CONV)], axis=1)
    spectra = jnp.zeros((kinds, CONV * 128), F32)
    step = 256
    for n in range(0, NT, step):
        wave = jnp.dot(turned[n : n + step, :], volt, preferred_element_type=F32)
        current = (strong * jnp.tanh(sharp * wave)).astype(BF16)
        spectra += jnp.dot(basis[:, n : n + step], current, preferred_element_type=F32)
    spectra = spectra * NT ** (-0.5)
    for c in range(CONV):
        for p in range(2):
            piece = spectra[p * H : p * H + H, c * 128 : c * 128 + 128]
            at = (2 * c + p) * H
            rows[pl.ds(2 * c + p, H, stride=ROWS), :] = piece
            lift_ref[at : at + H, :] = piece.astype(BF16)
    row = iota((16, 128), 0)
    notes = jnp.where(row == 0, span, jnp.where(row == 1, mark, 0.0))
    lift_ref[LIFT:, :] = notes.astype(BF16)
    out_ref[...] = rows[...].astype(BF16)


def sweeps_matrix(coefs, first, count):
    width = coefs.shape[1]
    rows = iota((width, width), 0)
    lanes = iota((1, width), 1)
    turned_r = jnp.zeros((width, width), F32)
    turned_i = jnp.zeros((width, width), F32)
    for k in range(LINKS):
        here = rows == lanes + coefs[8 + k : 9 + k].astype(I32)
        turned_r += jnp.where(here, coefs[1 + k : 2 + k], 0.0)
        turned_i += jnp.where(here, coefs[5 + k : 6 + k], 0.0)
    step_r, step_i = turned_r.T, turned_i.T
    mid_r, mid_i = step_r[first : first + count], step_i[first : first + count]
    twice = jnp.dot(
        jnp.concatenate([mid_r, mid_i], axis=0).astype(BF16),
        jnp.concatenate([step_r, step_i], axis=1).astype(BF16),
        preferred_element_type=F32,
    )
    same = iota((count, width), 0) + first == iota((count, width), 1)
    all_r = twice[:count, :width] - twice[count:, width:] + mid_r + jnp.where(same, 1.0, 0.0)
    all_i = twice[:count, width:] + twice[count:, :width] + mid_i
    q_r, q_i = product(all_r, all_i, coefs[0:1], coefs[4:5])
    return jnp.concatenate([q_r, q_i], axis=0).astype(BF16)


def volt_of(matrix, inject):
    count = matrix.shape[0] // 2
    acc = jnp.dot(matrix, inject, preferred_element_type=F32)
    return (acc[:count, :128] - acc[count:, 128:]).astype(BF16), (acc[:count, 128:] + acc[count:, :128]).astype(BF16)


def sweeps_kernel(coef_ref, q_ref):
    blank = jnp.zeros((coef_ref.shape[0], TILE), F32)
    tiles = q_ref.shape[0]
    for b in range(tiles):
        around = [coef_ref[:, t * TILE : t * TILE + TILE] if 0 <= t < tiles else blank for t in (b - 1, b, b + 1)]
        coefs = pltpu.roll(jnp.concatenate(around, axis=1), 2 * TILE + EDGE, 1)[:, :WIN]
        q_ref[b] = sweeps_matrix(coefs, EDGE, TILE)


def mix_kernel(got_ref, a_ref, b_ref, rows_ref, out_a_ref, out_b_ref):
    size = got_ref.shape[0]
    rows_ref[...] = got_ref[...].astype(F32)
    first, last = rows_ref[:16, :], pltpu.roll(rows_ref[size - 16 :, :], ROWS, 0)
    far = rows_ref[pl.ds(FAR, H, stride=ROWS), :]
    is_odd = ~even("bus")
    for ref, edge, range_rows in (
        (out_a_ref, a_ref, jnp.where(is_odd, last, first)),
        (out_b_ref, b_ref, jnp.where(is_odd, first, last)),
    ):
        ref[:16, :] = range_rows
        ref[16:32, :] = edge[...]
        ref[32:, :] = far


def inner_kernel(rows, q_ref, inject, volt_hbm, volt, sems):
    def part(p):
        return jnp.concatenate(
            [
                rows[pl.ds(h * HALF * ROWS + 2 * c + p, HALF, stride=ROWS), :]
                for h in range(2)
                for c in range(CONV)
            ],
            axis=0,
        )

    spectra = jnp.concatenate([part(0), part(1)], axis=1).astype(BF16)
    convs = H * CONV
    at = [
        jnp.sum(rows[pl.ds(h * HALF * ROWS + MARK, HALF, stride=ROWS), :], axis=0, keepdims=True)
        for h in range(2)
    ]
    at = jnp.concatenate(at, axis=1).astype(I32)
    lane = iota((1, convs), 1)
    source = lane // (CONV * HALF) * HALF + lane % HALF
    target = source * SUB + at
    buses = H * SUB
    owner = jnp.where(iota((buses, convs), 0) == target, 1.0, 0.0).astype(BF16)
    inject[...] = jnp.dot(owner, spectra, preferred_element_type=F32).astype(BF16)
    tiles = q_ref.shape[0]
    copies = []
    for b in range(tiles):
        first = max(b * TILE - EDGE, 0)
        last = min(b * TILE - EDGE + WIN, buses)
        pieces = [jnp.zeros((n, 256), BF16) for n in (first - b * TILE + EDGE, b * TILE - EDGE + WIN - last)]
        pieces.insert(1, inject[first:last, :])
        window = jnp.concatenate([x for x in pieces if x.shape[0]], axis=0)
        volt[0, 0, b * TILE : b * TILE + TILE, :], volt[1, 0, b * TILE : b * TILE + TILE, :] = volt_of(
            q_ref[b], window
        )
        if b % 2:
            place = pl.ds(b * TILE - TILE, 2 * TILE)
            for p in range(2):
                copies.append(
                    pltpu.make_async_copy(volt.at[p, 0, place], volt_hbm.at[p, 0, place], sems.at[b - 1 + p])
                )
                copies[-1].start()
    for copy in copies:
        copy.wait()


def edges(low, high, inject_ref, coef_ref, volt):
    buses = inject_ref.shape[0]

    def injected(edge, lane0):
        total_r = jnp.zeros((SUB, 128), F32)
        total_i = jnp.zeros((SUB, 128), F32)
        for c in range(CONV):
            at = c * HALF + lane0
            bus = jnp.broadcast_to(edge[MARK : MARK + 1, at : at + 1], (SUB, 128)).astype(I32)
            here = iota((SUB, 128), 0) == bus
            total_r += jnp.where(here, edge[2 * c : 2 * c + 1, :], 0.0)
            total_i += jnp.where(here, edge[2 * c + 1 : 2 * c + 2, :], 0.0)
        return jnp.concatenate([total_r, total_i], axis=1).astype(BF16)

    coefs = jnp.concatenate([low[16:32], coef_ref[:, :128]], axis=1)
    coefs = pltpu.roll(coefs, 128 + EDGE, 1)[:, :128]
    window = jnp.concatenate([injected(low, HALF - 1), inject_ref[: 128 - EDGE, :]], axis=0)
    volt[0, 0], volt[0, 1] = volt_of(sweeps_matrix(coefs, EDGE, EDGE), window)
    coefs = jnp.concatenate([coef_ref[:, buses - 128 :], high[16:32]], axis=1)
    coefs = pltpu.roll(coefs, 256 - EDGE, 1)[:, :128]
    window = jnp.concatenate([inject_ref[buses - 128 + EDGE :, :], injected(high, 0)], axis=0)
    volt[1, 0], volt[1, 1] = volt_of(sweeps_matrix(coefs, 128 - 2 * EDGE, EDGE), window)


def swapped(x):
    return pltpu.roll(x, 64, 1)


def packed_product(a, b, real):
    turned = swapped(b)
    return a * jnp.where(real, b, turned) + swapped(a) * jnp.where(real, -turned, b)


def finish_kernel(
    aux_ref, rows, mine_ref, beside_a_ref, beside_b_ref, halo_a_ref, halo_b_ref, inject_ref, coef_ref, done_hbm,
    near_hbm, volt_hbm, near, volt, out, sems,
):
    del done_hbm
    is_odd = ~even("bus")
    low = jnp.where(is_odd, halo_b_ref[...], halo_a_ref[...])
    high = jnp.where(is_odd, halo_a_ref[...], halo_b_ref[...])
    edges(low, high, inject_ref, coef_ref, volt)
    harm = lax.axis_index("harm")
    far = rows[pl.ds(FAR, H, stride=ROWS), :]
    far = jnp.where(harm == 0, low[32:], jnp.where(harm == H - 1, high[32:], far))
    near_converters(aux_ref, rows, far, (mine_ref, beside_a_ref, beside_b_ref), out)
    near[...] = out[...].astype(BF16)
    copies = [pltpu.make_async_copy(near, near_hbm, sems.at[4])]
    for e in range(2):
        for p in range(2):
            place = volt_hbm.at[p, 0, pl.ds(e * (inject_ref.shape[0] - EDGE), EDGE)]
            copies.append(pltpu.make_async_copy(volt.at[e, p], place, sems.at[2 * e + p]))
    for copy in copies:
        copy.start()
    for copy in copies:
        copy.wait()


def near_converters(aux_ref, rows, far, lifts, out):
    harm = lax.axis_index("harm")
    is_even = even("harm")
    a_at = jnp.where(is_even, 2, 0)
    b_at = 2 - a_at

    shape = (8, 128)
    lane = iota(shape, 1)
    real = lane < 64
    path = lane % 16
    notes = [ref[LIFT : LIFT + 16, :].astype(F32) for ref in lifts]
    spans = [aux_ref[1:2, :], aux_ref[2:3, :], notes[2][:1]]
    spans = [jnp.broadcast_to(x, shape).astype(I32) for x in spans]

    def place(bus, line):
        at = bus // SUB
        slot = jnp.where(at == 1, 0, jnp.where(at == a_at, 1, 2))
        return slot, line * SUB + bus % SUB

    def hop(bus, line):
        slot, at = place(bus, jnp.maximum(line - 1, 0))
        found = [jnp.take_along_axis(x, at, axis=1) for x in spans]
        far = jnp.where(slot == 0, found[0], jnp.where(slot == 1, found[1], found[2]))
        return bus + jnp.where(line == 0, 0, far)

    def coef_at(bus, line, used):
        slot, at = place(bus, line)
        return jnp.where(used, slot * 128 + at + jnp.where(real, 0, 64), -1)[:1]

    bus0 = jnp.broadcast_to(aux_ref[0:1, :], shape).astype(I32)
    valid = path < 1 + LINKS + LINKS * LINKS
    two = (path >= 1 + LINKS) & valid
    line1 = jnp.where(two, 1 + (path - 1 - LINKS) // LINKS, jnp.where(valid, path, 0))
    line2 = jnp.where(two, 1 + (path - 1 - LINKS) % LINKS, 0)
    bus1 = hop(bus0, line1)
    bus2 = hop(bus1, line2)
    places = [coef_at(bus0, line1, valid & (path >= 1)), coef_at(bus1, line2, two), coef_at(bus2, 0, valid)]
    pick = jnp.where(iota((3 * 128, 3 * 128), 0) == jnp.concatenate(places, axis=1), 1.0, 0.0).astype(BF16)
    window = jnp.concatenate(
        [
            rows[pl.ds(COEF, H, stride=ROWS), :].astype(BF16),
            rows[pl.ds(PAIR, H, stride=ROWS), :].astype(BF16),
            far.astype(BF16),
        ],
        axis=1,
    )
    found = jnp.dot(window, pick, preferred_element_type=F32)
    real, path = real[:1], path[:1]
    first = found[:, :128] + jnp.where(real & (path == 0), 1.0, 0.0)
    second = found[:, 128:256] + jnp.where(real & (path <= LINKS), 1.0, 0.0)
    weight = packed_product(packed_product(first, second, real), found[:, 256:], real)

    many = (128, 128)
    row = iota(many, 0)
    other = row % 64 % (3 * CONV)
    bus_of = jnp.zeros(many, I32)
    marks = [x[1:2] for x in notes]
    beside = jnp.where(is_even, 1, -1)
    for q, (at, column) in enumerate(((1, harm), (a_at, harm + beside), (b_at, harm - beside))):
        column = lax.rem(column + HALF, HALF)
        for c in range(CONV):
            bus = jnp.sum(jnp.where(iota((1, 128), 1) == c * HALF + column, marks[q], 0.0), axis=1, keepdims=True)
            bus = jnp.broadcast_to(bus.astype(I32), many) + at * SUB
            bus_of = jnp.where(other == q * CONV + c, bus, bus_of)
    wide = iota(many, 1)
    match = (row // 64 == wide // 64) & (row % 64 // (3 * CONV) == wide % 64 // 16) & (bus_of == bus2[:1])
    match = jnp.where(match, 1.0, 0.0).astype(BF16)
    high = weight.astype(BF16)
    rest = (weight - high.astype(F32)).astype(BF16)
    dims = (((1,), (1,)), ((), ()))
    table = lax.dot_general(high, match, dims, preferred_element_type=F32)
    table += lax.dot_general(rest, match, dims, preferred_element_type=F32)

    total = [[jnp.zeros((H, 128), F32) for _ in range(2)] for _ in range(CONV)]
    for q in range(3):
        for o in range(CONV):
            spec_r, spec_i = (lifts[q][(2 * o + p) * H : (2 * o + p + 1) * H, :].astype(F32) for p in range(2))
            for c in range(CONV):
                at = c * 3 * CONV + q * CONV + o
                add_r, add_i = product(table[:, at : at + 1], table[:, 64 + at : 65 + at], spec_r, spec_i)
                total[c][0] += add_r
                total[c][1] += add_i
    for c in range(CONV):
        for p in range(2):
            out[pl.ds(p * H * CONV + c, H, stride=CONV), :] = total[c][p]


VMEM = pl.BlockSpec(memory_space=pltpu.VMEM)
HBM = pl.BlockSpec(memory_space=pltpu.HBM)


def call(kernel, name, out_shape, in_specs, scratch=(), cost=(0, 0, 0), out_specs=None, aliases=None):
    flops, moved, hard = cost
    return pl.pallas_call(
        kernel,
        out_shape=out_shape,
        in_specs=in_specs,
        out_specs=out_specs or jax.tree.map(lambda _: VMEM, out_shape),
        input_output_aliases=aliases or {},
        scratch_shapes=list(scratch),
        compiler_params=pltpu.CompilerParams(vmem_limit_bytes=40 * 2**20),
        cost_estimate=pl.CostEstimate(flops=flops, bytes_accessed=moved, transcendentals=hard),
        name=name,
    )


def swaps(count):
    rounds = []
    for start in (0, 1):
        firsts = range(start, count - 1, 2)
        rounds.append([(i, i + 1) for i in firsts] + [(i + 1, i) for i in firsts])
    return rounds


def local(conv_volt, conv_power, conv_type, type_steep, conv_bus, admittance, link_offset):
    harm_count = lax.axis_size("harm")
    bus_count = lax.axis_size("bus")
    block = admittance.shape[3]
    snapshots = conv_volt.shape[3]
    tiles = block // TILE
    size = harm_count * ROWS
    kinds = 2 * H
    S = jax.ShapeDtypeStruct
    over_bus = swaps(bus_count)[::-1]
    number = lambda r: r % harm_count * bus_count + r // harm_count
    over_ranges = [[(number(s), number(d)) for s, d in pairs] for pairs in swaps(harm_count * bus_count)]

    basis = make_basis()
    coef, edge_a, edge_b, aux, payload, lift = call(
        begin_kernel,
        "begin",
        (
            S((16, block), F32),
            S((16, 128), F32),
            S((16, 128), F32),
            S((8, 128), F32),
            S((size, 128), BF16),
            S((LIFT + 16, 128), BF16),
        ),
        [HBM] * 9,
        [
            pltpu.VMEM((2, 4, 1, block), F32),
            pltpu.VMEM((LINKS, block), I32),
            pltpu.SMEM((CONV,), I32),
            pltpu.SMEM(type_steep.shape, F32),
            pltpu.SMEM((CONV,), I32),
            pltpu.VMEM((CONV, snapshots), F32),
            pltpu.VMEM((kinds * CONV, snapshots), BF16),
            pltpu.VMEM((NT, kinds), BF16),
            pltpu.VMEM((kinds, NT), BF16),
            pltpu.VMEM((kinds * CONV, snapshots), F32),
            pltpu.VMEM((harm_count, 128), F32),
            pltpu.VMEM((harm_count, 128), F32),
            pltpu.VMEM((size, 128), F32),
            pltpu.SemaphoreType.DMA((9,)),
        ],
        (2 * 2 * 128 * 1024 * 512, 2**20, 2**19),
    )(
        *(
            pltpu.with_memory_space_constraint(array, pltpu.HBM)
            for array in (
                admittance,
                link_offset,
                conv_type,
                type_steep,
                conv_bus,
                conv_power,
                conv_volt.reshape(kinds * CONV, snapshots),
                jnp.asarray(np.ascontiguousarray(basis.T)),
                jnp.asarray(basis),
            )
        )
    )

    four = (harm_count, ROWS // 4, 4, snapshots)
    got = lax.all_to_all(payload.reshape(four), "harm", split_axis=0, concat_axis=0, tiled=True)

    beside_a = lax.ppermute(lift, ("harm", "bus"), over_ranges[0])
    q = call(
        sweeps_kernel,
        "sweeps",
        S((tiles, 2 * TILE, WIN), BF16),
        [VMEM],
        cost=(2 * tiles * 256 * 256 * 512, 2**20, 0),
    )(coef)
    lift_b, q = lax.optimization_barrier((lift, q))
    beside_b = lax.ppermute(lift_b, ("harm", "bus"), over_ranges[1])
    got, q, beside_a = lax.optimization_barrier((got, q, beside_a))

    halo = S((32 + harm_count, 128), F32)
    rows, halo_a, halo_b = call(
        mix_kernel,
        "mix",
        (S((size, 128), F32), halo, halo),
        [VMEM] * 3,
    )(got.reshape(size, snapshots), edge_a, edge_b)
    halo_a = lax.ppermute(halo_a, "bus", over_bus[0])
    halo_b = lax.ppermute(halo_b, "bus", over_bus[1])
    out_volt = S((2, 1, block, snapshots), BF16)
    inject, bus_volt = call(
        inner_kernel,
        "inner",
        (S((block, 256), BF16), out_volt),
        [VMEM] * 2,
        [pltpu.VMEM((2, 1, block, snapshots), BF16), pltpu.SemaphoreType.DMA((tiles,))],
        (2 * tiles * 256 * 256 * 256, 2**20, 0),
        (VMEM, HBM),
    )(rows, q)
    beside_b, halo_a, halo_b, inject, bus_volt = lax.optimization_barrier((beside_b, halo_a, halo_b, inject, bus_volt))
    near, bus_volt = call(
        finish_kernel,
        "finish",
        (S((kinds * CONV, snapshots), BF16), out_volt),
        [VMEM] * 9 + [HBM],
        [
            pltpu.VMEM((kinds * CONV, snapshots), BF16),
            pltpu.VMEM((2, 2, EDGE, snapshots), BF16),
            pltpu.VMEM((kinds * CONV, 128), F32),
            pltpu.SemaphoreType.DMA((5,)),
        ],
        (2 * 10**7, 2**20, 0),
        (HBM, HBM),
        {9: 1},
    )(aux, rows, lift, beside_a, beside_b, halo_a, halo_b, inject, coef, bus_volt)
    return (bus_volt, near.reshape(2, H, CONV, snapshots))


def solution(mesh):
    in_specs = (
        P(None, None, ("bus", "harm"), None),
        P(("bus", "harm"), None),
        P(("bus", "harm")),
        P(),
        P(("bus", "harm")),
        P(None, None, "harm", "bus"),
        P(None, "bus"),
    )
    out_specs = (P(None, "harm", "bus", None), P(None, None, ("bus", "harm"), None))
    return jax.shard_map(local, mesh=mesh, in_specs=in_specs, out_specs=out_specs, check_vma=False)
```

```python
import math

import jax
import jax.numpy as jnp
import numpy as np
from jax import lax
from jax.experimental import pallas as pl
from jax.experimental.pallas import tpu as pltpu
from jax.sharding import PartitionSpec as P

H = 64
NT = 1024
REACH = 8
LINKS = 3
SUB = 16
CONV = 4
EDGE = 2 * REACH
TILE = 128
WIN = 256
ROWS = 12
COEF = 8
PAIR = 9
FAR = 10
MARK = 11
LIFT = CONV * 128
HALF = 32
F32 = jnp.float32
BF16 = jnp.bfloat16
I32 = jnp.int32


def make_basis():
    turn = np.arange(1, H + 1)[:, None] * np.arange(NT)[None, :] % NT
    angle = turn * (2.0 * math.pi / NT)
    return np.concatenate([np.cos(angle), -np.sin(angle)], axis=0).astype(BF16)


def iota(shape, dim):
    return lax.broadcasted_iota(I32, shape, dim)


def product(ar, ai, br, bi):
    return ar * br - ai * bi, ar * bi + ai * br


def grouped(x):
    k, j = iota((8, 128), 0), iota((8, 128), 1) // SUB
    for s in (1, 2, 4):
        later = pltpu.roll(pltpu.roll(x, s, 0), 128 - SUB * s, 1)
        sooner = pltpu.roll(pltpu.roll(x, 8 - s, 0), SUB * s, 1)
        bk, bj = (k // s) % 2, (j // s) % 2
        x = jnp.where(bk == bj, x, jnp.where(bk == 1, later, sooner))
    return x


def even(axis):
    return lax.rem(lax.axis_index(axis), 2) == 0


def begin_kernel(
    adm_hbm, off_hbm, type_hbm, steep_hbm, bus_hbm, power_hbm, volt_hbm, turned_hbm, basis_hbm,
    coef_ref, a_ref, b_ref, aux_ref, out_ref, lift_ref,
    adm, off, kind, steep, bus, power, volt_in, turned, basis, volts, groups, spans, rows, sems,
):
    pairs = [
        (adm_hbm, adm), (off_hbm, off), (type_hbm, kind), (steep_hbm, steep), (bus_hbm, bus), (power_hbm, power),
        (volt_hbm, volt_in), (turned_hbm, turned), (basis_hbm, basis),
    ]
    copies = [pltpu.make_async_copy(src, dst, sems.at[i]) for i, (src, dst) in enumerate(pairs)]
    for copy in copies:
        copy.start()
    for copy in copies:
        copy.wait()
    inv_r, inv_i = adm[0, 0], adm[1, 0]
    steps = [product(inv_r, inv_i, adm[0, k], adm[1, k]) for k in range(1, 1 + LINKS)]
    blank = jnp.zeros((5, inv_r.shape[1]), F32)
    coefs = jnp.concatenate(
        [inv_r] + [s[0] for s in steps] + [inv_i] + [s[1] for s in steps] + [off[...].astype(F32), blank], axis=0
    )
    coef_ref[...] = coefs
    tiles = coefs.shape[1] // 128
    for v in range(tiles):
        groups[v * 8 : v * 8 + 8, :] = grouped(coefs[:8, v * 128 : v * 128 + 128])
        spans[v * 8 : v * 8 + 8, :] = grouped(coefs[8:, v * 128 : v * 128 + 128])
    first, last = coefs[:, :128], coefs[:, tiles * 128 - 128 :]
    is_odd = ~even("bus")
    a_ref[...] = jnp.where(is_odd, last, first)
    b_ref[...] = jnp.where(is_odd, first, last)
    harm = lax.axis_index("harm")
    span = spans[pl.ds(harm, 1), :]
    aux_ref[1:2, :] = span
    aux_ref[2:3, :] = spans[pl.ds(harm + jnp.where(even("harm"), 1, -1), 1), :]
    group = groups[...]
    after, before = pltpu.roll(group, H - 1, 0), pltpu.roll(group, 1, 0)
    first_core = iota((H, 128), 0) % 2 == 0
    pair, far = jnp.where(first_core, after, before), jnp.where(first_core, before, after)
    rows[pl.ds(COEF, H, stride=ROWS), :] = group
    rows[pl.ds(PAIR, H, stride=ROWS), :] = pair
    rows[pl.ds(FAR, H, stride=ROWS), :] = far

    lane = iota((1, 128), 1)
    column = lax.rem(harm, HALF)
    mark = jnp.zeros((1, 128), F32)
    start = jnp.full((1, 128), SUB, F32)
    for c in range(CONV):
        number = lax.rem(bus[c], SUB).astype(F32)
        mark += jnp.where(lane == c * HALF + column, number, 0.0)
        start += jnp.where(lane % 64 // 16 == c, number, 0.0)
    aux_ref[0:1, :] = start
    rows[pl.ds(MARK, H, stride=ROWS), :] = jnp.broadcast_to(mark, (H, 128))

    volts[...] = volt_in[...].astype(F32)
    kinds = 2 * H
    volt = jnp.concatenate(
        [volts[pl.ds(c, kinds, stride=CONV), :].T for c in range(CONV)], axis=0
    ).astype(BF16)
    sharp = jnp.concatenate([jnp.full((128, 1), steep[kind[c]], F32) for c in range(CONV)], axis=0)
    strong = jnp.concatenate([power[...], jnp.zeros((8 - CONV, 128), F32)], axis=0).T
    strong = jnp.concatenate([strong[:, c : c + 1] for c in range(CONV)], axis=0)
    spectra = jnp.zeros((CONV * 128, kinds), F32)
    step = 256
    for n in range(0, NT, step):
        wave = jnp.dot(volt, basis[:, n : n + step], preferred_element_type=F32)
        current = (strong * jnp.tanh(sharp * wave)).astype(BF16)
        spectra += jnp.dot(current, turned[n : n + step, :], preferred_element_type=F32)
    spectra = spectra * NT ** (-0.5)
    lift_ref[:LIFT, :] = spectra.astype(BF16)
    for c in range(CONV):
        piece = spectra[c * 128 : c * 128 + 128].T
        for p in range(2):
            rows[pl.ds(2 * c + p, H, stride=ROWS), :] = piece[p * H : p * H + H]
    row = iota((16, 128), 0)
    notes = jnp.where(row == 0, span, jnp.where(row == 1, mark, 0.0))
    lift_ref[LIFT:, :] = notes.astype(BF16)
    out_ref[...] = rows[...].astype(BF16)


def sweeps_matrix(coefs, first, count):
    width = coefs.shape[1]
    rows = iota((width, width), 0)
    lanes = iota((1, width), 1)
    turned_r = jnp.zeros((width, width), F32)
    turned_i = jnp.zeros((width, width), F32)
    for k in range(LINKS):
        here = rows == lanes + coefs[8 + k : 9 + k].astype(I32)
        turned_r += jnp.where(here, coefs[1 + k : 2 + k], 0.0)
        turned_i += jnp.where(here, coefs[5 + k : 6 + k], 0.0)
    step_r, step_i = turned_r.T, turned_i.T
    mid_r, mid_i = step_r[first : first + count], step_i[first : first + count]
    twice = jnp.dot(
        jnp.concatenate([mid_r, mid_i], axis=0).astype(BF16),
        jnp.concatenate([step_r, step_i], axis=1).astype(BF16),
        preferred_element_type=F32,
    )
    same = iota((count, width), 0) + first == iota((count, width), 1)
    all_r = twice[:count, :width] - twice[count:, width:] + mid_r + jnp.where(same, 1.0, 0.0)
    all_i = twice[:count, width:] + twice[count:, :width] + mid_i
    q_r, q_i = product(all_r, all_i, coefs[0:1], coefs[4:5])
    return jnp.concatenate([q_r, q_i], axis=0).astype(BF16)


def volt_of(matrix, inject):
    count = matrix.shape[0] // 2
    acc = jnp.dot(matrix, inject, preferred_element_type=F32)
    return (acc[:count, :128] - acc[count:, 128:]).astype(BF16), (acc[:count, 128:] + acc[count:, :128]).astype(BF16)


def sweeps_kernel(coef_ref, q_ref):
    blank = jnp.zeros((coef_ref.shape[0], TILE), F32)
    tiles = q_ref.shape[0]
    for b in range(tiles):
        around = [coef_ref[:, t * TILE : t * TILE + TILE] if 0 <= t < tiles else blank for t in (b - 1, b, b + 1)]
        coefs = pltpu.roll(jnp.concatenate(around, axis=1), 2 * TILE + EDGE, 1)[:, :WIN]
        q_ref[b] = sweeps_matrix(coefs, EDGE, TILE)


def mix_kernel(got_ref, a_ref, b_ref, rows_ref, out_a_ref, out_b_ref):
    size = got_ref.shape[0]
    rows_ref[...] = got_ref[...].astype(F32)
    first, last = rows_ref[:16, :], pltpu.roll(rows_ref[size - 16 :, :], ROWS, 0)
    far = rows_ref[pl.ds(FAR, H, stride=ROWS), :]
    is_odd = ~even("bus")
    for ref, edge, range_rows in (
        (out_a_ref, a_ref, jnp.where(is_odd, last, first)),
        (out_b_ref, b_ref, jnp.where(is_odd, first, last)),
    ):
        ref[:16, :] = range_rows.astype(BF16)
        ref[16:32, :] = edge[...].astype(BF16)
        ref[32:, :] = far.astype(BF16)


def inner_kernel(rows, q_ref, inject, volt_hbm, volt, sems):
    def part(p):
        return jnp.concatenate(
            [
                rows[pl.ds(h * HALF * ROWS + 2 * c + p, HALF, stride=ROWS), :]
                for h in range(2)
                for c in range(CONV)
            ],
            axis=0,
        )

    spectra = jnp.concatenate([part(0), part(1)], axis=1).astype(BF16)
    convs = H * CONV
    at = [
        jnp.sum(rows[pl.ds(h * HALF * ROWS + MARK, HALF, stride=ROWS), :], axis=0, keepdims=True)
        for h in range(2)
    ]
    at = jnp.concatenate(at, axis=1).astype(I32)
    lane = iota((1, convs), 1)
    source = lane // (CONV * HALF) * HALF + lane % HALF
    target = source * SUB + at
    buses = H * SUB
    owner = jnp.where(iota((buses, convs), 0) == target, 1.0, 0.0).astype(BF16)
    inject[...] = jnp.dot(owner, spectra, preferred_element_type=F32).astype(BF16)
    tiles = q_ref.shape[0]
    copies = []
    for b in range(tiles):
        first = max(b * TILE - EDGE, 0)
        last = min(b * TILE - EDGE + WIN, buses)
        pieces = [jnp.zeros((n, 256), BF16) for n in (first - b * TILE + EDGE, b * TILE - EDGE + WIN - last)]
        pieces.insert(1, inject[first:last, :])
        window = jnp.concatenate([x for x in pieces if x.shape[0]], axis=0)
        volt[0, 0, b * TILE : b * TILE + TILE, :], volt[1, 0, b * TILE : b * TILE + TILE, :] = volt_of(
            q_ref[b], window
        )
        if b % 2:
            place = pl.ds(b * TILE - TILE, 2 * TILE)
            for p in range(2):
                copies.append(
                    pltpu.make_async_copy(volt.at[p, 0, place], volt_hbm.at[p, 0, place], sems.at[b - 1 + p])
                )
                copies[-1].start()
    for copy in copies:
        copy.wait()


def edges(low, high, inject_ref, coef_ref, volt):
    buses = inject_ref.shape[0]

    def injected(edge, lane0):
        total_r = jnp.zeros((SUB, 128), F32)
        total_i = jnp.zeros((SUB, 128), F32)
        for c in range(CONV):
            at = c * HALF + lane0
            bus = jnp.broadcast_to(edge[MARK : MARK + 1, at : at + 1], (SUB, 128)).astype(I32)
            here = iota((SUB, 128), 0) == bus
            total_r += jnp.where(here, edge[2 * c : 2 * c + 1, :], 0.0)
            total_i += jnp.where(here, edge[2 * c + 1 : 2 * c + 2, :], 0.0)
        return jnp.concatenate([total_r, total_i], axis=1).astype(BF16)

    coefs = jnp.concatenate([low[16:32], coef_ref[:, :128]], axis=1)
    coefs = pltpu.roll(coefs, 128 + EDGE, 1)[:, :128]
    window = jnp.concatenate([injected(low, HALF - 1), inject_ref[: 128 - EDGE, :]], axis=0)
    volt[0, 0], volt[0, 1] = volt_of(sweeps_matrix(coefs, EDGE, EDGE), window)
    coefs = jnp.concatenate([coef_ref[:, buses - 128 :], high[16:32]], axis=1)
    coefs = pltpu.roll(coefs, 256 - EDGE, 1)[:, :128]
    window = jnp.concatenate([inject_ref[buses - 128 + EDGE :, :], injected(high, 0)], axis=0)
    volt[1, 0], volt[1, 1] = volt_of(sweeps_matrix(coefs, 128 - 2 * EDGE, EDGE), window)


def swapped(x):
    return pltpu.roll(x, 64, 1)


def packed_product(a, b, real):
    turned = swapped(b)
    return a * jnp.where(real, b, turned) + swapped(a) * jnp.where(real, -turned, b)


def finish_kernel(
    aux_ref, rows, mine_ref, beside_a_ref, beside_b_ref, halo_a_ref, halo_b_ref, inject_ref, coef_ref, done_hbm,
    near_hbm, volt_hbm, near, volt, table, sums, out, sems,
):
    del done_hbm
    is_odd = ~even("bus")
    halo_a, halo_b = halo_a_ref[...].astype(F32), halo_b_ref[...].astype(F32)
    low, high = jnp.where(is_odd, halo_b, halo_a), jnp.where(is_odd, halo_a, halo_b)
    edges(low, high, inject_ref, coef_ref, volt)
    harm = lax.axis_index("harm")
    far = rows[pl.ds(FAR, H, stride=ROWS), :]
    far = jnp.where(harm == 0, low[32:], jnp.where(harm == H - 1, high[32:], far))
    near_converters(aux_ref, rows, far, (mine_ref, beside_a_ref, beside_b_ref), table, sums, out)
    near[...] = out[...].astype(BF16)
    copies = [pltpu.make_async_copy(near, near_hbm, sems.at[4])]
    for e in range(2):
        for p in range(2):
            place = volt_hbm.at[p, 0, pl.ds(e * (inject_ref.shape[0] - EDGE), EDGE)]
            copies.append(pltpu.make_async_copy(volt.at[e, p], place, sems.at[2 * e + p]))
    for copy in copies:
        copy.start()
    for copy in copies:
        copy.wait()


def near_converters(aux_ref, rows, far, lifts, table, sums, out):
    harm = lax.axis_index("harm")
    is_even = even("harm")
    a_at = jnp.where(is_even, 2, 0)
    b_at = 2 - a_at

    shape = (8, 128)
    lane = iota(shape, 1)
    real = lane < 64
    path = lane % 16
    notes = [ref[LIFT : LIFT + 16, :].astype(F32) for ref in lifts]
    spans = [aux_ref[1:2, :], aux_ref[2:3, :], notes[2][:1]]
    spans = [jnp.broadcast_to(x, shape).astype(I32) for x in spans]

    def place(bus, line):
        at = bus // SUB
        slot = jnp.where(at == 1, 0, jnp.where(at == a_at, 1, 2))
        return slot, line * SUB + bus % SUB

    def hop(bus, line):
        slot, at = place(bus, jnp.maximum(line - 1, 0))
        found = [jnp.take_along_axis(x, at, axis=1) for x in spans]
        far = jnp.where(slot == 0, found[0], jnp.where(slot == 1, found[1], found[2]))
        return bus + jnp.where(line == 0, 0, far)

    def coef_at(bus, line, used):
        slot, at = place(bus, line)
        return jnp.where(used, slot * 128 + at + jnp.where(real, 0, 64), -1)[:1]

    bus0 = jnp.broadcast_to(aux_ref[0:1, :], shape).astype(I32)
    valid = path < 1 + LINKS + LINKS * LINKS
    two = (path >= 1 + LINKS) & valid
    line1 = jnp.where(two, 1 + (path - 1 - LINKS) // LINKS, jnp.where(valid, path, 0))
    line2 = jnp.where(two, 1 + (path - 1 - LINKS) % LINKS, 0)
    bus1 = hop(bus0, line1)
    bus2 = hop(bus1, line2)
    places = [coef_at(bus0, line1, valid & (path >= 1)), coef_at(bus1, line2, two), coef_at(bus2, 0, valid)]
    pick = jnp.where(iota((3 * 128, 3 * 128), 0) == jnp.concatenate(places, axis=1), 1.0, 0.0).astype(BF16)
    window = jnp.concatenate(
        [
            rows[pl.ds(COEF, H, stride=ROWS), :].astype(BF16),
            rows[pl.ds(PAIR, H, stride=ROWS), :].astype(BF16),
            far.astype(BF16),
        ],
        axis=1,
    )
    found = jnp.dot(window, pick, preferred_element_type=F32)
    real, path = real[:1], path[:1]
    first = found[:, :128] + jnp.where(real & (path == 0), 1.0, 0.0)
    second = found[:, 128:256] + jnp.where(real & (path <= LINKS), 1.0, 0.0)
    weight = packed_product(packed_product(first, second, real), found[:, 256:], real)

    many = (128, 128)
    row = iota(many, 0)
    other = row % 64 % (3 * CONV)
    bus_of = jnp.zeros(many, I32)
    marks = [x[1:2] for x in notes]
    beside = jnp.where(is_even, 1, -1)
    for q, (at, column) in enumerate(((1, harm), (a_at, harm + beside), (b_at, harm - beside))):
        column = lax.rem(column + HALF, HALF)
        for c in range(CONV):
            bus = jnp.sum(jnp.where(iota((1, 128), 1) == c * HALF + column, marks[q], 0.0), axis=1, keepdims=True)
            bus = jnp.broadcast_to(bus.astype(I32), many) + at * SUB
            bus_of = jnp.where(other == q * CONV + c, bus, bus_of)
    wide = iota(many, 1)
    match = (row // 64 == wide // 64) & (row % 64 // (3 * CONV) == wide % 64 // 16) & (bus_of == bus2[:1])
    match = jnp.where(match, 1.0, 0.0).astype(BF16)
    weight = jnp.concatenate([weight, weight], axis=0)
    high = weight.astype(BF16)
    rest = (weight - high.astype(F32)).astype(BF16)
    dims = (((1,), (1,)), ((), ()))
    found = lax.dot_general(match, high, dims, preferred_element_type=F32)
    found += lax.dot_general(match, rest, dims, preferred_element_type=F32)
    table[:64, :] = found[:64]
    table[64:, :] = jnp.where(iota((64, 128), 1) < 64, -found[64:], found[64:])

    step = 32
    for at in range(0, 128, step):
        total = [jnp.zeros((step, 128), F32) for _ in range(CONV)]
        for q in range(3):
            for o in range(CONV):
                spec = lifts[q][o * 128 + at : o * 128 + at + step, :].astype(F32)
                turned = swapped(spec)
                for c in range(CONV):
                    n = c * 3 * CONV + q * CONV + o
                    total[c] += table[n : n + 1, :] * spec + table[64 + n : 65 + n, :] * turned
        for c in range(CONV):
            sums[c * 128 + at : c * 128 + at + step, :] = total[c]
    for c in range(CONV):
        turned = sums[c * 128 : c * 128 + 128, :].T
        for p in range(2):
            out[pl.ds(p * H * CONV + c, H, stride=CONV), :] = turned[p * H : p * H + H]


VMEM = pl.BlockSpec(memory_space=pltpu.VMEM)
HBM = pl.BlockSpec(memory_space=pltpu.HBM)


def call(kernel, name, out_shape, in_specs, scratch=(), cost=(0, 0, 0), out_specs=None, aliases=None):
    flops, moved, hard = cost
    return pl.pallas_call(
        kernel,
        out_shape=out_shape,
        in_specs=in_specs,
        out_specs=out_specs or jax.tree.map(lambda _: VMEM, out_shape),
        input_output_aliases=aliases or {},
        scratch_shapes=list(scratch),
        compiler_params=pltpu.CompilerParams(vmem_limit_bytes=40 * 2**20),
        cost_estimate=pl.CostEstimate(flops=flops, bytes_accessed=moved, transcendentals=hard),
        name=name,
    )


def swaps(count):
    rounds = []
    for start in (0, 1):
        firsts = range(start, count - 1, 2)
        rounds.append([(i, i + 1) for i in firsts] + [(i + 1, i) for i in firsts])
    return rounds


def local(conv_volt, conv_power, conv_type, type_steep, conv_bus, admittance, link_offset):
    harm_count = lax.axis_size("harm")
    bus_count = lax.axis_size("bus")
    block = admittance.shape[3]
    snapshots = conv_volt.shape[3]
    tiles = block // TILE
    size = harm_count * ROWS
    kinds = 2 * H
    S = jax.ShapeDtypeStruct
    over_bus = swaps(bus_count)[::-1]
    number = lambda r: r % harm_count * bus_count + r // harm_count
    over_ranges = [[(number(s), number(d)) for s, d in pairs] for pairs in swaps(harm_count * bus_count)]

    basis = make_basis()
    coef, edge_a, edge_b, aux, payload, lift = call(
        begin_kernel,
        "begin",
        (
            S((16, block), F32),
            S((16, 128), F32),
            S((16, 128), F32),
            S((8, 128), F32),
            S((size, 128), BF16),
            S((LIFT + 16, 128), BF16),
        ),
        [HBM] * 9,
        [
            pltpu.VMEM((2, 4, 1, block), F32),
            pltpu.VMEM((LINKS, block), I32),
            pltpu.SMEM((CONV,), I32),
            pltpu.SMEM(type_steep.shape, F32),
            pltpu.SMEM((CONV,), I32),
            pltpu.VMEM((CONV, snapshots), F32),
            pltpu.VMEM((kinds * CONV, snapshots), BF16),
            pltpu.VMEM((NT, kinds), BF16),
            pltpu.VMEM((kinds, NT), BF16),
            pltpu.VMEM((kinds * CONV, snapshots), F32),
            pltpu.VMEM((harm_count, 128), F32),
            pltpu.VMEM((harm_count, 128), F32),
            pltpu.VMEM((size, 128), F32),
            pltpu.SemaphoreType.DMA((9,)),
        ],
        (2 * 2 * 128 * 1024 * 512, 2**20, 2**19),
    )(
        *(
            pltpu.with_memory_space_constraint(array, pltpu.HBM)
            for array in (
                admittance,
                link_offset,
                conv_type,
                type_steep,
                conv_bus,
                conv_power,
                conv_volt.reshape(kinds * CONV, snapshots),
                jnp.asarray(np.ascontiguousarray(basis.T)),
                jnp.asarray(basis),
            )
        )
    )

    four = (harm_count, ROWS // 4, 4, snapshots)
    got = lax.all_to_all(payload.reshape(four), "harm", split_axis=0, concat_axis=0, tiled=True)

    beside_a = lax.ppermute(lift, ("harm", "bus"), over_ranges[0])
    q = call(
        sweeps_kernel,
        "sweeps",
        S((tiles, 2 * TILE, WIN), BF16),
        [VMEM],
        cost=(2 * tiles * 256 * 256 * 512, 2**20, 0),
    )(coef)
    lift_b, q = lax.optimization_barrier((lift, q))
    beside_b = lax.ppermute(lift_b, ("harm", "bus"), over_ranges[1])
    got, q, beside_a = lax.optimization_barrier((got, q, beside_a))

    halo = S((32 + harm_count, 128), BF16)
    rows, halo_a, halo_b = call(
        mix_kernel,
        "mix",
        (S((size, 128), F32), halo, halo),
        [VMEM] * 3,
    )(got.reshape(size, snapshots), edge_a, edge_b)
    halo_a = lax.ppermute(halo_a, "bus", over_bus[0])
    halo_b = lax.ppermute(halo_b, "bus", over_bus[1])
    out_volt = S((2, 1, block, snapshots), BF16)
    inject, bus_volt = call(
        inner_kernel,
        "inner",
        (S((block, 256), BF16), out_volt),
        [VMEM] * 2,
        [pltpu.VMEM((2, 1, block, snapshots), BF16), pltpu.SemaphoreType.DMA((tiles,))],
        (2 * tiles * 256 * 256 * 256, 2**20, 0),
        (VMEM, HBM),
    )(rows, q)
    beside_b, halo_a, halo_b, inject, bus_volt = lax.optimization_barrier((beside_b, halo_a, halo_b, inject, bus_volt))
    near, bus_volt = call(
        finish_kernel,
        "finish",
        (S((kinds * CONV, snapshots), BF16), out_volt),
        [VMEM] * 9 + [HBM],
        [
            pltpu.VMEM((kinds * CONV, snapshots), BF16),
            pltpu.VMEM((2, 2, EDGE, snapshots), BF16),
            pltpu.VMEM((128, 128), F32),
            pltpu.VMEM((CONV * 128, 128), F32),
            pltpu.VMEM((kinds * CONV, 128), F32),
            pltpu.SemaphoreType.DMA((5,)),
        ],
        (2 * 10**7, 2**20, 0),
        (HBM, HBM),
        {9: 1},
    )(aux, rows, lift, beside_a, beside_b, halo_a, halo_b, inject, coef, bus_volt)
    return (bus_volt, near.reshape(2, H, CONV, snapshots))


def solution(mesh):
    in_specs = (
        P(None, None, ("bus", "harm"), None),
        P(("bus", "harm"), None),
        P(("bus", "harm")),
        P(),
        P(("bus", "harm")),
        P(None, None, "harm", "bus"),
        P(None, "bus"),
    )
    out_specs = (P(None, "harm", "bus", None), P(None, None, ("bus", "harm"), None))
    return jax.shard_map(local, mesh=mesh, in_specs=in_specs, out_specs=out_specs, check_vma=False)
```

```python
import math

import jax
import jax.numpy as jnp
import numpy as np
from jax import lax
from jax.experimental import pallas as pl
from jax.experimental.pallas import tpu as pltpu
from jax.sharding import PartitionSpec as P

H = 64
NT = 1024
REACH = 8
LINKS = 3
SUB = 16
CONV = 4
EDGE = 2 * REACH
TILE = 128
WIN = 256
ROWS = 12
COEF = 8
PAIR = 9
FAR = 10
MARK = 11
LIFT = CONV * 128
HALF = 32
F32 = jnp.float32
BF16 = jnp.bfloat16
I32 = jnp.int32


def make_basis():
    turn = np.arange(1, H + 1)[:, None] * np.arange(NT)[None, :] % NT
    angle = turn * (2.0 * math.pi / NT)
    return np.concatenate([np.cos(angle), -np.sin(angle)], axis=0).astype(BF16)


def iota(shape, dim):
    return lax.broadcasted_iota(I32, shape, dim)


def product(ar, ai, br, bi):
    return ar * br - ai * bi, ar * bi + ai * br


def grouped(x):
    k, j = iota((8, 128), 0), iota((8, 128), 1) // SUB
    for s in (1, 2, 4):
        later = pltpu.roll(pltpu.roll(x, s, 0), 128 - SUB * s, 1)
        sooner = pltpu.roll(pltpu.roll(x, 8 - s, 0), SUB * s, 1)
        bk, bj = (k // s) % 2, (j // s) % 2
        x = jnp.where(bk == bj, x, jnp.where(bk == 1, later, sooner))
    return x


def even(axis):
    return lax.rem(lax.axis_index(axis), 2) == 0


def begin_kernel(
    adm_hbm, off_hbm, type_hbm, steep_hbm, bus_hbm, power_hbm, volt_hbm, turned_hbm, basis_hbm,
    coef_ref, a_ref, b_ref, aux_ref, spec_ref, out_hbm,
    adm, off, kind, steep, bus, power, volt_in, turned, basis, volts, groups, spans, rows, sent, sems,
):
    pairs = [
        (adm_hbm, adm), (off_hbm, off), (type_hbm, kind), (steep_hbm, steep), (bus_hbm, bus), (power_hbm, power),
        (volt_hbm, volt_in),
    ]
    for at in range(0, NT, NT // 2):
        pairs.append((turned_hbm.at[pl.ds(at, NT // 2)], turned.at[pl.ds(at, NT // 2)]))
    for at in (0, H):
        pairs.append((basis_hbm.at[pl.ds(at, H)], basis.at[pl.ds(at, H)]))
    copies = [pltpu.make_async_copy(src, dst, sems.at[i]) for i, (src, dst) in enumerate(pairs)]
    for copy in copies:
        copy.start()
    for copy in copies:
        copy.wait()
    inv_r, inv_i = adm[0, 0], adm[1, 0]
    steps = [product(inv_r, inv_i, adm[0, k], adm[1, k]) for k in range(1, 1 + LINKS)]
    blank = jnp.zeros((5, inv_r.shape[1]), F32)
    coefs = jnp.concatenate(
        [inv_r] + [s[0] for s in steps] + [inv_i] + [s[1] for s in steps] + [off[...].astype(F32), blank], axis=0
    )
    coef_ref[...] = coefs
    tiles = coefs.shape[1] // 128
    for v in range(tiles):
        groups[v * 8 : v * 8 + 8, :] = grouped(coefs[:8, v * 128 : v * 128 + 128])
        spans[v * 8 : v * 8 + 8, :] = grouped(coefs[8:, v * 128 : v * 128 + 128])
    first, last = coefs[:, :128], coefs[:, tiles * 128 - 128 :]
    is_odd = ~even("bus")
    a_ref[...] = jnp.where(is_odd, last, first)
    b_ref[...] = jnp.where(is_odd, first, last)
    harm = lax.axis_index("harm")
    span = spans[pl.ds(harm, 1), :]
    aux_ref[1:2, :] = span
    aux_ref[2:3, :] = spans[pl.ds(harm + jnp.where(even("harm"), 1, -1), 1), :]
    group = groups[...]
    after, before = pltpu.roll(group, H - 1, 0), pltpu.roll(group, 1, 0)
    first_core = iota((H, 128), 0) % 2 == 0
    pair, far = jnp.where(first_core, after, before), jnp.where(first_core, before, after)
    rows[pl.ds(COEF, H, stride=ROWS), :] = group
    rows[pl.ds(PAIR, H, stride=ROWS), :] = pair
    rows[pl.ds(FAR, H, stride=ROWS), :] = far

    lane = iota((1, 128), 1)
    column = lax.rem(harm, HALF)
    mark = jnp.zeros((1, 128), F32)
    start = jnp.full((1, 128), SUB, F32)
    for c in range(CONV):
        number = lax.rem(bus[c], SUB).astype(F32)
        mark += jnp.where(lane == c * HALF + column, number, 0.0)
        start += jnp.where(lane % 64 // 16 == c, number, 0.0)
    aux_ref[0:1, :] = start
    rows[pl.ds(MARK, H, stride=ROWS), :] = jnp.broadcast_to(mark, (H, 128))

    volts[...] = volt_in[...].astype(F32)
    kinds = 2 * H
    volt = jnp.concatenate(
        [volts[pl.ds(c, kinds, stride=CONV), :] for c in range(CONV)], axis=1
    ).astype(BF16)
    sharp = jnp.concatenate([jnp.full((1, 128), steep[kind[c]], F32) for c in range(CONV)], axis=1)
    strong = jnp.concatenate([power[c : c + 1, :] for c in range(CONV)], axis=1)
    spectra = jnp.zeros((kinds, CONV * 128), F32)
    step = 256
    for n in range(0, NT, step):
        wave = jnp.dot(turned[n : n + step, :], volt, preferred_element_type=F32)
        current = (strong * jnp.tanh(sharp * wave)).astype(BF16)
        spectra += jnp.dot(basis[:, n : n + step], current, preferred_element_type=F32)
    spectra = spectra * NT ** (-0.5)
    spec_ref[...] = spectra
    for c in range(CONV):
        for p in range(2):
            rows[pl.ds(2 * c + p, H, stride=ROWS), :] = spectra[p * H : p * H + H, c * 128 : c * 128 + 128]
    aux_ref[3:4, :] = mark
    size = rows.shape[0] // 4
    copies = []
    for at in range(0, 4 * size, size):
        part = pl.ds(at, size)
        sent[part, :] = rows[part, :].astype(BF16)
        copies.append(pltpu.make_async_copy(sent.at[part], out_hbm.at[part], sems.at[at // size]))
        copies[-1].start()
    for copy in copies:
        copy.wait()


def sweeps_matrix(coefs, first, count):
    width = coefs.shape[1]
    rows = iota((width, width), 0)
    lanes = iota((1, width), 1)
    turned_r = jnp.zeros((width, width), F32)
    turned_i = jnp.zeros((width, width), F32)
    for k in range(LINKS):
        here = rows == lanes + coefs[8 + k : 9 + k].astype(I32)
        turned_r += jnp.where(here, coefs[1 + k : 2 + k], 0.0)
        turned_i += jnp.where(here, coefs[5 + k : 6 + k], 0.0)
    step_r, step_i = turned_r.T, turned_i.T
    mid_r, mid_i = step_r[first : first + count], step_i[first : first + count]
    twice = jnp.dot(
        jnp.concatenate([mid_r, mid_i], axis=0).astype(BF16),
        jnp.concatenate([step_r, step_i], axis=1).astype(BF16),
        preferred_element_type=F32,
    )
    same = iota((count, width), 0) + first == iota((count, width), 1)
    all_r = twice[:count, :width] - twice[count:, width:] + mid_r + jnp.where(same, 1.0, 0.0)
    all_i = twice[:count, width:] + twice[count:, :width] + mid_i
    q_r, q_i = product(all_r, all_i, coefs[0:1], coefs[4:5])
    return jnp.concatenate([q_r, q_i], axis=0).astype(BF16)


def volt_of(matrix, inject):
    count = matrix.shape[0] // 2
    acc = jnp.dot(matrix, inject, preferred_element_type=F32)
    return (acc[:count, :128] - acc[count:, 128:]).astype(BF16), (acc[:count, 128:] + acc[count:, :128]).astype(BF16)


def sweeps_kernel(coef_ref, spec_ref, aux_ref, q_ref, lift_ref):
    for c in range(CONV):
        lift_ref[c * 128 : c * 128 + 128, :] = spec_ref[:, c * 128 : c * 128 + 128].T.astype(BF16)
    row = iota((16, 128), 0)
    notes = jnp.where(row == 0, aux_ref[1:2, :], jnp.where(row == 1, aux_ref[3:4, :], 0.0))
    lift_ref[LIFT:, :] = notes.astype(BF16)
    blank = jnp.zeros((coef_ref.shape[0], TILE), F32)
    tiles = q_ref.shape[0]
    for b in range(tiles):
        around = [coef_ref[:, t * TILE : t * TILE + TILE] if 0 <= t < tiles else blank for t in (b - 1, b, b + 1)]
        coefs = pltpu.roll(jnp.concatenate(around, axis=1), 2 * TILE + EDGE, 1)[:, :WIN]
        q_ref[b] = sweeps_matrix(coefs, EDGE, TILE)


def mix_kernel(got_ref, a_ref, b_ref, rows_ref, out_a_ref, out_b_ref):
    size = got_ref.shape[0]
    rows_ref[...] = got_ref[...].astype(F32)
    first, last = rows_ref[:16, :], pltpu.roll(rows_ref[size - 16 :, :], ROWS, 0)
    far = rows_ref[pl.ds(FAR, H, stride=ROWS), :]
    is_odd = ~even("bus")
    for ref, edge, range_rows in (
        (out_a_ref, a_ref, jnp.where(is_odd, last, first)),
        (out_b_ref, b_ref, jnp.where(is_odd, first, last)),
    ):
        ref[:16, :] = range_rows.astype(BF16)
        ref[16:32, :] = edge[...].astype(BF16)
        ref[32:, :] = far.astype(BF16)


def inner_kernel(rows, q_ref, inject, volt_hbm, volt, sems):
    def part(p):
        return jnp.concatenate(
            [
                rows[pl.ds(h * HALF * ROWS + 2 * c + p, HALF, stride=ROWS), :]
                for h in range(2)
                for c in range(CONV)
            ],
            axis=0,
        )

    spectra = jnp.concatenate([part(0), part(1)], axis=1).astype(BF16)
    convs = H * CONV
    at = [
        jnp.sum(rows[pl.ds(h * HALF * ROWS + MARK, HALF, stride=ROWS), :], axis=0, keepdims=True)
        for h in range(2)
    ]
    at = jnp.concatenate(at, axis=1).astype(I32)
    lane = iota((1, convs), 1)
    source = lane // (CONV * HALF) * HALF + lane % HALF
    target = source * SUB + at
    buses = H * SUB
    owner = jnp.where(iota((buses, convs), 0) == target, 1.0, 0.0).astype(BF16)
    inject[...] = jnp.dot(owner, spectra, preferred_element_type=F32).astype(BF16)
    tiles = q_ref.shape[0]
    copies = []
    for b in range(tiles):
        first = max(b * TILE - EDGE, 0)
        last = min(b * TILE - EDGE + WIN, buses)
        pieces = [jnp.zeros((n, 256), BF16) for n in (first - b * TILE + EDGE, b * TILE - EDGE + WIN - last)]
        pieces.insert(1, inject[first:last, :])
        window = jnp.concatenate([x for x in pieces if x.shape[0]], axis=0)
        volt[0, 0, b * TILE : b * TILE + TILE, :], volt[1, 0, b * TILE : b * TILE + TILE, :] = volt_of(
            q_ref[b], window
        )
        if b % 2:
            place = pl.ds(b * TILE - TILE, 2 * TILE)
            for p in range(2):
                copies.append(
                    pltpu.make_async_copy(volt.at[p, 0, place], volt_hbm.at[p, 0, place], sems.at[b - 1 + p])
                )
                copies[-1].start()
    for copy in copies:
        copy.wait()


def edges(low, high, inject_ref, coef_ref, volt):
    buses = inject_ref.shape[0]

    def injected(edge, lane0):
        total_r = jnp.zeros((SUB, 128), F32)
        total_i = jnp.zeros((SUB, 128), F32)
        for c in range(CONV):
            at = c * HALF + lane0
            bus = jnp.broadcast_to(edge[MARK : MARK + 1, at : at + 1], (SUB, 128)).astype(I32)
            here = iota((SUB, 128), 0) == bus
            total_r += jnp.where(here, edge[2 * c : 2 * c + 1, :], 0.0)
            total_i += jnp.where(here, edge[2 * c + 1 : 2 * c + 2, :], 0.0)
        return jnp.concatenate([total_r, total_i], axis=1).astype(BF16)

    coefs = jnp.concatenate([low[16:32], coef_ref[:, :128]], axis=1)
    coefs = pltpu.roll(coefs, 128 + EDGE, 1)[:, :128]
    window = jnp.concatenate([injected(low, HALF - 1), inject_ref[: 128 - EDGE, :]], axis=0)
    volt[0, 0], volt[0, 1] = volt_of(sweeps_matrix(coefs, EDGE, EDGE), window)
    coefs = jnp.concatenate([coef_ref[:, buses - 128 :], high[16:32]], axis=1)
    coefs = pltpu.roll(coefs, 256 - EDGE, 1)[:, :128]
    window = jnp.concatenate([inject_ref[buses - 128 + EDGE :, :], injected(high, 0)], axis=0)
    volt[1, 0], volt[1, 1] = volt_of(sweeps_matrix(coefs, 128 - 2 * EDGE, EDGE), window)


def swapped(x):
    return pltpu.roll(x, 64, 1)


def packed_product(a, b, real):
    turned = swapped(b)
    return a * jnp.where(real, b, turned) + swapped(a) * jnp.where(real, -turned, b)


def finish_kernel(
    aux_ref, rows, mine_ref, beside_a_ref, beside_b_ref, halo_a_ref, halo_b_ref, inject_ref, coef_ref, done_hbm,
    near_hbm, volt_hbm, near, volt, table, sums, out, sems,
):
    del done_hbm
    is_odd = ~even("bus")
    halo_a, halo_b = halo_a_ref[...].astype(F32), halo_b_ref[...].astype(F32)
    low, high = jnp.where(is_odd, halo_b, halo_a), jnp.where(is_odd, halo_a, halo_b)
    edges(low, high, inject_ref, coef_ref, volt)
    harm = lax.axis_index("harm")
    far = rows[pl.ds(FAR, H, stride=ROWS), :]
    far = jnp.where(harm == 0, low[32:], jnp.where(harm == H - 1, high[32:], far))
    near_converters(aux_ref, rows, far, (mine_ref, beside_a_ref, beside_b_ref), table, sums, out)
    near[...] = out[...].astype(BF16)
    copies = [pltpu.make_async_copy(near, near_hbm, sems.at[4])]
    for e in range(2):
        for p in range(2):
            place = volt_hbm.at[p, 0, pl.ds(e * (inject_ref.shape[0] - EDGE), EDGE)]
            copies.append(pltpu.make_async_copy(volt.at[e, p], place, sems.at[2 * e + p]))
    for copy in copies:
        copy.start()
    for copy in copies:
        copy.wait()


def near_converters(aux_ref, rows, far, lifts, table, sums, out):
    harm = lax.axis_index("harm")
    is_even = even("harm")
    a_at = jnp.where(is_even, 2, 0)
    b_at = 2 - a_at

    shape = (8, 128)
    lane = iota(shape, 1)
    real = lane < 64
    path = lane % 16
    notes = [ref[LIFT : LIFT + 16, :].astype(F32) for ref in lifts]
    spans = [aux_ref[1:2, :], aux_ref[2:3, :], notes[2][:1]]
    spans = [jnp.broadcast_to(x, shape).astype(I32) for x in spans]

    def place(bus, line):
        at = bus // SUB
        slot = jnp.where(at == 1, 0, jnp.where(at == a_at, 1, 2))
        return slot, line * SUB + bus % SUB

    def hop(bus, line):
        slot, at = place(bus, jnp.maximum(line - 1, 0))
        found = [jnp.take_along_axis(x, at, axis=1) for x in spans]
        far = jnp.where(slot == 0, found[0], jnp.where(slot == 1, found[1], found[2]))
        return bus + jnp.where(line == 0, 0, far)

    def coef_at(bus, line, used):
        slot, at = place(bus, line)
        return jnp.where(used, slot * 128 + at + jnp.where(real, 0, 64), -1)[:1]

    bus0 = jnp.broadcast_to(aux_ref[0:1, :], shape).astype(I32)
    valid = path < 1 + LINKS + LINKS * LINKS
    two = (path >= 1 + LINKS) & valid
    line1 = jnp.where(two, 1 + (path - 1 - LINKS) // LINKS, jnp.where(valid, path, 0))
    line2 = jnp.where(two, 1 + (path - 1 - LINKS) % LINKS, 0)
    bus1 = hop(bus0, line1)
    bus2 = hop(bus1, line2)
    places = [coef_at(bus0, line1, valid & (path >= 1)), coef_at(bus1, line2, two), coef_at(bus2, 0, valid)]
    pick = jnp.where(iota((3 * 128, 3 * 128), 0) == jnp.concatenate(places, axis=1), 1.0, 0.0).astype(BF16)
    window = jnp.concatenate(
        [
            rows[pl.ds(COEF, H, stride=ROWS), :].astype(BF16),
            rows[pl.ds(PAIR, H, stride=ROWS), :].astype(BF16),
            far.astype(BF16),
        ],
        axis=1,
    )
    found = jnp.dot(window, pick, preferred_element_type=F32)
    real, path = real[:1], path[:1]
    first = found[:, :128] + jnp.where(real & (path == 0), 1.0, 0.0)
    second = found[:, 128:256] + jnp.where(real & (path <= LINKS), 1.0, 0.0)
    weight = packed_product(packed_product(first, second, real), found[:, 256:], real)

    many = (128, 128)
    row = iota(many, 0)
    other = row % 64 % (3 * CONV)
    bus_of = jnp.zeros(many, I32)
    marks = [x[1:2] for x in notes]
    beside = jnp.where(is_even, 1, -1)
    for q, (at, column) in enumerate(((1, harm), (a_at, harm + beside), (b_at, harm - beside))):
        column = lax.rem(column + HALF, HALF)
        for c in range(CONV):
            bus = jnp.sum(jnp.where(iota((1, 128), 1) == c * HALF + column, marks[q], 0.0), axis=1, keepdims=True)
            bus = jnp.broadcast_to(bus.astype(I32), many) + at * SUB
            bus_of = jnp.where(other == q * CONV + c, bus, bus_of)
    wide = iota(many, 1)
    match = (row // 64 == wide // 64) & (row % 64 // (3 * CONV) == wide % 64 // 16) & (bus_of == bus2[:1])
    match = jnp.where(match, 1.0, 0.0).astype(BF16)
    weight = jnp.concatenate([weight, weight], axis=0)
    high = weight.astype(BF16)
    rest = (weight - high.astype(F32)).astype(BF16)
    dims = (((1,), (1,)), ((), ()))
    found = lax.dot_general(match, high, dims, preferred_element_type=F32)
    found += lax.dot_general(match, rest, dims, preferred_element_type=F32)
    table[:64, :] = found[:64]
    table[64:, :] = jnp.where(iota((64, 128), 1) < 64, -found[64:], found[64:])

    step = 32
    for at in range(0, 128, step):
        total = [jnp.zeros((step, 128), F32) for _ in range(CONV)]
        for q in range(3):
            for o in range(CONV):
                spec = lifts[q][o * 128 + at : o * 128 + at + step, :].astype(F32)
                turned = swapped(spec)
                for c in range(CONV):
                    n = c * 3 * CONV + q * CONV + o
                    total[c] += table[n : n + 1, :] * spec + table[64 + n : 65 + n, :] * turned
        for c in range(CONV):
            sums[c * 128 + at : c * 128 + at + step, :] = total[c]
    for c in range(CONV):
        turned = sums[c * 128 : c * 128 + 128, :].T
        for p in range(2):
            out[pl.ds(p * H * CONV + c, H, stride=CONV), :] = turned[p * H : p * H + H]


VMEM = pl.BlockSpec(memory_space=pltpu.VMEM)
HBM = pl.BlockSpec(memory_space=pltpu.HBM)


def call(kernel, name, out_shape, in_specs, scratch=(), cost=(0, 0, 0), out_specs=None, aliases=None):
    flops, moved, hard = cost
    return pl.pallas_call(
        kernel,
        out_shape=out_shape,
        in_specs=in_specs,
        out_specs=out_specs or jax.tree.map(lambda _: VMEM, out_shape),
        input_output_aliases=aliases or {},
        scratch_shapes=list(scratch),
        compiler_params=pltpu.CompilerParams(vmem_limit_bytes=40 * 2**20),
        cost_estimate=pl.CostEstimate(flops=flops, bytes_accessed=moved, transcendentals=hard),
        name=name,
    )


def swaps(count):
    rounds = []
    for start in (0, 1):
        firsts = range(start, count - 1, 2)
        rounds.append([(i, i + 1) for i in firsts] + [(i + 1, i) for i in firsts])
    return rounds


def local(conv_volt, conv_power, conv_type, type_steep, conv_bus, admittance, link_offset):
    harm_count = lax.axis_size("harm")
    bus_count = lax.axis_size("bus")
    block = admittance.shape[3]
    snapshots = conv_volt.shape[3]
    tiles = block // TILE
    size = harm_count * ROWS
    kinds = 2 * H
    S = jax.ShapeDtypeStruct
    over_bus = swaps(bus_count)[::-1]
    number = lambda r: r % harm_count * bus_count + r // harm_count
    over_ranges = [[(number(s), number(d)) for s, d in pairs] for pairs in swaps(harm_count * bus_count)]

    basis = make_basis()
    coef, edge_a, edge_b, aux, spectra, payload = call(
        begin_kernel,
        "begin",
        (
            S((16, block), F32),
            S((16, 128), F32),
            S((16, 128), F32),
            S((8, 128), F32),
            S((kinds, CONV * 128), F32),
            S((size, 128), BF16),
        ),
        [HBM] * 9,
        [
            pltpu.VMEM((2, 4, 1, block), F32),
            pltpu.VMEM((LINKS, block), I32),
            pltpu.SMEM((CONV,), I32),
            pltpu.SMEM(type_steep.shape, F32),
            pltpu.SMEM((CONV,), I32),
            pltpu.VMEM((CONV, snapshots), F32),
            pltpu.VMEM((kinds * CONV, snapshots), BF16),
            pltpu.VMEM((NT, kinds), BF16),
            pltpu.VMEM((kinds, NT), BF16),
            pltpu.VMEM((kinds * CONV, snapshots), F32),
            pltpu.VMEM((harm_count, 128), F32),
            pltpu.VMEM((harm_count, 128), F32),
            pltpu.VMEM((size, 128), F32),
            pltpu.VMEM((size, 128), BF16),
            pltpu.SemaphoreType.DMA((11,)),
        ],
        (2 * 2 * 128 * 1024 * 512, 2**20, 2**19),
        (VMEM,) * 5 + (HBM,),
    )(
        *(
            pltpu.with_memory_space_constraint(array, pltpu.HBM)
            for array in (
                admittance,
                link_offset,
                conv_type,
                type_steep,
                conv_bus,
                conv_power,
                conv_volt.reshape(kinds * CONV, snapshots),
                jnp.asarray(np.ascontiguousarray(basis.T)),
                jnp.asarray(basis),
            )
        )
    )

    four = (harm_count, ROWS // 4, 4, snapshots)
    got = lax.all_to_all(payload.reshape(four), "harm", split_axis=0, concat_axis=0, tiled=True)

    q, lift = call(
        sweeps_kernel,
        "sweeps",
        (S((tiles, 2 * TILE, WIN), BF16), S((LIFT + 16, 128), BF16)),
        [VMEM] * 3,
        cost=(2 * tiles * 256 * 256 * 512, 2**20, 0),
    )(coef, spectra, aux)
    beside_a = lax.ppermute(lift, ("harm", "bus"), over_ranges[0])
    beside_b = lax.ppermute(lift, ("harm", "bus"), over_ranges[1])
    got, q, beside_a = lax.optimization_barrier((got, q, beside_a))

    halo = S((32 + harm_count, 128), BF16)
    rows, halo_a, halo_b = call(
        mix_kernel,
        "mix",
        (S((size, 128), F32), halo, halo),
        [VMEM] * 3,
    )(got.reshape(size, snapshots), edge_a, edge_b)
    halo_a = lax.ppermute(halo_a, "bus", over_bus[0])
    halo_b = lax.ppermute(halo_b, "bus", over_bus[1])
    out_volt = S((2, 1, block, snapshots), BF16)
    inject, bus_volt = call(
        inner_kernel,
        "inner",
        (S((block, 256), BF16), out_volt),
        [VMEM] * 2,
        [pltpu.VMEM((2, 1, block, snapshots), BF16), pltpu.SemaphoreType.DMA((tiles,))],
        (2 * tiles * 256 * 256 * 256, 2**20, 0),
        (VMEM, HBM),
    )(rows, q)
    beside_b, halo_a, halo_b, inject, bus_volt = lax.optimization_barrier((beside_b, halo_a, halo_b, inject, bus_volt))
    near, bus_volt = call(
        finish_kernel,
        "finish",
        (S((kinds * CONV, snapshots), BF16), out_volt),
        [VMEM] * 9 + [HBM],
        [
            pltpu.VMEM((kinds * CONV, snapshots), BF16),
            pltpu.VMEM((2, 2, EDGE, snapshots), BF16),
            pltpu.VMEM((128, 128), F32),
            pltpu.VMEM((CONV * 128, 128), F32),
            pltpu.VMEM((kinds * CONV, 128), F32),
            pltpu.SemaphoreType.DMA((5,)),
        ],
        (2 * 10**7, 2**20, 0),
        (HBM, HBM),
        {9: 1},
    )(aux, rows, lift, beside_a, beside_b, halo_a, halo_b, inject, coef, bus_volt)
    return (bus_volt, near.reshape(2, H, CONV, snapshots))


def solution(mesh):
    in_specs = (
        P(None, None, ("bus", "harm"), None),
        P(("bus", "harm"), None),
        P(("bus", "harm")),
        P(),
        P(("bus", "harm")),
        P(None, None, "harm", "bus"),
        P(None, "bus"),
    )
    out_specs = (P(None, "harm", "bus", None), P(None, None, ("bus", "harm"), None))
    return jax.shard_map(local, mesh=mesh, in_specs=in_specs, out_specs=out_specs, check_vma=False)
```

```python
import math

import jax
import jax.numpy as jnp
import numpy as np
from jax import lax
from jax.experimental import pallas as pl
from jax.experimental.pallas import tpu as pltpu
from jax.sharding import PartitionSpec as P

H = 64
NT = 1024
REACH = 8
LINKS = 3
SUB = 16
CONV = 4
EDGE = 2 * REACH
TILE = 128
WIN = 256
ROWS = 12
COEF = 8
PAIR = 9
FAR = 10
MARK = 11
LIFT = CONV * 128
HALF = 32
F32 = jnp.float32
BF16 = jnp.bfloat16
I32 = jnp.int32


def make_basis():
    turn = np.arange(1, H + 1)[:, None] * np.arange(NT)[None, :] % NT
    angle = turn * (2.0 * math.pi / NT)
    return np.concatenate([np.cos(angle), -np.sin(angle)], axis=0).astype(BF16)


def iota(shape, dim):
    return lax.broadcasted_iota(I32, shape, dim)


def product(ar, ai, br, bi):
    return ar * br - ai * bi, ar * bi + ai * br


def grouped(x):
    k, j = iota((8, 128), 0), iota((8, 128), 1) // SUB
    for s in (1, 2, 4):
        later = pltpu.roll(pltpu.roll(x, s, 0), 128 - SUB * s, 1)
        sooner = pltpu.roll(pltpu.roll(x, 8 - s, 0), SUB * s, 1)
        bk, bj = (k // s) % 2, (j // s) % 2
        x = jnp.where(bk == bj, x, jnp.where(bk == 1, later, sooner))
    return x


def even(axis):
    return lax.rem(lax.axis_index(axis), 2) == 0


def begin_kernel(
    adm_hbm, off_hbm, type_hbm, steep_hbm, bus_hbm, power_hbm, volt_hbm, turned_hbm, basis_hbm,
    coef_ref, a_ref, b_ref, aux_ref, spec_ref, out_hbm,
    adm, off, kind, steep, bus, power, volt_in, turned, basis, volts, groups, spans, rows, sent, sems,
):
    pairs = [
        (adm_hbm, adm), (off_hbm, off), (type_hbm, kind), (steep_hbm, steep), (bus_hbm, bus), (power_hbm, power),
        (volt_hbm, volt_in),
    ]
    for at in range(0, NT, NT // 2):
        pairs.append((turned_hbm.at[pl.ds(at, NT // 2)], turned.at[pl.ds(at, NT // 2)]))
    for at in (0, H):
        pairs.append((basis_hbm.at[pl.ds(at, H)], basis.at[pl.ds(at, H)]))
    copies = [pltpu.make_async_copy(src, dst, sems.at[i]) for i, (src, dst) in enumerate(pairs)]
    for copy in copies:
        copy.start()
    for copy in copies:
        copy.wait()
    inv_r, inv_i = adm[0, 0], adm[1, 0]
    steps = [product(inv_r, inv_i, adm[0, k], adm[1, k]) for k in range(1, 1 + LINKS)]
    blank = jnp.zeros((5, inv_r.shape[1]), F32)
    coefs = jnp.concatenate(
        [inv_r] + [s[0] for s in steps] + [inv_i] + [s[1] for s in steps] + [off[...].astype(F32), blank], axis=0
    )
    coef_ref[...] = coefs
    tiles = coefs.shape[1] // 128
    for v in range(tiles):
        groups[v * 8 : v * 8 + 8, :] = grouped(coefs[:8, v * 128 : v * 128 + 128])
        spans[v * 8 : v * 8 + 8, :] = grouped(coefs[8:, v * 128 : v * 128 + 128])
    first, last = coefs[:, :128], coefs[:, tiles * 128 - 128 :]
    is_odd = ~even("bus")
    a_ref[...] = jnp.where(is_odd, last, first)
    b_ref[...] = jnp.where(is_odd, first, last)
    harm = lax.axis_index("harm")
    span = spans[pl.ds(harm, 1), :]
    aux_ref[1:2, :] = span
    aux_ref[2:3, :] = spans[pl.ds(harm + jnp.where(even("harm"), 1, -1), 1), :]
    group = groups[...]
    after, before = pltpu.roll(group, H - 1, 0), pltpu.roll(group, 1, 0)
    first_core = iota((H, 128), 0) % 2 == 0
    pair, far = jnp.where(first_core, after, before), jnp.where(first_core, before, after)
    rows[pl.ds(COEF, H, stride=ROWS), :] = group
    rows[pl.ds(PAIR, H, stride=ROWS), :] = pair
    rows[pl.ds(FAR, H, stride=ROWS), :] = far

    lane = iota((1, 128), 1)
    column = lax.rem(harm, HALF)
    mark = jnp.zeros((1, 128), F32)
    start = jnp.full((1, 128), SUB, F32)
    for c in range(CONV):
        number = lax.rem(bus[c], SUB).astype(F32)
        mark += jnp.where(lane == c * HALF + column, number, 0.0)
        start += jnp.where(lane % 64 // 16 == c, number, 0.0)
    aux_ref[0:1, :] = start
    rows[pl.ds(MARK, H, stride=ROWS), :] = jnp.broadcast_to(mark, (H, 128))

    volts[...] = volt_in[...].astype(F32)
    kinds = 2 * H
    volt = jnp.concatenate(
        [volts[pl.ds(c, kinds, stride=CONV), :] for c in range(CONV)], axis=1
    ).astype(BF16)
    sharp = jnp.concatenate([jnp.full((1, 128), steep[kind[c]], F32) for c in range(CONV)], axis=1)
    strong = jnp.concatenate([power[c : c + 1, :] for c in range(CONV)], axis=1)
    spectra = jnp.zeros((kinds, CONV * 128), F32)
    step = 256
    for n in range(0, NT, step):
        wave = jnp.dot(turned[n : n + step, :], volt, preferred_element_type=F32)
        current = (strong * jnp.tanh(sharp * wave)).astype(BF16)
        spectra += jnp.dot(basis[:, n : n + step], current, preferred_element_type=F32)
    spectra = spectra * NT ** (-0.5)
    spec_ref[...] = spectra
    for c in range(CONV):
        for p in range(2):
            rows[pl.ds(2 * c + p, H, stride=ROWS), :] = spectra[p * H : p * H + H, c * 128 : c * 128 + 128]
    aux_ref[3:4, :] = mark
    size = rows.shape[0] // 4
    copies = []
    for at in range(0, 4 * size, size):
        part = pl.ds(at, size)
        sent[part, :] = rows[part, :].astype(BF16)
        copies.append(pltpu.make_async_copy(sent.at[part], out_hbm.at[part], sems.at[at // size]))
        copies[-1].start()
    for copy in copies:
        copy.wait()


def sweeps_matrix(coefs, first, count):
    width = coefs.shape[1]
    rows = iota((width, width), 0)
    lanes = iota((1, width), 1)
    turned_r = jnp.zeros((width, width), F32)
    turned_i = jnp.zeros((width, width), F32)
    for k in range(LINKS):
        here = rows == lanes + coefs[8 + k : 9 + k].astype(I32)
        turned_r += jnp.where(here, coefs[1 + k : 2 + k], 0.0)
        turned_i += jnp.where(here, coefs[5 + k : 6 + k], 0.0)
    step_r, step_i = turned_r.T, turned_i.T
    mid_r, mid_i = step_r[first : first + count], step_i[first : first + count]
    twice = jnp.dot(
        jnp.concatenate([mid_r, mid_i], axis=0).astype(BF16),
        jnp.concatenate([step_r, step_i], axis=1).astype(BF16),
        preferred_element_type=F32,
    )
    same = iota((count, width), 0) + first == iota((count, width), 1)
    all_r = twice[:count, :width] - twice[count:, width:] + mid_r + jnp.where(same, 1.0, 0.0)
    all_i = twice[:count, width:] + twice[count:, :width] + mid_i
    q_r, q_i = product(all_r, all_i, coefs[0:1], coefs[4:5])
    return jnp.concatenate([q_r, q_i], axis=0).astype(BF16)


def volt_of(matrix, inject):
    count = matrix.shape[0] // 2
    acc = jnp.dot(matrix, inject, preferred_element_type=F32)
    return (acc[:count, :128] - acc[count:, 128:]).astype(BF16), (acc[:count, 128:] + acc[count:, :128]).astype(BF16)


def sweeps_kernel(coef_ref, spec_ref, aux_ref, q_ref, lift_ref):
    for c in range(CONV):
        lift_ref[c * 128 : c * 128 + 128, :] = spec_ref[:, c * 128 : c * 128 + 128].T.astype(BF16)
    row = iota((16, 128), 0)
    notes = jnp.where(row == 0, aux_ref[1:2, :], jnp.where(row == 1, aux_ref[3:4, :], 0.0))
    lift_ref[LIFT:, :] = notes.astype(BF16)
    blank = jnp.zeros((coef_ref.shape[0], TILE), F32)
    tiles = q_ref.shape[0]
    for b in range(tiles):
        around = [coef_ref[:, t * TILE : t * TILE + TILE] if 0 <= t < tiles else blank for t in (b - 1, b, b + 1)]
        coefs = pltpu.roll(jnp.concatenate(around, axis=1), 2 * TILE + EDGE, 1)[:, :WIN]
        q_ref[b] = sweeps_matrix(coefs, EDGE, TILE)


def mix_kernel(got_ref, a_ref, b_ref, rows_ref, out_a_ref, out_b_ref):
    size = got_ref.shape[0]
    rows_ref[...] = got_ref[...].astype(F32)
    first, last = rows_ref[:16, :], pltpu.roll(rows_ref[size - 16 :, :], ROWS, 0)
    far = rows_ref[pl.ds(FAR, H, stride=ROWS), :]
    is_odd = ~even("bus")
    for ref, edge, range_rows in (
        (out_a_ref, a_ref, jnp.where(is_odd, last, first)),
        (out_b_ref, b_ref, jnp.where(is_odd, first, last)),
    ):
        ref[:16, :] = range_rows.astype(BF16)
        ref[16:32, :] = edge[...].astype(BF16)
        ref[32:, :] = far.astype(BF16)


def inner_kernel(
    rows, q_ref, aux_ref, mine_ref, beside_a_ref, beside_b_ref, inject, found_ref, pick_ref, match_ref, volt_hbm, volt, sems
):
    aim(aux_ref, rows, (mine_ref, beside_a_ref, beside_b_ref), found_ref, pick_ref, match_ref)

    def part(p):
        return jnp.concatenate(
            [
                rows[pl.ds(h * HALF * ROWS + 2 * c + p, HALF, stride=ROWS), :]
                for h in range(2)
                for c in range(CONV)
            ],
            axis=0,
        )

    spectra = jnp.concatenate([part(0), part(1)], axis=1).astype(BF16)
    convs = H * CONV
    at = [
        jnp.sum(rows[pl.ds(h * HALF * ROWS + MARK, HALF, stride=ROWS), :], axis=0, keepdims=True)
        for h in range(2)
    ]
    at = jnp.concatenate(at, axis=1).astype(I32)
    lane = iota((1, convs), 1)
    source = lane // (CONV * HALF) * HALF + lane % HALF
    target = source * SUB + at
    buses = H * SUB
    owner = jnp.where(iota((buses, convs), 0) == target, 1.0, 0.0).astype(BF16)
    inject[...] = jnp.dot(owner, spectra, preferred_element_type=F32).astype(BF16)
    tiles = q_ref.shape[0]
    copies = []
    for b in range(tiles):
        first = max(b * TILE - EDGE, 0)
        last = min(b * TILE - EDGE + WIN, buses)
        pieces = [jnp.zeros((n, 256), BF16) for n in (first - b * TILE + EDGE, b * TILE - EDGE + WIN - last)]
        pieces.insert(1, inject[first:last, :])
        window = jnp.concatenate([x for x in pieces if x.shape[0]], axis=0)
        volt[0, 0, b * TILE : b * TILE + TILE, :], volt[1, 0, b * TILE : b * TILE + TILE, :] = volt_of(
            q_ref[b], window
        )
        if b % 2:
            place = pl.ds(b * TILE - TILE, 2 * TILE)
            for p in range(2):
                copies.append(
                    pltpu.make_async_copy(volt.at[p, 0, place], volt_hbm.at[p, 0, place], sems.at[b - 1 + p])
                )
                copies[-1].start()
    for copy in copies:
        copy.wait()


def edges(low, high, inject_ref, coef_ref, volt):
    buses = inject_ref.shape[0]

    def injected(edge, lane0):
        total_r = jnp.zeros((SUB, 128), F32)
        total_i = jnp.zeros((SUB, 128), F32)
        for c in range(CONV):
            at = c * HALF + lane0
            bus = jnp.broadcast_to(edge[MARK : MARK + 1, at : at + 1], (SUB, 128)).astype(I32)
            here = iota((SUB, 128), 0) == bus
            total_r += jnp.where(here, edge[2 * c : 2 * c + 1, :], 0.0)
            total_i += jnp.where(here, edge[2 * c + 1 : 2 * c + 2, :], 0.0)
        return jnp.concatenate([total_r, total_i], axis=1).astype(BF16)

    coefs = jnp.concatenate([low[16:32], coef_ref[:, :128]], axis=1)
    coefs = pltpu.roll(coefs, 128 + EDGE, 1)[:, :128]
    window = jnp.concatenate([injected(low, HALF - 1), inject_ref[: 128 - EDGE, :]], axis=0)
    volt[0, 0], volt[0, 1] = volt_of(sweeps_matrix(coefs, EDGE, EDGE), window)
    coefs = jnp.concatenate([coef_ref[:, buses - 128 :], high[16:32]], axis=1)
    coefs = pltpu.roll(coefs, 256 - EDGE, 1)[:, :128]
    window = jnp.concatenate([inject_ref[buses - 128 + EDGE :, :], injected(high, 0)], axis=0)
    volt[1, 0], volt[1, 1] = volt_of(sweeps_matrix(coefs, 128 - 2 * EDGE, EDGE), window)


def swapped(x):
    return pltpu.roll(x, 64, 1)


def packed_product(a, b, real):
    turned = swapped(b)
    return a * jnp.where(real, b, turned) + swapped(a) * jnp.where(real, -turned, b)


def finish_kernel(
    found_ref, pick_ref, match_ref, rows, mine_ref, beside_a_ref, beside_b_ref, halo_a_ref, halo_b_ref, inject_ref,
    coef_ref, done_hbm,
    near_hbm, volt_hbm, near, volt, table, sums, out, sems,
):
    del done_hbm
    is_odd = ~even("bus")
    halo_a, halo_b = halo_a_ref[...].astype(F32), halo_b_ref[...].astype(F32)
    low, high = jnp.where(is_odd, halo_b, halo_a), jnp.where(is_odd, halo_a, halo_b)
    edges(low, high, inject_ref, coef_ref, volt)
    harm = lax.axis_index("harm")
    far = rows[pl.ds(FAR, H, stride=ROWS), :]
    far = jnp.where(harm == 0, low[32:], jnp.where(harm == H - 1, high[32:], far))
    near_converters(found_ref, pick_ref, match_ref, far, (mine_ref, beside_a_ref, beside_b_ref), table, sums, out)
    near[...] = out[...].astype(BF16)
    copies = [pltpu.make_async_copy(near, near_hbm, sems.at[4])]
    for e in range(2):
        for p in range(2):
            place = volt_hbm.at[p, 0, pl.ds(e * (inject_ref.shape[0] - EDGE), EDGE)]
            copies.append(pltpu.make_async_copy(volt.at[e, p], place, sems.at[2 * e + p]))
    for copy in copies:
        copy.start()
    for copy in copies:
        copy.wait()


def aim(aux_ref, rows, lifts, found_ref, pick_ref, match_ref):
    harm = lax.axis_index("harm")
    is_even = even("harm")
    a_at = jnp.where(is_even, 2, 0)
    b_at = 2 - a_at

    shape = (8, 128)
    lane = iota(shape, 1)
    real = lane < 64
    path = lane % 16
    notes = [ref[LIFT : LIFT + 16, :].astype(F32) for ref in lifts]
    spans = [aux_ref[1:2, :], aux_ref[2:3, :], notes[2][:1]]
    spans = [jnp.broadcast_to(x, shape).astype(I32) for x in spans]

    def place(bus, line):
        at = bus // SUB
        slot = jnp.where(at == 1, 0, jnp.where(at == a_at, 1, 2))
        return slot, line * SUB + bus % SUB

    def hop(bus, line):
        slot, at = place(bus, jnp.maximum(line - 1, 0))
        found = [jnp.take_along_axis(x, at, axis=1) for x in spans]
        far = jnp.where(slot == 0, found[0], jnp.where(slot == 1, found[1], found[2]))
        return bus + jnp.where(line == 0, 0, far)

    def coef_at(bus, line, used):
        slot, at = place(bus, line)
        return jnp.where(used, slot * 128 + at + jnp.where(real, 0, 64), -1)[:1]

    bus0 = jnp.broadcast_to(aux_ref[0:1, :], shape).astype(I32)
    valid = path < 1 + LINKS + LINKS * LINKS
    two = (path >= 1 + LINKS) & valid
    line1 = jnp.where(two, 1 + (path - 1 - LINKS) // LINKS, jnp.where(valid, path, 0))
    line2 = jnp.where(two, 1 + (path - 1 - LINKS) % LINKS, 0)
    bus1 = hop(bus0, line1)
    bus2 = hop(bus1, line2)
    places = [coef_at(bus0, line1, valid & (path >= 1)), coef_at(bus1, line2, two), coef_at(bus2, 0, valid)]
    pick = jnp.where(iota((3 * 128, 3 * 128), 0) == jnp.concatenate(places, axis=1), 1.0, 0.0).astype(BF16)
    pick_ref[...] = pick[256:]
    window = jnp.concatenate(
        [rows[pl.ds(COEF, H, stride=ROWS), :], rows[pl.ds(PAIR, H, stride=ROWS), :]], axis=1
    ).astype(BF16)
    found_ref[...] = jnp.dot(window, pick[:256], preferred_element_type=F32)

    many = (128, 128)
    row = iota(many, 0)
    other = row % 64 % (3 * CONV)
    bus_of = jnp.zeros(many, I32)
    marks = [x[1:2] for x in notes]
    beside = jnp.where(is_even, 1, -1)
    for q, (at, column) in enumerate(((1, harm), (a_at, harm + beside), (b_at, harm - beside))):
        column = lax.rem(column + HALF, HALF)
        for c in range(CONV):
            bus = jnp.sum(jnp.where(iota((1, 128), 1) == c * HALF + column, marks[q], 0.0), axis=1, keepdims=True)
            bus = jnp.broadcast_to(bus.astype(I32), many) + at * SUB
            bus_of = jnp.where(other == q * CONV + c, bus, bus_of)
    wide = iota(many, 1)
    match = (row // 64 == wide // 64) & (row % 64 // (3 * CONV) == wide % 64 // 16) & (bus_of == bus2[:1])
    match_ref[...] = jnp.where(match, 1.0, 0.0).astype(BF16)


def near_converters(found_ref, pick_ref, match_ref, far, lifts, table, sums, out):
    lane = iota((1, 128), 1)
    real, path = lane < 64, lane % 16
    found = found_ref[...] + jnp.dot(far.astype(BF16), pick_ref[...], preferred_element_type=F32)
    first = found[:, :128] + jnp.where(real & (path == 0), 1.0, 0.0)
    second = found[:, 128:256] + jnp.where(real & (path <= LINKS), 1.0, 0.0)
    weight = packed_product(packed_product(first, second, real), found[:, 256:], real)

    weight = jnp.concatenate([weight, weight], axis=0)
    high = weight.astype(BF16)
    rest = (weight - high.astype(F32)).astype(BF16)
    dims = (((1,), (1,)), ((), ()))
    found = lax.dot_general(match_ref[...], high, dims, preferred_element_type=F32)
    found += lax.dot_general(match_ref[...], rest, dims, preferred_element_type=F32)
    table[:64, :] = found[:64]
    table[64:, :] = jnp.where(iota((64, 128), 1) < 64, -found[64:], found[64:])

    step = 32
    for at in range(0, 128, step):
        total = [jnp.zeros((step, 128), F32) for _ in range(CONV)]
        for q in range(3):
            for o in range(CONV):
                spec = lifts[q][o * 128 + at : o * 128 + at + step, :].astype(F32)
                turned = swapped(spec)
                for c in range(CONV):
                    n = c * 3 * CONV + q * CONV + o
                    total[c] += table[n : n + 1, :] * spec + table[64 + n : 65 + n, :] * turned
        for c in range(CONV):
            sums[c * 128 + at : c * 128 + at + step, :] = total[c]
    for c in range(CONV):
        turned = sums[c * 128 : c * 128 + 128, :].T
        for p in range(2):
            out[pl.ds(p * H * CONV + c, H, stride=CONV), :] = turned[p * H : p * H + H]


VMEM = pl.BlockSpec(memory_space=pltpu.VMEM)
HBM = pl.BlockSpec(memory_space=pltpu.HBM)


def call(kernel, name, out_shape, in_specs, scratch=(), cost=(0, 0, 0), out_specs=None, aliases=None):
    flops, moved, hard = cost
    return pl.pallas_call(
        kernel,
        out_shape=out_shape,
        in_specs=in_specs,
        out_specs=out_specs or jax.tree.map(lambda _: VMEM, out_shape),
        input_output_aliases=aliases or {},
        scratch_shapes=list(scratch),
        compiler_params=pltpu.CompilerParams(vmem_limit_bytes=40 * 2**20),
        cost_estimate=pl.CostEstimate(flops=flops, bytes_accessed=moved, transcendentals=hard),
        name=name,
    )


def swaps(count):
    rounds = []
    for start in (0, 1):
        firsts = range(start, count - 1, 2)
        rounds.append([(i, i + 1) for i in firsts] + [(i + 1, i) for i in firsts])
    return rounds


def local(conv_volt, conv_power, conv_type, type_steep, conv_bus, admittance, link_offset):
    harm_count = lax.axis_size("harm")
    bus_count = lax.axis_size("bus")
    block = admittance.shape[3]
    snapshots = conv_volt.shape[3]
    tiles = block // TILE
    size = harm_count * ROWS
    kinds = 2 * H
    S = jax.ShapeDtypeStruct
    over_bus = swaps(bus_count)[::-1]
    number = lambda r: r % harm_count * bus_count + r // harm_count
    over_ranges = [[(number(s), number(d)) for s, d in pairs] for pairs in swaps(harm_count * bus_count)]

    basis = make_basis()
    coef, edge_a, edge_b, aux, spectra, payload = call(
        begin_kernel,
        "begin",
        (
            S((16, block), F32),
            S((16, 128), F32),
            S((16, 128), F32),
            S((8, 128), F32),
            S((kinds, CONV * 128), F32),
            S((size, 128), BF16),
        ),
        [HBM] * 9,
        [
            pltpu.VMEM((2, 4, 1, block), F32),
            pltpu.VMEM((LINKS, block), I32),
            pltpu.SMEM((CONV,), I32),
            pltpu.SMEM(type_steep.shape, F32),
            pltpu.SMEM((CONV,), I32),
            pltpu.VMEM((CONV, snapshots), F32),
            pltpu.VMEM((kinds * CONV, snapshots), BF16),
            pltpu.VMEM((NT, kinds), BF16),
            pltpu.VMEM((kinds, NT), BF16),
            pltpu.VMEM((kinds * CONV, snapshots), F32),
            pltpu.VMEM((harm_count, 128), F32),
            pltpu.VMEM((harm_count, 128), F32),
            pltpu.VMEM((size, 128), F32),
            pltpu.VMEM((size, 128), BF16),
            pltpu.SemaphoreType.DMA((11,)),
        ],
        (2 * 2 * 128 * 1024 * 512, 2**20, 2**19),
        (VMEM,) * 5 + (HBM,),
    )(
        *(
            pltpu.with_memory_space_constraint(array, pltpu.HBM)
            for array in (
                admittance,
                link_offset,
                conv_type,
                type_steep,
                conv_bus,
                conv_power,
                conv_volt.reshape(kinds * CONV, snapshots),
                jnp.asarray(np.ascontiguousarray(basis.T)),
                jnp.asarray(basis),
            )
        )
    )

    four = (harm_count, ROWS // 4, 4, snapshots)
    got = lax.all_to_all(payload.reshape(four), "harm", split_axis=0, concat_axis=0, tiled=True)

    q, lift = call(
        sweeps_kernel,
        "sweeps",
        (S((tiles, 2 * TILE, WIN), BF16), S((LIFT + 16, 128), BF16)),
        [VMEM] * 3,
        cost=(2 * tiles * 256 * 256 * 512, 2**20, 0),
    )(coef, spectra, aux)
    beside_a = lax.ppermute(lift, ("harm", "bus"), over_ranges[0])
    beside_b = lax.ppermute(lift, ("harm", "bus"), over_ranges[1])
    got, q, beside_a = lax.optimization_barrier((got, q, beside_a))

    halo = S((32 + harm_count, 128), BF16)
    rows, halo_a, halo_b = call(
        mix_kernel,
        "mix",
        (S((size, 128), F32), halo, halo),
        [VMEM] * 3,
    )(got.reshape(size, snapshots), edge_a, edge_b)
    halo_a = lax.ppermute(halo_a, "bus", over_bus[0])
    halo_b = lax.ppermute(halo_b, "bus", over_bus[1])
    out_volt = S((2, 1, block, snapshots), BF16)
    inject, found, pick, match, bus_volt = call(
        inner_kernel,
        "inner",
        (S((block, 256), BF16), S((harm_count, 384), F32), S((128, 384), BF16), S((128, 128), BF16), out_volt),
        [VMEM] * 6,
        [pltpu.VMEM((2, 1, block, snapshots), BF16), pltpu.SemaphoreType.DMA((tiles,))],
        (2 * tiles * 256 * 256 * 256, 2**20, 0),
        (VMEM,) * 4 + (HBM,),
    )(rows, q, aux, lift, beside_a, beside_b)
    halo_a, halo_b, inject, bus_volt = lax.optimization_barrier((halo_a, halo_b, inject, bus_volt))
    near, bus_volt = call(
        finish_kernel,
        "finish",
        (S((kinds * CONV, snapshots), BF16), out_volt),
        [VMEM] * 11 + [HBM],
        [
            pltpu.VMEM((kinds * CONV, snapshots), BF16),
            pltpu.VMEM((2, 2, EDGE, snapshots), BF16),
            pltpu.VMEM((128, 128), F32),
            pltpu.VMEM((CONV * 128, 128), F32),
            pltpu.VMEM((kinds * CONV, 128), F32),
            pltpu.SemaphoreType.DMA((5,)),
        ],
        (2 * 10**7, 2**20, 0),
        (HBM, HBM),
        {11: 1},
    )(found, pick, match, rows, lift, beside_a, beside_b, halo_a, halo_b, inject, coef, bus_volt)
    return (bus_volt, near.reshape(2, H, CONV, snapshots))


def solution(mesh):
    in_specs = (
        P(None, None, ("bus", "harm"), None),
        P(("bus", "harm"), None),
        P(("bus", "harm")),
        P(),
        P(("bus", "harm")),
        P(None, None, "harm", "bus"),
        P(None, "bus"),
    )
    out_specs = (P(None, "harm", "bus", None), P(None, None, ("bus", "harm"), None))
    return jax.shard_map(local, mesh=mesh, in_specs=in_specs, out_specs=out_specs, check_vma=False)
```

```python
import math

import jax
import jax.numpy as jnp
import numpy as np
from jax import lax
from jax.experimental import pallas as pl
from jax.experimental.pallas import tpu as pltpu
from jax.sharding import PartitionSpec as P

H = 64
NT = 1024
REACH = 8
LINKS = 3
SUB = 16
CONV = 4
EDGE = 2 * REACH
TILE = 128
WIN = 256
ROWS = 12
COEF = 8
PAIR = 9
FAR = 10
MARK = 11
LIFT = CONV * 128
HALF = 32
F32 = jnp.float32
BF16 = jnp.bfloat16
I32 = jnp.int32


def make_basis():
    turn = np.arange(1, H + 1)[:, None] * np.arange(NT)[None, :] % NT
    angle = turn * (2.0 * math.pi / NT)
    return np.concatenate([np.cos(angle), -np.sin(angle)], axis=0).astype(BF16)


def iota(shape, dim):
    return lax.broadcasted_iota(I32, shape, dim)


def product(ar, ai, br, bi):
    return ar * br - ai * bi, ar * bi + ai * br


def grouped(x):
    k, j = iota((8, 128), 0), iota((8, 128), 1) // SUB
    for s in (1, 2, 4):
        later = pltpu.roll(pltpu.roll(x, s, 0), 128 - SUB * s, 1)
        sooner = pltpu.roll(pltpu.roll(x, 8 - s, 0), SUB * s, 1)
        bk, bj = (k // s) % 2, (j // s) % 2
        x = jnp.where(bk == bj, x, jnp.where(bk == 1, later, sooner))
    return x


def even(axis):
    return lax.rem(lax.axis_index(axis), 2) == 0


def begin_kernel(
    adm_hbm, off_hbm, type_hbm, steep_hbm, bus_hbm, power_hbm, volt_hbm, turned_hbm, basis_hbm,
    coef_ref, a_ref, b_ref, aux_ref, spec_ref, out_hbm,
    adm, off, kind, steep, bus, power, volt_in, turned, basis, volts, groups, spans, rows, sent, sems,
):
    pairs = [
        (adm_hbm, adm), (off_hbm, off), (type_hbm, kind), (steep_hbm, steep), (bus_hbm, bus), (power_hbm, power),
        (volt_hbm, volt_in),
    ]
    for at in range(0, NT, NT // 2):
        pairs.append((turned_hbm.at[pl.ds(at, NT // 2)], turned.at[pl.ds(at, NT // 2)]))
    for at in (0, H):
        pairs.append((basis_hbm.at[pl.ds(at, H)], basis.at[pl.ds(at, H)]))
    copies = [pltpu.make_async_copy(src, dst, sems.at[i]) for i, (src, dst) in enumerate(pairs)]
    for copy in copies:
        copy.start()
    for copy in copies:
        copy.wait()
    inv_r, inv_i = adm[0, 0], adm[1, 0]
    steps = [product(inv_r, inv_i, adm[0, k], adm[1, k]) for k in range(1, 1 + LINKS)]
    blank = jnp.zeros((5, inv_r.shape[1]), F32)
    coefs = jnp.concatenate(
        [inv_r] + [s[0] for s in steps] + [inv_i] + [s[1] for s in steps] + [off[...].astype(F32), blank], axis=0
    )
    coef_ref[...] = coefs
    tiles = coefs.shape[1] // 128
    for v in range(tiles):
        groups[v * 8 : v * 8 + 8, :] = grouped(coefs[:8, v * 128 : v * 128 + 128])
        spans[v * 8 : v * 8 + 8, :] = grouped(coefs[8:, v * 128 : v * 128 + 128])
    first, last = coefs[:, :128], coefs[:, tiles * 128 - 128 :]
    is_odd = even("bus")
    a_ref[...] = jnp.where(is_odd, last, first)
    b_ref[...] = jnp.where(is_odd, first, last)
    harm = lax.axis_index("harm")
    span = spans[pl.ds(harm, 1), :]
    aux_ref[1:2, :] = span
    aux_ref[2:3, :] = spans[pl.ds(harm + jnp.where(even("harm"), 1, -1), 1), :]
    group = groups[...]
    after, before = pltpu.roll(group, H - 1, 0), pltpu.roll(group, 1, 0)
    first_core = iota((H, 128), 0) % 2 == 0
    pair, far = jnp.where(first_core, after, before), jnp.where(first_core, before, after)
    rows[pl.ds(COEF, H, stride=ROWS), :] = group
    rows[pl.ds(PAIR, H, stride=ROWS), :] = pair
    rows[pl.ds(FAR, H, stride=ROWS), :] = far

    lane = iota((1, 128), 1)
    column = lax.rem(harm, HALF)
    mark = jnp.zeros((1, 128), F32)
    start = jnp.full((1, 128), SUB, F32)
    for c in range(CONV):
        number = lax.rem(bus[c], SUB).astype(F32)
        mark += jnp.where(lane == c * HALF + column, number, 0.0)
        start += jnp.where(lane % 64 // 16 == c, number, 0.0)
    aux_ref[0:1, :] = start
    rows[pl.ds(MARK, H, stride=ROWS), :] = jnp.broadcast_to(mark, (H, 128))

    volts[...] = volt_in[...].astype(F32)
    kinds = 2 * H
    volt = jnp.concatenate(
        [volts[pl.ds(c, kinds, stride=CONV), :] for c in range(CONV)], axis=1
    ).astype(BF16)
    sharp = jnp.concatenate([jnp.full((1, 128), steep[kind[c]], F32) for c in range(CONV)], axis=1)
    strong = jnp.concatenate([power[c : c + 1, :] for c in range(CONV)], axis=1)
    spectra = jnp.zeros((kinds, CONV * 128), F32)
    step = 256
    for n in range(0, NT, step):
        wave = jnp.dot(turned[n : n + step, :], volt, preferred_element_type=F32)
        current = (strong * jnp.tanh(sharp * wave)).astype(BF16)
        spectra += jnp.dot(basis[:, n : n + step], current, preferred_element_type=F32)
    spectra = spectra * NT ** (-0.5)
    spec_ref[...] = spectra
    for c in range(CONV):
        for p in range(2):
            rows[pl.ds(2 * c + p, H, stride=ROWS), :] = spectra[p * H : p * H + H, c * 128 : c * 128 + 128]
    aux_ref[3:4, :] = mark
    size = rows.shape[0] // 4
    copies = []
    for at in range(0, 4 * size, size):
        part = pl.ds(at, size)
        sent[part, :] = rows[part, :].astype(BF16)
        copies.append(pltpu.make_async_copy(sent.at[part], out_hbm.at[part], sems.at[at // size]))
        copies[-1].start()
    for copy in copies:
        copy.wait()


def sweeps_matrix(coefs, first, count):
    width = coefs.shape[1]
    rows = iota((width, width), 0)
    lanes = iota((1, width), 1)
    turned_r = jnp.zeros((width, width), F32)
    turned_i = jnp.zeros((width, width), F32)
    for k in range(LINKS):
        here = rows == lanes + coefs[8 + k : 9 + k].astype(I32)
        turned_r += jnp.where(here, coefs[1 + k : 2 + k], 0.0)
        turned_i += jnp.where(here, coefs[5 + k : 6 + k], 0.0)
    step_r, step_i = turned_r.T, turned_i.T
    mid_r, mid_i = step_r[first : first + count], step_i[first : first + count]
    twice = jnp.dot(
        jnp.concatenate([mid_r, mid_i], axis=0).astype(BF16),
        jnp.concatenate([step_r, step_i], axis=1).astype(BF16),
        preferred_element_type=F32,
    )
    same = iota((count, width), 0) + first == iota((count, width), 1)
    all_r = twice[:count, :width] - twice[count:, width:] + mid_r + jnp.where(same, 1.0, 0.0)
    all_i = twice[:count, width:] + twice[count:, :width] + mid_i
    q_r, q_i = product(all_r, all_i, coefs[0:1], coefs[4:5])
    return jnp.concatenate([q_r, q_i], axis=0).astype(BF16)


def volt_of(matrix, inject):
    count = matrix.shape[0] // 2
    acc = jnp.dot(matrix, inject, preferred_element_type=F32)
    return (acc[:count, :128] - acc[count:, 128:]).astype(BF16), (acc[:count, 128:] + acc[count:, :128]).astype(BF16)


def sweeps_kernel(coef_ref, spec_ref, aux_ref, q_ref, lift_ref):
    for c in range(CONV):
        lift_ref[c * 128 : c * 128 + 128, :] = spec_ref[:, c * 128 : c * 128 + 128].T.astype(BF16)
    row = iota((16, 128), 0)
    notes = jnp.where(row == 0, aux_ref[1:2, :], jnp.where(row == 1, aux_ref[3:4, :], 0.0))
    lift_ref[LIFT:, :] = notes.astype(BF16)
    blank = jnp.zeros((coef_ref.shape[0], TILE), F32)
    tiles = q_ref.shape[0]
    for b in range(tiles):
        around = [coef_ref[:, t * TILE : t * TILE + TILE] if 0 <= t < tiles else blank for t in (b - 1, b, b + 1)]
        coefs = pltpu.roll(jnp.concatenate(around, axis=1), 2 * TILE + EDGE, 1)[:, :WIN]
        q_ref[b] = sweeps_matrix(coefs, EDGE, TILE)


def mix_kernel(got_ref, a_ref, b_ref, rows_ref, out_a_ref, out_b_ref):
    size = got_ref.shape[0]
    rows_ref[...] = got_ref[...].astype(F32)
    first, last = rows_ref[:16, :], pltpu.roll(rows_ref[size - 16 :, :], ROWS, 0)
    far = rows_ref[pl.ds(FAR, H, stride=ROWS), :]
    is_odd = even("bus")
    for ref, edge, range_rows in (
        (out_a_ref, a_ref, jnp.where(is_odd, last, first)),
        (out_b_ref, b_ref, jnp.where(is_odd, first, last)),
    ):
        ref[:16, :] = range_rows.astype(BF16)
        ref[16:32, :] = edge[...].astype(BF16)
        ref[32:, :] = far.astype(BF16)


def inner_kernel(
    rows, q_ref, aux_ref, mine_ref, beside_a_ref, beside_b_ref, inject, found_ref, pick_ref, match_ref, volt_hbm, volt, sems
):
    aim(aux_ref, rows, (mine_ref, beside_a_ref, beside_b_ref), found_ref, pick_ref, match_ref)

    def part(p):
        return jnp.concatenate(
            [
                rows[pl.ds(h * HALF * ROWS + 2 * c + p, HALF, stride=ROWS), :]
                for h in range(2)
                for c in range(CONV)
            ],
            axis=0,
        )

    spectra = jnp.concatenate([part(0), part(1)], axis=1).astype(BF16)
    convs = H * CONV
    at = [
        jnp.sum(rows[pl.ds(h * HALF * ROWS + MARK, HALF, stride=ROWS), :], axis=0, keepdims=True)
        for h in range(2)
    ]
    at = jnp.concatenate(at, axis=1).astype(I32)
    lane = iota((1, convs), 1)
    source = lane // (CONV * HALF) * HALF + lane % HALF
    target = source * SUB + at
    buses = H * SUB
    owner = jnp.where(iota((buses, convs), 0) == target, 1.0, 0.0).astype(BF16)
    inject[...] = jnp.dot(owner, spectra, preferred_element_type=F32).astype(BF16)
    tiles = q_ref.shape[0]
    copies = []
    for b in range(tiles):
        first = max(b * TILE - EDGE, 0)
        last = min(b * TILE - EDGE + WIN, buses)
        pieces = [jnp.zeros((n, 256), BF16) for n in (first - b * TILE + EDGE, b * TILE - EDGE + WIN - last)]
        pieces.insert(1, inject[first:last, :])
        window = jnp.concatenate([x for x in pieces if x.shape[0]], axis=0)
        volt[0, 0, b * TILE : b * TILE + TILE, :], volt[1, 0, b * TILE : b * TILE + TILE, :] = volt_of(
            q_ref[b], window
        )
        if b % 2:
            place = pl.ds(b * TILE - TILE, 2 * TILE)
            for p in range(2):
                copies.append(
                    pltpu.make_async_copy(volt.at[p, 0, place], volt_hbm.at[p, 0, place], sems.at[b - 1 + p])
                )
                copies[-1].start()
    for copy in copies:
        copy.wait()


def edges(low, high, inject_ref, coef_ref, volt):
    buses = inject_ref.shape[0]

    def injected(edge, lane0):
        total_r = jnp.zeros((SUB, 128), F32)
        total_i = jnp.zeros((SUB, 128), F32)
        for c in range(CONV):
            at = c * HALF + lane0
            bus = jnp.broadcast_to(edge[MARK : MARK + 1, at : at + 1], (SUB, 128)).astype(I32)
            here = iota((SUB, 128), 0) == bus
            total_r += jnp.where(here, edge[2 * c : 2 * c + 1, :], 0.0)
            total_i += jnp.where(here, edge[2 * c + 1 : 2 * c + 2, :], 0.0)
        return jnp.concatenate([total_r, total_i], axis=1).astype(BF16)

    coefs = jnp.concatenate([low[16:32], coef_ref[:, :128]], axis=1)
    coefs = pltpu.roll(coefs, 128 + EDGE, 1)[:, :128]
    window = jnp.concatenate([injected(low, HALF - 1), inject_ref[: 128 - EDGE, :]], axis=0)
    volt[0, 0], volt[0, 1] = volt_of(sweeps_matrix(coefs, EDGE, EDGE), window)
    coefs = jnp.concatenate([coef_ref[:, buses - 128 :], high[16:32]], axis=1)
    coefs = pltpu.roll(coefs, 256 - EDGE, 1)[:, :128]
    window = jnp.concatenate([inject_ref[buses - 128 + EDGE :, :], injected(high, 0)], axis=0)
    volt[1, 0], volt[1, 1] = volt_of(sweeps_matrix(coefs, 128 - 2 * EDGE, EDGE), window)


def swapped(x):
    return pltpu.roll(x, 64, 1)


def packed_product(a, b, real):
    turned = swapped(b)
    return a * jnp.where(real, b, turned) + swapped(a) * jnp.where(real, -turned, b)


def finish_kernel(
    found_ref, pick_ref, match_ref, rows, mine_ref, beside_a_ref, beside_b_ref, halo_a_ref, halo_b_ref, inject_ref,
    coef_ref, done_hbm,
    near_hbm, volt_hbm, near, volt, table, sums, out, sems,
):
    del done_hbm
    is_odd = even("bus")
    halo_a, halo_b = halo_a_ref[...].astype(F32), halo_b_ref[...].astype(F32)
    low, high = jnp.where(is_odd, halo_b, halo_a), jnp.where(is_odd, halo_a, halo_b)
    edges(low, high, inject_ref, coef_ref, volt)
    harm = lax.axis_index("harm")
    far = rows[pl.ds(FAR, H, stride=ROWS), :]
    far = jnp.where(harm == 0, low[32:], jnp.where(harm == H - 1, high[32:], far))
    near_converters(found_ref, pick_ref, match_ref, far, (mine_ref, beside_a_ref, beside_b_ref), table, sums, out)
    near[...] = out[...].astype(BF16)
    copies = [pltpu.make_async_copy(near, near_hbm, sems.at[4])]
    for e in range(2):
        for p in range(2):
            place = volt_hbm.at[p, 0, pl.ds(e * (inject_ref.shape[0] - EDGE), EDGE)]
            copies.append(pltpu.make_async_copy(volt.at[e, p], place, sems.at[2 * e + p]))
    for copy in copies:
        copy.start()
    for copy in copies:
        copy.wait()


def aim(aux_ref, rows, lifts, found_ref, pick_ref, match_ref):
    harm = lax.axis_index("harm")
    is_even = even("harm")
    a_at = jnp.where(is_even, 2, 0)
    b_at = 2 - a_at

    shape = (8, 128)
    lane = iota(shape, 1)
    real = lane < 64
    path = lane % 16
    notes = [ref[LIFT : LIFT + 16, :].astype(F32) for ref in lifts]
    spans = [aux_ref[1:2, :], aux_ref[2:3, :], notes[2][:1]]
    spans = [jnp.broadcast_to(x, shape).astype(I32) for x in spans]

    def place(bus, line):
        at = bus // SUB
        slot = jnp.where(at == 1, 0, jnp.where(at == a_at, 1, 2))
        return slot, line * SUB + bus % SUB

    def hop(bus, line):
        slot, at = place(bus, jnp.maximum(line - 1, 0))
        found = [jnp.take_along_axis(x, at, axis=1) for x in spans]
        far = jnp.where(slot == 0, found[0], jnp.where(slot == 1, found[1], found[2]))
        return bus + jnp.where(line == 0, 0, far)

    def coef_at(bus, line, used):
        slot, at = place(bus, line)
        return jnp.where(used, slot * 128 + at + jnp.where(real, 0, 64), -1)[:1]

    bus0 = jnp.broadcast_to(aux_ref[0:1, :], shape).astype(I32)
    valid = path < 1 + LINKS + LINKS * LINKS
    two = (path >= 1 + LINKS) & valid
    line1 = jnp.where(two, 1 + (path - 1 - LINKS) // LINKS, jnp.where(valid, path, 0))
    line2 = jnp.where(two, 1 + (path - 1 - LINKS) % LINKS, 0)
    bus1 = hop(bus0, line1)
    bus2 = hop(bus1, line2)
    places = [coef_at(bus0, line1, valid & (path >= 1)), coef_at(bus1, line2, two), coef_at(bus2, 0, valid)]
    pick = jnp.where(iota((3 * 128, 3 * 128), 0) == jnp.concatenate(places, axis=1), 1.0, 0.0).astype(BF16)
    pick_ref[...] = pick[256:]
    window = jnp.concatenate(
        [rows[pl.ds(COEF, H, stride=ROWS), :], rows[pl.ds(PAIR, H, stride=ROWS), :]], axis=1
    ).astype(BF16)
    found_ref[...] = jnp.dot(window, pick[:256], preferred_element_type=F32)

    many = (128, 128)
    row = iota(many, 0)
    other = row % 64 % (3 * CONV)
    bus_of = jnp.zeros(many, I32)
    marks = [x[1:2] for x in notes]
    beside = jnp.where(is_even, 1, -1)
    for q, (at, column) in enumerate(((1, harm), (a_at, harm + beside), (b_at, harm - beside))):
        column = lax.rem(column + HALF, HALF)
        for c in range(CONV):
            bus = jnp.sum(jnp.where(iota((1, 128), 1) == c * HALF + column, marks[q], 0.0), axis=1, keepdims=True)
            bus = jnp.broadcast_to(bus.astype(I32), many) + at * SUB
            bus_of = jnp.where(other == q * CONV + c, bus, bus_of)
    wide = iota(many, 1)
    match = (row // 64 == wide // 64) & (row % 64 // (3 * CONV) == wide % 64 // 16) & (bus_of == bus2[:1])
    match_ref[...] = jnp.where(match, 1.0, 0.0).astype(BF16)


def near_converters(found_ref, pick_ref, match_ref, far, lifts, table, sums, out):
    lane = iota((1, 128), 1)
    real, path = lane < 64, lane % 16
    found = found_ref[...] + jnp.dot(far.astype(BF16), pick_ref[...], preferred_element_type=F32)
    first = found[:, :128] + jnp.where(real & (path == 0), 1.0, 0.0)
    second = found[:, 128:256] + jnp.where(real & (path <= LINKS), 1.0, 0.0)
    weight = packed_product(packed_product(first, second, real), found[:, 256:], real)

    weight = jnp.concatenate([weight, weight], axis=0)
    high = weight.astype(BF16)
    rest = (weight - high.astype(F32)).astype(BF16)
    dims = (((1,), (1,)), ((), ()))
    found = lax.dot_general(match_ref[...], high, dims, preferred_element_type=F32)
    found += lax.dot_general(match_ref[...], rest, dims, preferred_element_type=F32)
    table[:64, :] = found[:64]
    table[64:, :] = jnp.where(iota((64, 128), 1) < 64, -found[64:], found[64:])

    step = 32
    for at in range(0, 128, step):
        total = [jnp.zeros((step, 128), F32) for _ in range(CONV)]
        for q in range(3):
            for o in range(CONV):
                spec = lifts[q][o * 128 + at : o * 128 + at + step, :].astype(F32)
                turned = swapped(spec)
                for c in range(CONV):
                    n = c * 3 * CONV + q * CONV + o
                    total[c] += table[n : n + 1, :] * spec + table[64 + n : 65 + n, :] * turned
        for c in range(CONV):
            sums[c * 128 + at : c * 128 + at + step, :] = total[c]
    for c in range(CONV):
        turned = sums[c * 128 : c * 128 + 128, :].T
        for p in range(2):
            out[pl.ds(p * H * CONV + c, H, stride=CONV), :] = turned[p * H : p * H + H]


VMEM = pl.BlockSpec(memory_space=pltpu.VMEM)
HBM = pl.BlockSpec(memory_space=pltpu.HBM)


def call(kernel, name, out_shape, in_specs, scratch=(), cost=(0, 0, 0), out_specs=None, aliases=None):
    flops, moved, hard = cost
    return pl.pallas_call(
        kernel,
        out_shape=out_shape,
        in_specs=in_specs,
        out_specs=out_specs or jax.tree.map(lambda _: VMEM, out_shape),
        input_output_aliases=aliases or {},
        scratch_shapes=list(scratch),
        compiler_params=pltpu.CompilerParams(vmem_limit_bytes=40 * 2**20),
        cost_estimate=pl.CostEstimate(flops=flops, bytes_accessed=moved, transcendentals=hard),
        name=name,
    )


def swaps(count):
    rounds = []
    for start in (0, 1):
        firsts = range(start, count - 1, 2)
        rounds.append([(i, i + 1) for i in firsts] + [(i + 1, i) for i in firsts])
    return rounds


def local(conv_volt, conv_power, conv_type, type_steep, conv_bus, admittance, link_offset):
    harm_count = lax.axis_size("harm")
    bus_count = lax.axis_size("bus")
    block = admittance.shape[3]
    snapshots = conv_volt.shape[3]
    tiles = block // TILE
    size = harm_count * ROWS
    kinds = 2 * H
    S = jax.ShapeDtypeStruct
    over_bus = swaps(bus_count)
    number = lambda r: r % harm_count * bus_count + r // harm_count
    over_ranges = [[(number(s), number(d)) for s, d in pairs] for pairs in swaps(harm_count * bus_count)]

    basis = make_basis()
    coef, edge_a, edge_b, aux, spectra, payload = call(
        begin_kernel,
        "begin",
        (
            S((16, block), F32),
            S((16, 128), F32),
            S((16, 128), F32),
            S((8, 128), F32),
            S((kinds, CONV * 128), F32),
            S((size, 128), BF16),
        ),
        [HBM] * 9,
        [
            pltpu.VMEM((2, 4, 1, block), F32),
            pltpu.VMEM((LINKS, block), I32),
            pltpu.SMEM((CONV,), I32),
            pltpu.SMEM(type_steep.shape, F32),
            pltpu.SMEM((CONV,), I32),
            pltpu.VMEM((CONV, snapshots), F32),
            pltpu.VMEM((kinds * CONV, snapshots), BF16),
            pltpu.VMEM((NT, kinds), BF16),
            pltpu.VMEM((kinds, NT), BF16),
            pltpu.VMEM((kinds * CONV, snapshots), F32),
            pltpu.VMEM((harm_count, 128), F32),
            pltpu.VMEM((harm_count, 128), F32),
            pltpu.VMEM((size, 128), F32),
            pltpu.VMEM((size, 128), BF16),
            pltpu.SemaphoreType.DMA((11,)),
        ],
        (2 * 2 * 128 * 1024 * 512, 2**20, 2**19),
        (VMEM,) * 5 + (HBM,),
    )(
        *(
            pltpu.with_memory_space_constraint(array, pltpu.HBM)
            for array in (
                admittance,
                link_offset,
                conv_type,
                type_steep,
                conv_bus,
                conv_power,
                conv_volt.reshape(kinds * CONV, snapshots),
                jnp.asarray(np.ascontiguousarray(basis.T)),
                jnp.asarray(basis),
            )
        )
    )

    four = (harm_count, ROWS // 4, 4, snapshots)
    got = lax.all_to_all(payload.reshape(four), "harm", split_axis=0, concat_axis=0, tiled=True)

    q, lift = call(
        sweeps_kernel,
        "sweeps",
        (S((tiles, 2 * TILE, WIN), BF16), S((LIFT + 16, 128), BF16)),
        [VMEM] * 3,
        cost=(2 * tiles * 256 * 256 * 512, 2**20, 0),
    )(coef, spectra, aux)
    beside_a = lax.ppermute(lift, ("harm", "bus"), over_ranges[0])
    beside_b = lax.ppermute(lift, ("harm", "bus"), over_ranges[1])
    got, q, beside_a = lax.optimization_barrier((got, q, beside_a))

    halo = S((32 + harm_count, 128), BF16)
    rows, halo_a, halo_b = call(
        mix_kernel,
        "mix",
        (S((size, 128), F32), halo, halo),
        [VMEM] * 3,
    )(got.reshape(size, snapshots), edge_a, edge_b)
    halo_a = lax.ppermute(halo_a, "bus", over_bus[0])
    halo_b = lax.ppermute(halo_b, "bus", over_bus[1])
    out_volt = S((2, 1, block, snapshots), BF16)
    inject, found, pick, match, bus_volt = call(
        inner_kernel,
        "inner",
        (S((block, 256), BF16), S((harm_count, 384), F32), S((128, 384), BF16), S((128, 128), BF16), out_volt),
        [VMEM] * 6,
        [pltpu.VMEM((2, 1, block, snapshots), BF16), pltpu.SemaphoreType.DMA((tiles,))],
        (2 * tiles * 256 * 256 * 256, 2**20, 0),
        (VMEM,) * 4 + (HBM,),
    )(rows, q, aux, lift, beside_a, beside_b)
    halo_a, halo_b, inject, bus_volt = lax.optimization_barrier((halo_a, halo_b, inject, bus_volt))
    near, bus_volt = call(
        finish_kernel,
        "finish",
        (S((kinds * CONV, snapshots), BF16), out_volt),
        [VMEM] * 11 + [HBM],
        [
            pltpu.VMEM((kinds * CONV, snapshots), BF16),
            pltpu.VMEM((2, 2, EDGE, snapshots), BF16),
            pltpu.VMEM((128, 128), F32),
            pltpu.VMEM((CONV * 128, 128), F32),
            pltpu.VMEM((kinds * CONV, 128), F32),
            pltpu.SemaphoreType.DMA((5,)),
        ],
        (2 * 10**7, 2**20, 0),
        (HBM, HBM),
        {11: 1},
    )(found, pick, match, rows, lift, beside_a, beside_b, halo_a, halo_b, inject, coef, bus_volt)
    return (bus_volt, near.reshape(2, H, CONV, snapshots))


def solution(mesh):
    in_specs = (
        P(None, None, ("bus", "harm"), None),
        P(("bus", "harm"), None),
        P(("bus", "harm")),
        P(),
        P(("bus", "harm")),
        P(None, None, "harm", "bus"),
        P(None, "bus"),
    )
    out_specs = (P(None, "harm", "bus", None), P(None, None, ("bus", "harm"), None))
    return jax.shard_map(local, mesh=mesh, in_specs=in_specs, out_specs=out_specs, check_vma=False)
```

```python
import math

import jax
import jax.numpy as jnp
import numpy as np
from jax import lax
from jax.experimental import pallas as pl
from jax.experimental.pallas import tpu as pltpu
from jax.sharding import PartitionSpec as P

H = 64
NT = 1024
REACH = 8
LINKS = 3
SUB = 16
CONV = 4
EDGE = 2 * REACH
TILE = 128
WIN = 256
ROWS = 12
COEF = 8
PAIR = 9
FAR = 10
MARK = 11
LIFT = CONV * 128
HALF = 32
F32 = jnp.float32
BF16 = jnp.bfloat16
I32 = jnp.int32


def make_basis():
    turn = np.arange(1, H + 1)[:, None] * np.arange(NT)[None, :] % NT
    angle = turn * (2.0 * math.pi / NT)
    return np.concatenate([np.cos(angle), -np.sin(angle)], axis=0).astype(BF16)


def iota(shape, dim):
    return lax.broadcasted_iota(I32, shape, dim)


def product(ar, ai, br, bi):
    return ar * br - ai * bi, ar * bi + ai * br


def grouped(x):
    k, j = iota((8, 128), 0), iota((8, 128), 1) // SUB
    for s in (1, 2, 4):
        later = pltpu.roll(pltpu.roll(x, s, 0), 128 - SUB * s, 1)
        sooner = pltpu.roll(pltpu.roll(x, 8 - s, 0), SUB * s, 1)
        bk, bj = (k // s) % 2, (j // s) % 2
        x = jnp.where(bk == bj, x, jnp.where(bk == 1, later, sooner))
    return x


def even(axis):
    return lax.rem(lax.axis_index(axis), 2) == 0


def begin_kernel(
    adm_hbm, off_hbm, type_hbm, steep_hbm, bus_hbm, power_hbm, volt_hbm, turned_hbm, basis_hbm,
    coef_ref, a_ref, b_ref, aux_ref, spec_ref, out_hbm,
    adm, off, kind, steep, bus, power, volt_in, turned, basis, volts, groups, spans, rows, sent, sems,
):
    pairs = [
        (adm_hbm, adm), (off_hbm, off), (type_hbm, kind), (steep_hbm, steep), (bus_hbm, bus), (power_hbm, power),
        (volt_hbm, volt_in),
    ]
    for at in range(0, NT, NT // 2):
        pairs.append((turned_hbm.at[pl.ds(at, NT // 2)], turned.at[pl.ds(at, NT // 2)]))
    for at in (0, H):
        pairs.append((basis_hbm.at[pl.ds(at, H)], basis.at[pl.ds(at, H)]))
    copies = [pltpu.make_async_copy(src, dst, sems.at[i]) for i, (src, dst) in enumerate(pairs)]
    for copy in copies:
        copy.start()
    for copy in copies[:7]:
        copy.wait()
    inv_r, inv_i = adm[0, 0], adm[1, 0]
    steps = [product(inv_r, inv_i, adm[0, k], adm[1, k]) for k in range(1, 1 + LINKS)]
    blank = jnp.zeros((5, inv_r.shape[1]), F32)
    coefs = jnp.concatenate(
        [inv_r] + [s[0] for s in steps] + [inv_i] + [s[1] for s in steps] + [off[...].astype(F32), blank], axis=0
    )
    coef_ref[...] = coefs
    tiles = coefs.shape[1] // 128
    for v in range(tiles):
        groups[v * 8 : v * 8 + 8, :] = grouped(coefs[:8, v * 128 : v * 128 + 128])
        spans[v * 8 : v * 8 + 8, :] = grouped(coefs[8:, v * 128 : v * 128 + 128])
    first, last = coefs[:, :128], coefs[:, tiles * 128 - 128 :]
    is_odd = even("bus")
    a_ref[...] = jnp.where(is_odd, last, first)
    b_ref[...] = jnp.where(is_odd, first, last)
    harm = lax.axis_index("harm")
    span = spans[pl.ds(harm, 1), :]
    aux_ref[1:2, :] = span
    aux_ref[2:3, :] = spans[pl.ds(harm + jnp.where(even("harm"), 1, -1), 1), :]
    group = groups[...]
    after, before = pltpu.roll(group, H - 1, 0), pltpu.roll(group, 1, 0)
    first_core = iota((H, 128), 0) % 2 == 0
    pair, far = jnp.where(first_core, after, before), jnp.where(first_core, before, after)
    rows[pl.ds(COEF, H, stride=ROWS), :] = group
    rows[pl.ds(PAIR, H, stride=ROWS), :] = pair
    rows[pl.ds(FAR, H, stride=ROWS), :] = far

    lane = iota((1, 128), 1)
    column = lax.rem(harm, HALF)
    mark = jnp.zeros((1, 128), F32)
    start = jnp.full((1, 128), SUB, F32)
    for c in range(CONV):
        number = lax.rem(bus[c], SUB).astype(F32)
        mark += jnp.where(lane == c * HALF + column, number, 0.0)
        start += jnp.where(lane % 64 // 16 == c, number, 0.0)
    aux_ref[0:1, :] = start
    rows[pl.ds(MARK, H, stride=ROWS), :] = jnp.broadcast_to(mark, (H, 128))

    volts[...] = volt_in[...].astype(F32)
    kinds = 2 * H
    volt = jnp.concatenate(
        [volts[pl.ds(c, kinds, stride=CONV), :] for c in range(CONV)], axis=1
    ).astype(BF16)
    sharp = jnp.concatenate([jnp.full((1, 128), steep[kind[c]], F32) for c in range(CONV)], axis=1)
    strong = jnp.concatenate([power[c : c + 1, :] for c in range(CONV)], axis=1)
    for copy in copies[7:]:
        copy.wait()
    spectra = jnp.zeros((kinds, CONV * 128), F32)
    step = 256
    for n in range(0, NT, step):
        wave = jnp.dot(turned[n : n + step, :], volt, preferred_element_type=F32)
        current = (strong * jnp.tanh(sharp * wave)).astype(BF16)
        spectra += jnp.dot(basis[:, n : n + step], current, preferred_element_type=F32)
    spectra = spectra * NT ** (-0.5)
    spec_ref[...] = spectra
    for c in range(CONV):
        for p in range(2):
            rows[pl.ds(2 * c + p, H, stride=ROWS), :] = spectra[p * H : p * H + H, c * 128 : c * 128 + 128]
    aux_ref[3:4, :] = mark
    size = rows.shape[0] // 2
    copies = []
    for at in range(0, 2 * size, size):
        part = pl.ds(at, size)
        sent[part, :] = rows[part, :].astype(BF16)
        copies.append(pltpu.make_async_copy(sent.at[part], out_hbm.at[part], sems.at[at // size]))
        copies[-1].start()
    for copy in copies:
        copy.wait()


def sweeps_matrix(coefs, first, count):
    width = coefs.shape[1]
    rows = iota((width, width), 0)
    lanes = iota((1, width), 1)
    turned_r = jnp.zeros((width, width), F32)
    turned_i = jnp.zeros((width, width), F32)
    for k in range(LINKS):
        here = rows == lanes + coefs[8 + k : 9 + k].astype(I32)
        turned_r += jnp.where(here, coefs[1 + k : 2 + k], 0.0)
        turned_i += jnp.where(here, coefs[5 + k : 6 + k], 0.0)
    step_r, step_i = turned_r.T, turned_i.T
    mid_r, mid_i = step_r[first : first + count], step_i[first : first + count]
    twice = jnp.dot(
        jnp.concatenate([mid_r, mid_i], axis=0).astype(BF16),
        jnp.concatenate([step_r, step_i], axis=1).astype(BF16),
        preferred_element_type=F32,
    )
    same = iota((count, width), 0) + first == iota((count, width), 1)
    all_r = twice[:count, :width] - twice[count:, width:] + mid_r + jnp.where(same, 1.0, 0.0)
    all_i = twice[:count, width:] + twice[count:, :width] + mid_i
    q_r, q_i = product(all_r, all_i, coefs[0:1], coefs[4:5])
    return jnp.concatenate([q_r, q_i], axis=0).astype(BF16)


def volt_of(matrix, inject):
    count = matrix.shape[0] // 2
    acc = jnp.dot(matrix, inject, preferred_element_type=F32)
    return (acc[:count, :128] - acc[count:, 128:]).astype(BF16), (acc[:count, 128:] + acc[count:, :128]).astype(BF16)


def sweeps_kernel(coef_ref, spec_ref, aux_ref, q_ref, lift_ref):
    for c in range(CONV):
        lift_ref[c * 128 : c * 128 + 128, :] = spec_ref[:, c * 128 : c * 128 + 128].T.astype(BF16)
    row = iota((16, 128), 0)
    notes = jnp.where(row == 0, aux_ref[1:2, :], jnp.where(row == 1, aux_ref[3:4, :], 0.0))
    lift_ref[LIFT:, :] = notes.astype(BF16)
    blank = jnp.zeros((coef_ref.shape[0], TILE), F32)
    tiles = q_ref.shape[0]
    for b in range(tiles):
        around = [coef_ref[:, t * TILE : t * TILE + TILE] if 0 <= t < tiles else blank for t in (b - 1, b, b + 1)]
        coefs = pltpu.roll(jnp.concatenate(around, axis=1), 2 * TILE + EDGE, 1)[:, :WIN]
        q_ref[b] = sweeps_matrix(coefs, EDGE, TILE)


def mix_kernel(got_ref, a_ref, b_ref, rows_ref, out_a_ref, out_b_ref):
    size = got_ref.shape[0]
    rows_ref[...] = got_ref[...].astype(F32)
    first, last = rows_ref[:16, :], pltpu.roll(rows_ref[size - 16 :, :], ROWS, 0)
    far = rows_ref[pl.ds(FAR, H, stride=ROWS), :]
    is_odd = even("bus")
    for ref, edge, range_rows in (
        (out_a_ref, a_ref, jnp.where(is_odd, last, first)),
        (out_b_ref, b_ref, jnp.where(is_odd, first, last)),
    ):
        ref[:16, :] = range_rows.astype(BF16)
        ref[16:32, :] = edge[...].astype(BF16)
        ref[32:, :] = far.astype(BF16)


def inner_kernel(
    rows, q_ref, aux_ref, mine_ref, beside_a_ref, beside_b_ref, inject, found_ref, pick_ref, match_ref, volt_hbm, volt, sems
):
    aim(aux_ref, rows, (mine_ref, beside_a_ref, beside_b_ref), found_ref, pick_ref, match_ref)

    def part(p):
        return jnp.concatenate(
            [
                rows[pl.ds(h * HALF * ROWS + 2 * c + p, HALF, stride=ROWS), :]
                for h in range(2)
                for c in range(CONV)
            ],
            axis=0,
        )

    spectra = jnp.concatenate([part(0), part(1)], axis=1).astype(BF16)
    convs = H * CONV
    at = [
        jnp.sum(rows[pl.ds(h * HALF * ROWS + MARK, HALF, stride=ROWS), :], axis=0, keepdims=True)
        for h in range(2)
    ]
    at = jnp.concatenate(at, axis=1).astype(I32)
    lane = iota((1, convs), 1)
    source = lane // (CONV * HALF) * HALF + lane % HALF
    target = source * SUB + at
    buses = H * SUB
    owner = jnp.where(iota((buses, convs), 0) == target, 1.0, 0.0).astype(BF16)
    inject[...] = jnp.dot(owner, spectra, preferred_element_type=F32).astype(BF16)
    tiles = q_ref.shape[0]
    copies = []
    for b in range(tiles):
        first = max(b * TILE - EDGE, 0)
        last = min(b * TILE - EDGE + WIN, buses)
        pieces = [jnp.zeros((n, 256), BF16) for n in (first - b * TILE + EDGE, b * TILE - EDGE + WIN - last)]
        pieces.insert(1, inject[first:last, :])
        window = jnp.concatenate([x for x in pieces if x.shape[0]], axis=0)
        volt[0, 0, b * TILE : b * TILE + TILE, :], volt[1, 0, b * TILE : b * TILE + TILE, :] = volt_of(
            q_ref[b], window
        )
        if b % 2:
            place = pl.ds(b * TILE - TILE, 2 * TILE)
            for p in range(2):
                copies.append(
                    pltpu.make_async_copy(volt.at[p, 0, place], volt_hbm.at[p, 0, place], sems.at[b - 1 + p])
                )
                copies[-1].start()
    for copy in copies:
        copy.wait()


def edges(low, high, inject_ref, coef_ref, volt):
    buses = inject_ref.shape[0]

    def injected(edge, lane0):
        total_r = jnp.zeros((SUB, 128), F32)
        total_i = jnp.zeros((SUB, 128), F32)
        for c in range(CONV):
            at = c * HALF + lane0
            bus = jnp.broadcast_to(edge[MARK : MARK + 1, at : at + 1], (SUB, 128)).astype(I32)
            here = iota((SUB, 128), 0) == bus
            total_r += jnp.where(here, edge[2 * c : 2 * c + 1, :], 0.0)
            total_i += jnp.where(here, edge[2 * c + 1 : 2 * c + 2, :], 0.0)
        return jnp.concatenate([total_r, total_i], axis=1).astype(BF16)

    coefs = jnp.concatenate([low[16:32], coef_ref[:, :128]], axis=1)
    coefs = pltpu.roll(coefs, 128 + EDGE, 1)[:, :128]
    window = jnp.concatenate([injected(low, HALF - 1), inject_ref[: 128 - EDGE, :]], axis=0)
    volt[0, 0], volt[0, 1] = volt_of(sweeps_matrix(coefs, EDGE, EDGE), window)
    coefs = jnp.concatenate([coef_ref[:, buses - 128 :], high[16:32]], axis=1)
    coefs = pltpu.roll(coefs, 256 - EDGE, 1)[:, :128]
    window = jnp.concatenate([inject_ref[buses - 128 + EDGE :, :], injected(high, 0)], axis=0)
    volt[1, 0], volt[1, 1] = volt_of(sweeps_matrix(coefs, 128 - 2 * EDGE, EDGE), window)


def swapped(x):
    return pltpu.roll(x, 64, 1)


def packed_product(a, b, real):
    turned = swapped(b)
    return a * jnp.where(real, b, turned) + swapped(a) * jnp.where(real, -turned, b)


def finish_kernel(
    found_ref, pick_ref, match_ref, rows, mine_ref, beside_a_ref, beside_b_ref, halo_a_ref, halo_b_ref, inject_ref,
    coef_ref, done_hbm,
    near_hbm, volt_hbm, near, volt, table, sums, out, sems,
):
    del done_hbm
    is_odd = even("bus")
    halo_a, halo_b = halo_a_ref[...].astype(F32), halo_b_ref[...].astype(F32)
    low, high = jnp.where(is_odd, halo_b, halo_a), jnp.where(is_odd, halo_a, halo_b)
    edges(low, high, inject_ref, coef_ref, volt)
    harm = lax.axis_index("harm")
    far = rows[pl.ds(FAR, H, stride=ROWS), :]
    far = jnp.where(harm == 0, low[32:], jnp.where(harm == H - 1, high[32:], far))
    near_converters(found_ref, pick_ref, match_ref, far, (mine_ref, beside_a_ref, beside_b_ref), table, sums, out)
    near[...] = out[...].astype(BF16)
    copies = [pltpu.make_async_copy(near, near_hbm, sems.at[4])]
    for e in range(2):
        for p in range(2):
            place = volt_hbm.at[p, 0, pl.ds(e * (inject_ref.shape[0] - EDGE), EDGE)]
            copies.append(pltpu.make_async_copy(volt.at[e, p], place, sems.at[2 * e + p]))
    for copy in copies:
        copy.start()
    for copy in copies:
        copy.wait()


def aim(aux_ref, rows, lifts, found_ref, pick_ref, match_ref):
    harm = lax.axis_index("harm")
    is_even = even("harm")
    a_at = jnp.where(is_even, 2, 0)
    b_at = 2 - a_at

    shape = (8, 128)
    lane = iota(shape, 1)
    real = lane < 64
    path = lane % 16
    notes = [ref[LIFT : LIFT + 16, :].astype(F32) for ref in lifts]
    spans = [aux_ref[1:2, :], aux_ref[2:3, :], notes[2][:1]]
    spans = [jnp.broadcast_to(x, shape).astype(I32) for x in spans]

    def place(bus, line):
        at = bus // SUB
        slot = jnp.where(at == 1, 0, jnp.where(at == a_at, 1, 2))
        return slot, line * SUB + bus % SUB

    def hop(bus, line):
        slot, at = place(bus, jnp.maximum(line - 1, 0))
        found = [jnp.take_along_axis(x, at, axis=1) for x in spans]
        far = jnp.where(slot == 0, found[0], jnp.where(slot == 1, found[1], found[2]))
        return bus + jnp.where(line == 0, 0, far)

    def coef_at(bus, line, used):
        slot, at = place(bus, line)
        return jnp.where(used, slot * 128 + at + jnp.where(real, 0, 64), -1)[:1]

    bus0 = jnp.broadcast_to(aux_ref[0:1, :], shape).astype(I32)
    valid = path < 1 + LINKS + LINKS * LINKS
    two = (path >= 1 + LINKS) & valid
    line1 = jnp.where(two, 1 + (path - 1 - LINKS) // LINKS, jnp.where(valid, path, 0))
    line2 = jnp.where(two, 1 + (path - 1 - LINKS) % LINKS, 0)
    bus1 = hop(bus0, line1)
    bus2 = hop(bus1, line2)
    places = [coef_at(bus0, line1, valid & (path >= 1)), coef_at(bus1, line2, two), coef_at(bus2, 0, valid)]
    pick = jnp.where(iota((3 * 128, 3 * 128), 0) == jnp.concatenate(places, axis=1), 1.0, 0.0).astype(BF16)
    pick_ref[...] = pick[256:]
    window = jnp.concatenate(
        [rows[pl.ds(COEF, H, stride=ROWS), :], rows[pl.ds(PAIR, H, stride=ROWS), :]], axis=1
    ).astype(BF16)
    found_ref[...] = jnp.dot(window, pick[:256], preferred_element_type=F32)

    many = (128, 128)
    row = iota(many, 0)
    other = row % 64 % (3 * CONV)
    bus_of = jnp.zeros(many, I32)
    marks = [x[1:2] for x in notes]
    beside = jnp.where(is_even, 1, -1)
    for q, (at, column) in enumerate(((1, harm), (a_at, harm + beside), (b_at, harm - beside))):
        column = lax.rem(column + HALF, HALF)
        for c in range(CONV):
            bus = jnp.sum(jnp.where(iota((1, 128), 1) == c * HALF + column, marks[q], 0.0), axis=1, keepdims=True)
            bus = jnp.broadcast_to(bus.astype(I32), many) + at * SUB
            bus_of = jnp.where(other == q * CONV + c, bus, bus_of)
    wide = iota(many, 1)
    match = (row // 64 == wide // 64) & (row % 64 // (3 * CONV) == wide % 64 // 16) & (bus_of == bus2[:1])
    match_ref[...] = jnp.where(match, 1.0, 0.0).astype(BF16)


def near_converters(found_ref, pick_ref, match_ref, far, lifts, table, sums, out):
    lane = iota((1, 128), 1)
    real, path = lane < 64, lane % 16
    found = found_ref[...] + jnp.dot(far.astype(BF16), pick_ref[...], preferred_element_type=F32)
    first = found[:, :128] + jnp.where(real & (path == 0), 1.0, 0.0)
    second = found[:, 128:256] + jnp.where(real & (path <= LINKS), 1.0, 0.0)
    weight = packed_product(packed_product(first, second, real), found[:, 256:], real)

    weight = jnp.concatenate([weight, weight], axis=0)
    high = weight.astype(BF16)
    rest = (weight - high.astype(F32)).astype(BF16)
    dims = (((1,), (1,)), ((), ()))
    found = lax.dot_general(match_ref[...], high, dims, preferred_element_type=F32)
    found += lax.dot_general(match_ref[...], rest, dims, preferred_element_type=F32)
    table[:64, :] = found[:64]
    table[64:, :] = jnp.where(iota((64, 128), 1) < 64, -found[64:], found[64:])

    step = 32
    for at in range(0, 128, step):
        total = [jnp.zeros((step, 128), F32) for _ in range(CONV)]
        for q in range(3):
            for o in range(CONV):
                spec = lifts[q][o * 128 + at : o * 128 + at + step, :].astype(F32)
                turned = swapped(spec)
                for c in range(CONV):
                    n = c * 3 * CONV + q * CONV + o
                    total[c] += table[n : n + 1, :] * spec + table[64 + n : 65 + n, :] * turned
        for c in range(CONV):
            sums[c * 128 + at : c * 128 + at + step, :] = total[c]
    for c in range(CONV):
        turned = sums[c * 128 : c * 128 + 128, :].T
        for p in range(2):
            out[pl.ds(p * H * CONV + c, H, stride=CONV), :] = turned[p * H : p * H + H]


VMEM = pl.BlockSpec(memory_space=pltpu.VMEM)
HBM = pl.BlockSpec(memory_space=pltpu.HBM)


def call(kernel, name, out_shape, in_specs, scratch=(), cost=(0, 0, 0), out_specs=None, aliases=None):
    flops, moved, hard = cost
    return pl.pallas_call(
        kernel,
        out_shape=out_shape,
        in_specs=in_specs,
        out_specs=out_specs or jax.tree.map(lambda _: VMEM, out_shape),
        input_output_aliases=aliases or {},
        scratch_shapes=list(scratch),
        compiler_params=pltpu.CompilerParams(vmem_limit_bytes=40 * 2**20),
        cost_estimate=pl.CostEstimate(flops=flops, bytes_accessed=moved, transcendentals=hard),
        name=name,
    )


def swaps(count):
    rounds = []
    for start in (0, 1):
        firsts = range(start, count - 1, 2)
        rounds.append([(i, i + 1) for i in firsts] + [(i + 1, i) for i in firsts])
    return rounds


def local(conv_volt, conv_power, conv_type, type_steep, conv_bus, admittance, link_offset):
    harm_count = lax.axis_size("harm")
    bus_count = lax.axis_size("bus")
    block = admittance.shape[3]
    snapshots = conv_volt.shape[3]
    tiles = block // TILE
    size = harm_count * ROWS
    kinds = 2 * H
    S = jax.ShapeDtypeStruct
    over_bus = swaps(bus_count)
    number = lambda r: r % harm_count * bus_count + r // harm_count
    over_ranges = [[(number(s), number(d)) for s, d in pairs] for pairs in swaps(harm_count * bus_count)]

    basis = make_basis()
    coef, edge_a, edge_b, aux, spectra, payload = call(
        begin_kernel,
        "begin",
        (
            S((16, block), F32),
            S((16, 128), F32),
            S((16, 128), F32),
            S((8, 128), F32),
            S((kinds, CONV * 128), F32),
            S((size, 128), BF16),
        ),
        [HBM] * 9,
        [
            pltpu.VMEM((2, 4, 1, block), F32),
            pltpu.VMEM((LINKS, block), I32),
            pltpu.SMEM((CONV,), I32),
            pltpu.SMEM(type_steep.shape, F32),
            pltpu.SMEM((CONV,), I32),
            pltpu.VMEM((CONV, snapshots), F32),
            pltpu.VMEM((kinds * CONV, snapshots), BF16),
            pltpu.VMEM((NT, kinds), BF16),
            pltpu.VMEM((kinds, NT), BF16),
            pltpu.VMEM((kinds * CONV, snapshots), F32),
            pltpu.VMEM((harm_count, 128), F32),
            pltpu.VMEM((harm_count, 128), F32),
            pltpu.VMEM((size, 128), F32),
            pltpu.VMEM((size, 128), BF16),
            pltpu.SemaphoreType.DMA((11,)),
        ],
        (2 * 2 * 128 * 1024 * 512, 2**20, 2**19),
        (VMEM,) * 5 + (HBM,),
    )(
        *(
            pltpu.with_memory_space_constraint(array, pltpu.HBM)
            for array in (
                admittance,
                link_offset,
                conv_type,
                type_steep,
                conv_bus,
                conv_power,
                conv_volt.reshape(kinds * CONV, snapshots),
                jnp.asarray(np.ascontiguousarray(basis.T)),
                jnp.asarray(basis),
            )
        )
    )

    four = (harm_count, ROWS // 4, 4, snapshots)
    got = lax.all_to_all(payload.reshape(four), "harm", split_axis=0, concat_axis=0, tiled=True)

    q, lift = call(
        sweeps_kernel,
        "sweeps",
        (S((tiles, 2 * TILE, WIN), BF16), S((LIFT + 16, 128), BF16)),
        [VMEM] * 3,
        cost=(2 * tiles * 256 * 256 * 512, 2**20, 0),
    )(coef, spectra, aux)
    beside_a = lax.ppermute(lift, ("harm", "bus"), over_ranges[0])
    beside_b = lax.ppermute(lift, ("harm", "bus"), over_ranges[1])
    got, q, beside_a = lax.optimization_barrier((got, q, beside_a))

    halo = S((32 + harm_count, 128), BF16)
    rows, halo_a, halo_b = call(
        mix_kernel,
        "mix",
        (S((size, 128), F32), halo, halo),
        [VMEM] * 3,
    )(got.reshape(size, snapshots), edge_a, edge_b)
    halo_a = lax.ppermute(halo_a, "bus", over_bus[0])
    halo_b = lax.ppermute(halo_b, "bus", over_bus[1])
    out_volt = S((2, 1, block, snapshots), BF16)
    inject, found, pick, match, bus_volt = call(
        inner_kernel,
        "inner",
        (S((block, 256), BF16), S((harm_count, 384), F32), S((128, 384), BF16), S((128, 128), BF16), out_volt),
        [VMEM] * 6,
        [pltpu.VMEM((2, 1, block, snapshots), BF16), pltpu.SemaphoreType.DMA((tiles,))],
        (2 * tiles * 256 * 256 * 256, 2**20, 0),
        (VMEM,) * 4 + (HBM,),
    )(rows, q, aux, lift, beside_a, beside_b)
    halo_a, halo_b, inject, bus_volt = lax.optimization_barrier((halo_a, halo_b, inject, bus_volt))
    near, bus_volt = call(
        finish_kernel,
        "finish",
        (S((kinds * CONV, snapshots), BF16), out_volt),
        [VMEM] * 11 + [HBM],
        [
            pltpu.VMEM((kinds * CONV, snapshots), BF16),
            pltpu.VMEM((2, 2, EDGE, snapshots), BF16),
            pltpu.VMEM((128, 128), F32),
            pltpu.VMEM((CONV * 128, 128), F32),
            pltpu.VMEM((kinds * CONV, 128), F32),
            pltpu.SemaphoreType.DMA((5,)),
        ],
        (2 * 10**7, 2**20, 0),
        (HBM, HBM),
        {11: 1},
    )(found, pick, match, rows, lift, beside_a, beside_b, halo_a, halo_b, inject, coef, bus_volt)
    return (bus_volt, near.reshape(2, H, CONV, snapshots))


def solution(mesh):
    in_specs = (
        P(None, None, ("bus", "harm"), None),
        P(("bus", "harm"), None),
        P(("bus", "harm")),
        P(),
        P(("bus", "harm")),
        P(None, None, "harm", "bus"),
        P(None, "bus"),
    )
    out_specs = (P(None, "harm", "bus", None), P(None, None, ("bus", "harm"), None))
    return jax.shard_map(local, mesh=mesh, in_specs=in_specs, out_specs=out_specs, check_vma=False)
```
